32 devices in a mesh: res: 8 (over z, y), nbr: 4 (over x, core).
Axes of the slice: x: 2, y: 2, z: 4, core: 2. Of those that a mesh axis runs over, the one named last changes fastest.
Arguments:
- nodes: float32 [1024, 512], P(('res', 'nbr')), may hold values from -6 to 6
- edges: float32 [1024, 60, 192], P('res', 'nbr'), may hold values from -6 to 6
- protein_ids: int32 [1024], P(('res', 'nbr')), may hold values from 0 to 5, as said below
- time_index: int32 [6], replicated, may hold values from 0 to 127
- neighbors: int32 [1024, 60], P('res', 'nbr'), may hold values from 0 to 1023, as said below
- edge_mask: int32 [1024, 60], P('res', 'nbr'), may hold values from 0 to 1, as said below
- time_table: float32 [128, 512], P('res', 'nbr'), may hold values from -3 to 3
- msg_in: float32 [2, 1216, 512], P(None, 'res', 'nbr'), may hold values from -0.15625 to 0.15625
- msg_mid: float32 [2, 512, 512], P(None, 'res', 'nbr'), may hold values from -0.25 to 0.25
- msg_out: float32 [2, 512, 512], P(None, 'res', 'nbr'), may hold values from -0.5 to 0.5
- ffn_in: float32 [2, 512, 2048], P(None, 'res', 'nbr'), may hold values from -0.25 to 0.25
- ffn_out: float32 [2, 2048, 512], P(None, 'nbr', 'res'), may hold values from -0.125 to 0.125
- edge_in: float32 [2, 1216, 192], P(None, 'res', 'nbr'), may hold values from -0.15625 to 0.15625
- edge_hidden: float32 [2, 2, 192, 192], P(None, None, 'res', 'nbr'), may hold values from -0.4375 to 0.4375
- node_gains: float32 [2, 2, 512], replicated, may hold values from 0.25 to 1.75
- node_biases: float32 [2, 6, 512], replicated, may hold values from -1 to 1
- ffn_bias: float32 [2, 2048], replicated, may hold values from -1 to 1
- edge_gains: float32 [2, 192], replicated, may hold values from 0.25 to 1.75
- edge_biases: float32 [2, 4, 192], replicated, may hold values from -1 to 1
- d_nodes: float32 [1024, 512], P(('res', 'nbr')), may hold values from -6 to 6
- d_edges: float32 [1024, 60, 192], P('res', 'nbr'), may hold values from -6 to 6
Outputs:
- nodes_out: float32 [1024, 512], P(('res', 'nbr'))
- edges_out: float32 [1024, 60, 192], P('res', 'nbr')
- g_nodes: float32 [1024, 512], P(('res', 'nbr'))
- g_edges: float32 [1024, 60, 192], P('res', 'nbr')
- g_time_table: float32 [128, 512], P('res', 'nbr')
- g_msg_in: float32 [2, 1216, 512], P(None, 'res', 'nbr')
- g_msg_mid: float32 [2, 512, 512], P(None, 'res', 'nbr')
- g_msg_out: float32 [2, 512, 512], P(None, 'res', 'nbr')
- g_ffn_in: float32 [2, 512, 2048], P(None, 'res', 'nbr')
- g_ffn_out: float32 [2, 2048, 512], P(None, 'nbr', 'res')
- g_edge_in: float32 [2, 1216, 192], P(None, 'res', 'nbr')
- g_edge_hidden: float32 [2, 2, 192, 192], P(None, None, 'res', 'nbr')
- g_node_gains: float32 [2, 2, 512], replicated
- g_node_biases: float32 [2, 6, 512], replicated
- g_ffn_bias: float32 [2, 2048], replicated
- g_edge_gains: float32 [2, 192], replicated
- g_edge_biases: float32 [2, 4, 192], replicated
The draws below stay inside these ranges and needn't reach their ends.
Inputs may be any that keep to these rules, and one draw needn't show every extreme that they name: `protein_ids`: protein numbers never fall along the residues and each protein covers a run of one or more residues; one protein covers residues of every index of res. `neighbors`: every neighbour lies in the same protein as its residue and at most 128 positions from it. `edge_mask`: slot 0 of every residue is used.
All inputs are finite; a program needn't handle non-finite values.
Results may differ from the reference program's by a relative error of at most 0.02.
Values may be sent and summed in bfloat16 or wider, within the bound.
A program may use at most 256 MiB of HBM per device.

```python
import math
from functools import partial
import jax
import jax.numpy as jnp
from jax import lax

D = 512
DE = 192
FF = 2048
K = 60
LAYERS = 2
TIMES = 128
PROTEINS = 6
R_DEV = 128
DIN = 1216
RES = 1024


def protein_layout(key):
    layout_key = jax.random.fold_in(key, 11)
    short_key, place_key = jax.random.split(layout_key)
    shorts = jax.random.randint(short_key, (PROTEINS - 1,), 1, max(2, R_DEV // 5))
    before = jax.random.randint(place_key, (), 0, PROTEINS)
    order = jnp.arange(PROTEINS, dtype=jnp.int32)
    short_at = jnp.clip(jnp.where(order < before, order, order - 1), 0, PROTEINS - 2)
    lengths = jnp.where(order == before, RES - jnp.sum(shorts), shorts[short_at])
    starts = jnp.cumsum(lengths) - lengths
    position = jnp.arange(RES, dtype=jnp.int32)
    ids = jnp.sum((position[:, None] >= starts[None, 1:]).astype(jnp.int32), axis=1)
    return (ids, starts, lengths)


def draw_protein_ids(key, part):
    ids, starts, lengths = protein_layout(key)
    return ids.astype(jnp.int32)


def draw_neighbors(key, part):
    ids, starts, lengths = protein_layout(key)
    key = jax.random.fold_in(key, 2)
    offsets = jax.random.randint(key, (RES, K), -R_DEV, R_DEV + 1)
    position = jnp.arange(RES, dtype=jnp.int32)[:, None]
    lowest = starts[ids][:, None]
    highest = lowest + lengths[ids][:, None] - 1
    return jnp.clip(position + offsets, lowest, highest).astype(jnp.int32)


def draw_edge_mask(key, part):
    key = jax.random.fold_in(key, 3)
    rate_key, coin_key = jax.random.split(key)
    group_count = (RES + 15) // 16
    rates = jax.random.randint(rate_key, (group_count,), 20, 101)
    coins = jax.random.randint(coin_key, (RES, K), 0, 100)
    row_rates = rates[jnp.arange(RES, dtype=jnp.int32) // 16]
    chosen = (coins < row_rates[:, None]).astype(jnp.int32)
    return chosen.at[:, 0].set(1).astype(jnp.int32)


def touch_ends(values, key, smallest, top_value):
    spot = [jax.random.randint(jax.random.fold_in(key, axis), (), 0, length) for axis, length in enumerate(values.shape)]
    longest = values.shape.index(max(values.shape))
    next_to = spot[:longest] + [(spot[longest] + 1) % values.shape[longest]] + spot[longest + 1:]
    return values.at[tuple(spot)].set(smallest).at[tuple(next_to)].set(top_value)


def block_levels(stream_key, dims, cuts, least, largest):
    level, own = 1.0, jax.random.fold_in(stream_key, 6)
    for dim, shards_of in cuts:
        draws = jnp.exp(jax.random.uniform(jax.random.fold_in(own, dim), (shards_of,), jnp.float32, least / len(cuts), largest / len(cuts)))
        level = level * jnp.repeat(draws, dims[dim] // shards_of).reshape([-1 if axis == dim else 1 for axis in range(len(dims))])
    return level


def scatter_about(stream_key, dims, spread, bound, shards=(), kind=jnp.bfloat16):
    array = spread * jax.random.normal(stream_key, dims, jnp.float32)
    if shards:
        array = array * block_levels(stream_key, dims, shards, -0.22, 0.18)
    return jnp.clip(array, -bound, bound).astype(kind)


def setup_inputs(seed: int = 0) -> dict:
    arg_keys = jax.random.split(jax.random.key(seed), 22)
    return {
        "nodes": scatter_about(arg_keys[0], (RES, D), 1.0, 6.0, ((0, 32),), jnp.float32),
        "edges": scatter_about(arg_keys[1], (RES, K, DE), 1.0, 6.0, ((0, 8), (1, 4)), jnp.float32),
        "protein_ids": draw_protein_ids(jax.random.fold_in(arg_keys[21], 71), 0),
        "time_index": touch_ends(jax.random.randint(arg_keys[3], (PROTEINS,), 0, TIMES), jax.random.fold_in(arg_keys[3], 1), 0, TIMES - 1).astype(jnp.int32),
        "neighbors": draw_neighbors(jax.random.fold_in(arg_keys[21], 71), 0),
        "edge_mask": draw_edge_mask(jax.random.fold_in(arg_keys[21], 71), 0),
        "time_table": scatter_about(arg_keys[6], (TIMES, D), 0.5, 3.0, ((0, 8), (1, 4)), jnp.float32),
        "msg_in": scatter_about(arg_keys[7], (LAYERS, DIN, D), DIN ** -0.5, 0.15625, ((1, 8), (2, 4)), jnp.float32),
        "msg_mid": scatter_about(arg_keys[8], (LAYERS, D, D), D ** -0.5, 0.25, ((1, 8), (2, 4)), jnp.float32),
        "msg_out": scatter_about(arg_keys[9], (LAYERS, D, D), (D // 4) ** -0.5, 0.5, ((1, 8), (2, 4)), jnp.float32),
        "ffn_in": scatter_about(arg_keys[10], (LAYERS, D, FF), D ** -0.5, 0.25, ((1, 8), (2, 4)), jnp.float32),
        "ffn_out": scatter_about(arg_keys[11], (LAYERS, FF, D), FF ** -0.5, 0.125, ((1, 4), (2, 8)), jnp.float32),
        "edge_in": scatter_about(arg_keys[12], (LAYERS, DIN, DE), DIN ** -0.5, 0.15625, ((1, 8), (2, 4)), jnp.float32),
        "edge_hidden": scatter_about(arg_keys[13], (LAYERS, 2, DE, DE), DE ** -0.5, 0.4375, ((2, 8), (3, 4)), jnp.float32),
        "node_gains": jnp.clip(1.0 + 0.15 * jax.random.normal(arg_keys[14], (LAYERS, 2, D), jnp.float32), 0.25, 1.75),
        "node_biases": scatter_about(arg_keys[15], (LAYERS, 6, D), 0.2, 1.0, (), jnp.float32),
        "ffn_bias": scatter_about(arg_keys[16], (LAYERS, FF), 0.2, 1.0, (), jnp.float32),
        "edge_gains": jnp.clip(1.0 + 0.15 * jax.random.normal(arg_keys[17], (LAYERS, DE), jnp.float32), 0.25, 1.75),
        "edge_biases": scatter_about(arg_keys[18], (LAYERS, 4, DE), 0.2, 1.0, (), jnp.float32),
        "d_nodes": scatter_about(arg_keys[19], (RES, D), 1.0, 6.0, ((0, 32),), jnp.float32),
        "d_edges": scatter_about(arg_keys[20], (RES, K, DE), 1.0, 6.0, ((0, 8), (1, 4)), jnp.float32),
    }


NORM_EPS = 1e-05
PRECISE = lax.Precision.HIGHEST

@jax.custom_vjp
def low(v):
    return lax.optimization_barrier(v.astype(jnp.bfloat16)).astype(jnp.float32)

@jax.custom_vjp
def low_back(v):
    return v

def low_keep(v):
    return (low(v), None)

def low_pass(kept, grad):
    return (grad,)

def back_keep(v):
    return (v, None)

def back_low(kept, grad):
    return (low(grad),)
low.defvjp(low_keep, low_pass)
low_back.defvjp(back_keep, back_low)

def layer_norm(value, gain, shift):
    centre = lax.optimization_barrier(jnp.mean(value, axis=-1, keepdims=True))
    offset = value - centre
    spread_sq = lax.optimization_barrier(jnp.mean(offset * offset, axis=-1, keepdims=True))
    return offset * lax.rsqrt(spread_sq + NORM_EPS) * gain + shift

def product(inputs, weight):
    return jnp.einsum('nc,cd->nd', inputs, weight, precision=PRECISE)

def perceptron(inputs, first, bias_one, middle, bias_two, last, bias_three):
    pre_one = low_back(product(inputs, first) + bias_one)
    act_one = low(jax.nn.gelu(pre_one))
    pre_two = low_back(product(act_one, middle) + bias_two)
    act_two = low(jax.nn.gelu(pre_two))
    return product(act_two, last) + bias_three

def edge_rows(index, own_rows, edge_piece, states_low):
    row_count, slot_count = index.shape
    node_width = own_rows.shape[1]
    mine = jnp.broadcast_to(own_rows[:, None, :], (row_count, slot_count, node_width))
    other = jnp.take(states_low, index, axis=0)
    joined = jnp.concatenate([mine, other, edge_piece], axis=2)
    return joined.reshape(row_count * slot_count, joined.shape[2])

def forward(integers, nodes, edges, time_table, msg_in, msg_mid, msg_out, ffn_in, ffn_out, edge_in, edge_hidden, node_gains, node_biases, ffn_bias, edge_gains, edge_biases):
    protein_ids, time_index, neighbors, edge_mask = integers
    block_size = math.gcd(RES, 64)
    groups = RES // block_size
    step_rows = time_index[protein_ids]
    state = nodes + low(time_table)[step_rows]
    edge_state = edges
    ones_float = edge_mask.astype(jnp.float32)
    counts = lax.optimization_barrier(jnp.sum(ones_float, axis=1))
    index_blocks = neighbors.reshape(groups, block_size, neighbors.shape[1])
    mask_blocks = ones_float.reshape(groups, block_size, neighbors.shape[1])
    edge_shape = (groups, block_size) + edges.shape[1:]
    for layer_at in range(LAYERS):
        biases_now = node_biases[layer_at]
        edge_bias_now = edge_biases[layer_at]
        states_low = low(state)
        edges_low = low(edge_state)
        w_first = low(msg_in[layer_at])
        w_middle = low(msg_mid[layer_at])
        w_last = low(msg_out[layer_at])

        def message(pieces):
            index, mask_piece, own_rows, edge_piece = pieces
            inputs = edge_rows(index, own_rows, edge_piece, states_low)
            result = perceptron(inputs, w_first, biases_now[0], w_middle, biases_now[1], w_last, biases_now[2])
            result = result.reshape(index.shape[0], index.shape[1], result.shape[1])
            return low_back(lax.optimization_barrier(jnp.sum(result * mask_piece[:, :, None], axis=1)))
        totals = lax.map(jax.checkpoint(message), (index_blocks, mask_blocks, states_low.reshape(groups, block_size, -1), edges_low.reshape(edge_shape)))
        totals = totals.reshape(RES, totals.shape[2])
        hidden_one = layer_norm(state + totals / counts[:, None], node_gains[layer_at, 0], biases_now[4])
        pre_ffn = low_back(product(low(hidden_one), low(ffn_in[layer_at])) + ffn_bias[layer_at])
        branch = low_back(product(low(jax.nn.gelu(pre_ffn)), low(ffn_out[layer_at])) + biases_now[3])
        hidden_two = layer_norm(hidden_one + branch, node_gains[layer_at, 1], biases_now[5])
        two_low = low(hidden_two)
        e_first = low(edge_in[layer_at])
        e_middle = low(edge_hidden[layer_at, 0])
        e_last = low(edge_hidden[layer_at, 1])

        def update(pieces):
            index, own_rows, edge_piece, edge_full = pieces
            inputs = edge_rows(index, own_rows, edge_piece, two_low)
            result = low_back(perceptron(inputs, e_first, edge_bias_now[0], e_middle, edge_bias_now[1], e_last, edge_bias_now[2]))
            return layer_norm(edge_full + result.reshape(edge_full.shape), edge_gains[layer_at], edge_bias_now[3])
        new_edges = lax.map(jax.checkpoint(update), (index_blocks, two_low.reshape(groups, block_size, -1), edges_low.reshape(edge_shape), edge_state.reshape(edge_shape)))
        state = hidden_two
        edge_state = new_edges.reshape(edges.shape)
    return (state, edge_state)

def reference(nodes, edges, protein_ids, time_index, neighbors, edge_mask, time_table, msg_in, msg_mid, msg_out, ffn_in, ffn_out, edge_in, edge_hidden, node_gains, node_biases, ffn_bias, edge_gains, edge_biases, d_nodes, d_edges):
    integers = (protein_ids, time_index, neighbors, edge_mask)
    outputs, pullback = jax.vjp(partial(forward, integers), nodes, edges, time_table, msg_in, msg_mid, msg_out, ffn_in, ffn_out, edge_in, edge_hidden, node_gains, node_biases, ffn_bias, edge_gains, edge_biases)
    grads = pullback((d_nodes, d_edges))
    return (outputs[0], outputs[1], grads[0], grads[1], grads[2], grads[3], grads[4], grads[5], grads[6], grads[7], grads[8], grads[9], grads[10], grads[11], grads[12], grads[13], grads[14])
```

```python
import functools

import jax
import jax.numpy as jnp
from jax import lax
from jax.experimental import pallas as pl
from jax.experimental.pallas import tpu as pltpu
from jax.sharding import PartitionSpec as P

NORM_EPS = 1e-05
F32 = jnp.float32
BF16 = jnp.bfloat16
MESH = pl.DeviceIdType.MESH
LANES = 128
CHUNK = 5
TANH_A = 0.7978845608028654
TANH_B = 0.044715
B1, B2, B3, B5, SH1, SH2, GN1, GN2, FB, C1, C2, C3, C4, GE = range(14)
VECTORS = 14


def nn(left, right):
    return jnp.dot(left, right, preferred_element_type=F32)


def nt(left, right):
    return lax.dot_general(left, right, (((1,), (1,)), ((), ())), preferred_element_type=F32)


def tn(left, right):
    return lax.dot_general(left, right, (((0,), (0,)), ((), ())), preferred_element_type=F32)


def gelu_pair(z):
    sq = z * z
    half = 0.5 + 0.5 * jnp.tanh(z * (TANH_A + (TANH_A * TANH_B) * sq))
    value = z * half
    slope = half + (value * (1.0 - half)) * (2.0 * TANH_A + (6.0 * TANH_A * TANH_B) * sq)
    return value.astype(BF16), slope.astype(BF16)


def norm_parts(value):
    scale = 1.0 / value.shape[0]
    centre = jnp.sum(value, axis=0, keepdims=True) * scale
    offset = value - centre
    spread = jnp.sum(offset * offset, axis=0, keepdims=True) * scale
    rstd = lax.rsqrt(spread + NORM_EPS)
    return offset * rstd, rstd


def norm_back(hat, rstd, gain, grad):
    scale = 1.0 / hat.shape[0]
    weighted = grad * gain
    first = jnp.sum(weighted, axis=0, keepdims=True) * scale
    second = jnp.sum(weighted * hat, axis=0, keepdims=True) * scale
    return rstd * (weighted - first - hat * second)


def whole_kernel(
    res_total,
    nbr_total,
    h0_ref,
    dh_ref,
    idx_ref,
    mask_ref,
    cnt_ref,
    edges_ref,
    dedges_ref,
    vec_ref,
    w_in,
    w_et,
    w_mid,
    w_midt,
    w_out,
    f_in,
    f_outt,
    e_int,
    e_e,
    e_hid,
    e_hidt,
    nodes_out,
    edges_out,
    g_nodes,
    g_edges,
    g_in,
    g_mid,
    g_out,
    g_fin,
    g_foutt,
    g_eint,
    g_ehid,
    g_vec,
    onehot,
    eb,
    u1,
    s1,
    s2,
    w1,
    t1,
    w2,
    t2,
    psum,
    proj,
    proj_e,
    own,
    own_e,
    state,
    ext,
    joined_a,
    joined_c,
    h1b,
    act,
    slope_f,
    ubar,
    acc_mid,
    acc_e,
    acc_z,
    acc_zs,
    acc_b2,
    acc_h2,
    acc_h3,
    acc_ee,
    acc_t,
    acc_ts,
    acc_c,
    zbuf,
    vrow,
    dcur,
    g_part,
    halo_send,
    halo_recv,
    ar_part,
    ar_one,
    ar_two,
    ar_three,
    ar_tot,
    send_sem,
    recv_sem,
):
    r = lax.axis_index("res")
    n = lax.axis_index("nbr")
    core = lax.rem(n, 2)
    buddy = n + 1 - 2 * core
    across = lax.rem(n + 2, 4)
    slots = idx_ref.shape[0]
    chunks = slots // CHUNK
    width = h0_ref.shape[0]
    ew = edges_ref.shape[1]
    half_rows = width // 2
    has_prev = r > 0
    has_next = r < res_total - 1
    sem_at = [0]
    ar_at = [0]

    def next_sem():
        at = sem_at[0]
        sem_at[0] = at + 1
        return send_sem.at[at], recv_sem.at[at]

    def remote(src, dst, device):
        ss, rs = next_sem()
        return pltpu.make_async_remote_copy(
            src_ref=src, dst_ref=dst, send_sem=ss, recv_sem=rs, device_id=device, device_id_type=MESH
        )

    def vec(layer, which, rows=None):
        at = layer * VECTORS + which
        return vec_ref[0 : (width if rows is None else rows), at : at + 1]

    def put_vec(layer, which, value):
        at = layer * VECTORS + which
        g_vec[0 : value.shape[0], at : at + 1] = jnp.sum(value, axis=1, keepdims=True)

    zero_tile = jnp.zeros((width, LANES), BF16)
    for b in range(3):
        ext[b, 0] = zero_tile
        ext[b, 2] = zero_tile
        halo_recv[b, 0] = zero_tile
        halo_recv[b, 1] = zero_tile
    barrier = pltpu.get_barrier_semaphore()
    pl.semaphore_signal(barrier, inc=1, device_id=(r, buddy), device_id_type=MESH)
    pl.semaphore_signal(barrier, inc=1, device_id=(r, across), device_id_type=MESH)

    @pl.when(has_prev)
    def _():
        pl.semaphore_signal(barrier, inc=1, device_id=(r - 1, n), device_id_type=MESH)

    @pl.when(has_next)
    def _():
        pl.semaphore_signal(barrier, inc=1, device_id=(r + 1, n), device_id_type=MESH)

    peers = 2 + jnp.minimum(r, 1) + jnp.minimum(res_total - 1 - r, 1)
    pl.semaphore_wait(barrier, peers)

    def two_way(to_prev, at_prev, to_next, at_next):
        up = remote(to_prev, at_prev, (r - 1, n))
        down = remote(to_next, at_next, (r + 1, n))

        @pl.when(has_prev)
        def _():
            up.start()

        @pl.when(has_next)
        def _():
            down.start()

        @pl.when(has_prev)
        def _():
            up.wait_send()
            down.wait_recv()

        @pl.when(has_next)
        def _():
            down.wait_send()
            up.wait_recv()

    def all_reduce(value):
        at = ar_at[0] % 2
        ar_at[0] += 1
        mine = pl.multiple_of(core * half_rows, half_rows)
        theirs = pl.multiple_of(half_rows - mine, half_rows)
        ar_part[at] = value
        one = remote(ar_part.at[at, pl.ds(theirs, half_rows)], ar_one.at[at], (r, buddy))
        one.start()
        one.wait()
        ar_two[at] = ar_part[at, pl.ds(mine, half_rows)] + ar_one[at]
        two = remote(ar_two.at[at], ar_three.at[at], (r, across))
        two.start()
        two.wait()
        ar_tot[at, pl.ds(mine, half_rows)] = ar_two[at] + ar_three[at]
        span = ar_tot.at[at, pl.ds(mine, half_rows)]
        three = remote(span, span, (r, buddy))
        three.start()
        three.wait()
        return ar_tot.at[at]

    def extended(b):
        return jnp.concatenate([ext[b, 0], ext[b, 1], ext[b, 2]], axis=1)

    def halo(b, value):
        ext[b, 1] = value
        two_way(ext.at[b, 1], ext.at[b, 2], ext.at[b, 1], ext.at[b, 0])

    def halo_back(b, g_ext, g_own):
        halo_send[0] = g_ext[:, :LANES].astype(BF16)
        halo_send[1] = g_ext[:, 2 * LANES :].astype(BF16)
        g_part[...] = g_ext[:, LANES : 2 * LANES] + g_own
        two_way(halo_send.at[0], halo_recv.at[b, 1], halo_send.at[1], halo_recv.at[b, 0])
        total = g_part[...] + halo_recv[b, 0].astype(F32) + halo_recv[b, 1].astype(F32)
        return all_reduce(total)

    cells = lax.broadcasted_iota(jnp.int32, (3 * LANES, LANES), 0)

    def make_onehot(s, _):
        onehot[s] = jnp.where(cells == idx_ref[pl.ds(s, 1), :], 1.0, 0.0).astype(BF16)
        eb[0, s] = edges_ref[s].astype(BF16)
        return 0

    lax.fori_loop(0, slots, make_onehot, 0)
    counts = cnt_ref[...]
    inv_counts = 1.0 / counts

    def prepare_message(layer):
        proj[:, : 3 * LANES] = tn(w_in[layer, width : 2 * width, :], extended(layer)).astype(BF16)
        proj[:, 3 * LANES :] = w_et[layer]
        own[...] = tn(w_in[layer, :width, :], ext[layer, 1]) + vec(layer, B1)
        ubar[layer] = jnp.zeros((width, LANES), F32)

    def prepare_edge(layer):
        proj_e[:, : 3 * LANES] = nn(e_int[layer, :, width : 2 * width], extended(layer + 1)).astype(BF16)
        proj_e[:, 3 * LANES :] = e_int[layer, :, 2 * width :]
        own_e[...] = nn(e_int[layer, :, :width], ext[layer + 1, 1]) + vec(layer, C1, ew)

    def lanes_of(ref, base, *lead):
        return jnp.concatenate([ref[(*lead, base + j)] for j in range(CHUNK)], axis=1)

    def edge_at(layer, base):
        return base if layer == 0 else slots

    def message_forward(layer, base):
        rows = jnp.concatenate([lanes_of(onehot, base), lanes_of(eb, base, layer)], axis=0)
        zbuf[...] = nn(proj[...], rows)
        for j in range(CHUNK):
            z = zbuf[:, j * LANES : (j + 1) * LANES] + own[...]
            u1[layer, base + j], s1[layer, base + j] = gelu_pair(z)
        zbuf[...] = nn(w_midt[layer], lanes_of(u1, base, layer))
        for j in range(CHUNK):
            z = zbuf[:, j * LANES : (j + 1) * LANES] + vec(layer, B2)
            u2, s2[layer, base + j] = gelu_pair(z)
            ubar[layer] += u2.astype(F32) * mask_ref[pl.ds(base + j, 1), :]

    def edge_forward(layer, base, edge_ref, save):
        rows = jnp.concatenate([lanes_of(onehot, base), lanes_of(eb, base, layer)], axis=0)
        z = nn(proj_e[...], rows)
        for j in range(CHUNK):
            zj = z[:, j * LANES : (j + 1) * LANES] + own_e[...]
            w1[edge_at(layer, base) + j], t1[edge_at(layer, base) + j] = gelu_pair(zj)
        z = nn(e_hidt[layer, 0], lanes_of(w1, edge_at(layer, base)))
        for j in range(CHUNK):
            zj = z[:, j * LANES : (j + 1) * LANES] + vec(layer, C2, ew)
            w2[edge_at(layer, base) + j], t2[edge_at(layer, base) + j] = gelu_pair(zj)
        z = nn(e_hidt[layer, 1], lanes_of(w2, edge_at(layer, base)))
        for j in range(CHUNK):
            p = edge_ref[base + j] + z[:, j * LANES : (j + 1) * LANES] + vec(layer, C3, ew)
            hat, rstd = norm_parts(p)
            save(j, hat, rstd, p, hat * vec(layer, GE, ew) + vec(layer, C4, ew))

    def node_update(layer):
        total = all_reduce(ubar[layer])[...]
        high = total.astype(BF16)
        low = (total - high.astype(F32)).astype(BF16)
        sums = tn(w_out[layer], high) + tn(w_out[layer], low) + counts * vec(layer, B3)
        merged = state[layer] + sums * inv_counts
        joined_a[layer] = merged
        hat, _ = norm_parts(merged)
        hidden = hat * vec(layer, GN1) + vec(layer, SH1)
        h1b[layer] = hidden.astype(BF16)
        pre = tn(f_in[layer], h1b[layer]) + vec(layer, FB)
        act[layer], slope_f[layer] = gelu_pair(pre)
        branch = all_reduce(nn(f_outt[layer], act[layer]))[...]
        joined = hidden + (branch + vec(layer, B5))
        joined_c[layer] = joined
        hat, _ = norm_parts(joined)
        state[layer + 1] = hat * vec(layer, GN2) + vec(layer, SH2)
        halo(layer + 1, state[layer + 1].astype(BF16))

    def clear_edge():
        acc_h2[...] = jnp.zeros_like(acc_h2)
        acc_h3[...] = jnp.zeros_like(acc_h3)
        acc_ee[...] = jnp.zeros_like(acc_ee)
        acc_t[...] = jnp.zeros_like(acc_t)
        acc_ts[...] = jnp.zeros_like(acc_ts)
        acc_c[...] = jnp.zeros_like(acc_c)

    def clear_message():
        acc_mid[...] = jnp.zeros_like(acc_mid)
        acc_e[...] = jnp.zeros_like(acc_e)
        acc_z[...] = jnp.zeros_like(acc_z)
        acc_zs[...] = jnp.zeros_like(acc_zs)
        acc_b2[...] = jnp.zeros_like(acc_b2)

    def edge_backward(layer, base, parts):
        lows = []
        for j in range(CHUNK):
            hat, rstd, grad = parts(j)
            acc_c[0] += grad * hat
            acc_c[1] += grad
            dp = norm_back(hat, rstd, vec(layer, GE, ew), grad)
            g_edges[base + j] = dp
            low = dp.astype(BF16)
            acc_c[2] += low.astype(F32)
            lows.append(low)
        out = jnp.concatenate(lows, axis=1)
        acc_h3[...] += nt(lanes_of(w2, edge_at(layer, base)), out)
        grad_two = (nn(e_hid[layer, 1], out) * lanes_of(t2, edge_at(layer, base)).astype(F32)).astype(BF16)
        for j in range(CHUNK):
            acc_c[3] += grad_two[:, j * LANES : (j + 1) * LANES].astype(F32)
        acc_h2[...] += nt(lanes_of(w1, edge_at(layer, base)), grad_two)
        grad_one = (nn(e_hid[layer, 0], grad_two) * lanes_of(t1, edge_at(layer, base)).astype(F32)).astype(BF16)
        for j in range(CHUNK):
            acc_ts[...] += grad_one[:, j * LANES : (j + 1) * LANES].astype(F32)
        acc_t[...] += nt(grad_one, lanes_of(onehot, base))
        acc_ee[...] += nt(grad_one, lanes_of(eb, base, layer))
        back = nn(e_e[layer], grad_one)
        for j in range(CHUNK):
            g_edges[base + j] += back[:, j * LANES : (j + 1) * LANES]

    def edge_finish(layer):
        put_vec(layer, GE, acc_c[0])
        put_vec(layer, C4, acc_c[1])
        put_vec(layer, C3, acc_c[2])
        put_vec(layer, C2, acc_c[3])
        put_vec(layer, C1, acc_ts[...])
        g_ehid[layer, 0] = acc_h2[...].astype(BF16)
        g_ehid[layer, 1] = acc_h3[...].astype(BF16)
        table = acc_t[...].astype(BF16)
        sums = acc_ts[...].astype(BF16)
        g_eint[layer, :, :width] = nt(sums, ext[layer + 1, 1]).astype(BF16)
        g_eint[layer, :, width : 2 * width] = nt(table, extended(layer + 1)).astype(BF16)
        g_eint[layer, :, 2 * width :] = acc_ee[...].astype(BF16)
        g_ext = tn(e_int[layer, :, width : 2 * width], table)
        g_own = tn(e_int[layer, :, :width], sums)
        return g_ext, g_own

    def message_backward(layer, base, add_edge):
        grads = []
        for j in range(CHUNK):
            s = base + j
            dz = (vrow[...] * mask_ref[pl.ds(s, 1), :] * s2[layer, s].astype(F32)).astype(BF16)
            acc_b2[...] += dz.astype(F32)
            grads.append(dz)
        grad_two = jnp.concatenate(grads, axis=1)
        acc_mid[...] += nt(lanes_of(u1, base, layer), grad_two)
        zbuf[...] = nn(w_mid[layer], grad_two)
        grads = []
        for j in range(CHUNK):
            s = base + j
            dz = (zbuf[:, j * LANES : (j + 1) * LANES] * s1[layer, s].astype(F32)).astype(BF16)
            acc_zs[...] += dz.astype(F32)
            grads.append(dz)
        grad_one = jnp.concatenate(grads, axis=1)
        acc_z[...] += nt(grad_one, lanes_of(onehot, base))
        acc_e[...] += nt(lanes_of(eb, base, layer), grad_one)
        back = nn(w_in[layer, 2 * width :, :], grad_one)
        for j in range(CHUNK):
            add_edge(base + j, back[:, j * LANES : (j + 1) * LANES])

    def message_finish(layer):
        put_vec(layer, B2, acc_b2[...])
        put_vec(layer, B1, acc_zs[...])
        g_mid[layer] = acc_mid[...].astype(BF16)
        table = acc_z[...].astype(BF16)
        sums = acc_zs[...].astype(BF16)
        g_in[layer, :width] = nt(ext[layer, 1], sums).astype(BF16)
        g_in[layer, width : 2 * width] = nt(extended(layer), table).astype(BF16)
        g_in[layer, 2 * width :] = acc_e[...].astype(BF16)
        g_ext = nn(w_in[layer, width : 2 * width, :], table)
        g_own = nn(w_in[layer, :width, :], sums)
        return g_ext, g_own

    def node_back(layer):
        grad = dcur[...]
        hat, rstd = norm_parts(joined_c[layer])
        put_vec(layer, GN2, grad * hat)
        put_vec(layer, SH2, grad)
        dc = norm_back(hat, rstd, vec(layer, GN2), grad)
        dy = dc.astype(BF16)
        put_vec(layer, B5, dy.astype(F32))
        df = (tn(f_outt[layer], dy) * slope_f[layer].astype(F32)).astype(BF16)
        put_vec(layer, FB, df.astype(F32))
        total = all_reduce(nn(f_in[layer], df))
        g_foutt[layer] = nt(dy, act[layer]).astype(BF16)
        g_fin[layer] = nt(h1b[layer], df).astype(BF16)
        grad = dc + total[...]
        hat, rstd = norm_parts(joined_a[layer])
        put_vec(layer, GN1, grad * hat)
        put_vec(layer, SH1, grad)
        da = norm_back(hat, rstd, vec(layer, GN1), grad)
        dcur[...] = da
        ds = (da * inv_counts).astype(BF16)
        put_vec(layer, B3, ds.astype(F32) * counts)
        g_out[layer] = nt(ubar[layer].astype(BF16), ds).astype(BF16)
        vrow[...] = nn(w_out[layer], ds)

    state[0] = h0_ref[...]
    halo(0, state[0].astype(BF16))
    prepare_message(0)

    def loop_a(i, _):
        message_forward(0, i * CHUNK)
        return 0

    lax.fori_loop(0, chunks, loop_a, 0)
    node_update(0)
    prepare_edge(0)
    prepare_message(1)

    def loop_b(i, _):
        base = i * CHUNK

        def save(j, hat, rstd, p, value):
            psum[base + j] = p
            edges_out[base + j] = value
            eb[1, base + j] = value.astype(BF16)

        edge_forward(0, base, edges_ref, save)
        message_forward(1, base)
        return 0

    lax.fori_loop(0, chunks, loop_b, 0)
    node_update(1)
    nodes_out[...] = state[2].T
    prepare_edge(1)
    clear_edge()

    def loop_c(i, _):
        base = i * CHUNK
        kept = {}

        def save(j, hat, rstd, p, value):
            edges_out[base + j] = value
            kept[j] = (hat, rstd)

        edge_forward(1, base, edges_out, save)
        edge_backward(1, base, lambda j: (*kept[j], dedges_ref[base + j]))
        return 0

    lax.fori_loop(0, chunks, loop_c, 0)
    g_ext, g_own = edge_finish(1)
    dcur[...] = dh_ref[...] + halo_back(0, g_ext, g_own)[...]
    node_back(1)
    clear_message()
    clear_edge()

    def loop_d(i, _):
        base = i * CHUNK

        def add_edge(s, value):
            g_edges[s] += value

        message_backward(1, base, add_edge)
        edge_backward(0, base, lambda j: (*norm_parts(psum[base + j]), g_edges[base + j]))
        return 0

    lax.fori_loop(0, chunks, loop_d, 0)
    m_ext, m_own = message_finish(1)
    e_ext, e_own = edge_finish(0)
    dcur[...] += halo_back(1, m_ext + e_ext, m_own + e_own)[...]
    node_back(0)
    clear_message()

    def loop_e(i, _):
        base = i * CHUNK

        def add_edge(s, value):
            g_edges[s] = g_edges[s] + value

        message_backward(0, base, add_edge)
        return 0

    lax.fori_loop(0, chunks, loop_e, 0)
    m_ext, m_own = message_finish(0)
    final = dcur[...] + halo_back(2, m_ext, m_own)[...]
    g_nodes[...] = final.T


def vmem(shape, dtype):
    return pltpu.VMEM(shape, dtype)


def run_whole(h0, dh, idx, mask, counts, edges, d_edges, vectors, weights, res_total, nbr_total):
    width, lanes = h0.shape
    slots, ew, _ = edges.shape
    w_in, f_in = weights[0], weights[5]
    layers, rows_in, _ = w_in.shape
    ff = f_in.shape[2]
    out_shape = (
        jax.ShapeDtypeStruct((lanes, width), F32),
        jax.ShapeDtypeStruct((slots, ew, lanes), F32),
        jax.ShapeDtypeStruct((lanes, width), F32),
        jax.ShapeDtypeStruct((slots, ew, lanes), F32),
        jax.ShapeDtypeStruct((layers, rows_in, width), BF16),
        jax.ShapeDtypeStruct((layers, width, width), BF16),
        jax.ShapeDtypeStruct((layers, width, width), BF16),
        jax.ShapeDtypeStruct((layers, width, ff), BF16),
        jax.ShapeDtypeStruct((layers, width, ff), BF16),
        jax.ShapeDtypeStruct((layers, ew, rows_in), BF16),
        jax.ShapeDtypeStruct((layers, 2, ew, ew), BF16),
        jax.ShapeDtypeStruct((width, 32), F32),
    )
    per_slot = lambda rows: vmem((layers, slots, rows, lanes), BF16)
    scratch = [
        vmem((slots, 3 * lanes, lanes), BF16),
        per_slot(ew),
        per_slot(width),
        per_slot(width),
        per_slot(width),
        vmem((slots + CHUNK, ew, lanes), BF16),
        vmem((slots + CHUNK, ew, lanes), BF16),
        vmem((slots + CHUNK, ew, lanes), BF16),
        vmem((slots + CHUNK, ew, lanes), BF16),
        vmem((slots, ew, lanes), F32),
        vmem((width, 3 * lanes + ew), BF16),
        vmem((ew, 3 * lanes + ew), BF16),
        vmem((width, lanes), F32),
        vmem((ew, lanes), F32),
        vmem((3, width, lanes), F32),
        vmem((3, 3, width, lanes), BF16),
        vmem((layers, width, lanes), F32),
        vmem((layers, width, lanes), F32),
        vmem((layers, width, lanes), BF16),
        vmem((layers, ff, lanes), BF16),
        vmem((layers, ff, lanes), BF16),
        vmem((layers, width, lanes), F32),
        vmem((width, width), F32),
        vmem((ew, width), F32),
        vmem((width, 3 * lanes), F32),
        vmem((width, lanes), F32),
        vmem((width, lanes), F32),
        vmem((ew, ew), F32),
        vmem((ew, ew), F32),
        vmem((ew, ew), F32),
        vmem((ew, 3 * lanes), F32),
        vmem((ew, lanes), F32),
        vmem((4, ew, lanes), F32),
        vmem((width, CHUNK * lanes), F32),
        vmem((width, lanes), F32),
        vmem((width, lanes), F32),
        vmem((width, lanes), F32),
        vmem((2, width, lanes), BF16),
        vmem((3, 2, width, lanes), BF16),
        vmem((2, width, lanes), F32),
        vmem((2, width // 2, lanes), F32),
        vmem((2, width // 2, lanes), F32),
        vmem((2, width // 2, lanes), F32),
        vmem((2, width, lanes), F32),
        pltpu.SemaphoreType.DMA((48,)),
        pltpu.SemaphoreType.DMA((48,)),
    ]
    operands = (h0, dh, idx, mask, counts, edges, d_edges, vectors, *weights)
    return pl.pallas_call(
        functools.partial(whole_kernel, res_total, nbr_total),
        out_shape=out_shape,
        in_specs=[pl.BlockSpec(memory_space=pltpu.VMEM)] * len(operands),
        out_specs=[pl.BlockSpec(memory_space=pltpu.VMEM)] * len(out_shape),
        scratch_shapes=scratch,
        compiler_params=pltpu.CompilerParams(
            collective_id=1, has_side_effects=True, vmem_limit_bytes=62 * 1024 * 1024
        ),
    )(*operands)


def gather_all(value, res_dim, nbr_dim):
    value = lax.all_gather(value, "res", axis=res_dim, tiled=True)
    return lax.all_gather(value, "nbr", axis=nbr_dim, tiled=True)


def scatter_sum(value, res_dim, nbr_dim):
    value = lax.psum_scatter(value, "res", scatter_dimension=res_dim, tiled=True)
    return lax.psum_scatter(value, "nbr", scatter_dimension=nbr_dim, tiled=True).astype(F32)


def per_device(
    nodes,
    edges,
    protein_ids,
    time_index,
    neighbors,
    edge_mask,
    time_table,
    msg_in,
    msg_mid,
    msg_out,
    ffn_in,
    ffn_out,
    edge_in,
    edge_hidden,
    node_gains,
    node_biases,
    ffn_bias,
    edge_gains,
    edge_biases,
    d_nodes,
    d_edges,
):
    res_total, nbr_total = lax.axis_size("res"), lax.axis_size("nbr")
    width = nodes.shape[1]
    ew = edges.shape[2]
    row_count, slot_count = neighbors.shape
    own_rows = nodes.shape[0]
    layers = msg_in.shape[0]
    n_at = lax.axis_index("nbr")
    ff = ffn_bias.shape[1] // nbr_total

    low = lambda a: a.astype(BF16)
    table_low = gather_all(low(time_table), 0, 1)
    w_in = gather_all(low(msg_in), 1, 2)
    w_mid = gather_all(low(msg_mid), 1, 2)
    w_out = gather_all(low(msg_out), 1, 2)
    e_in = gather_all(low(edge_in), 1, 2)
    e_hid = gather_all(low(edge_hidden), 2, 3)
    f_in = lax.all_gather(low(ffn_in), "res", axis=1, tiled=True)
    f_outt = lax.all_gather(jnp.swapaxes(low(ffn_out), 1, 2), "res", axis=1, tiled=True)
    weights = (
        w_in,
        jnp.swapaxes(w_in[:, 2 * width :], 1, 2),
        w_mid,
        jnp.swapaxes(w_mid, 1, 2),
        w_out,
        f_in,
        f_outt,
        jnp.swapaxes(e_in, 1, 2),
        e_in[:, 2 * width :],
        e_hid,
        jnp.swapaxes(e_hid, 2, 3),
    )
    matches = protein_ids[:, None] == jnp.arange(time_index.shape[0], dtype=jnp.int32)[None, :]
    step_rows = jnp.sum(jnp.where(matches, time_index[None, :], 0), axis=1)
    step_onehot = (
        step_rows[:, None] == jnp.arange(table_low.shape[0], dtype=jnp.int32)[None, :]
    ).astype(BF16)
    state = nodes + jnp.dot(step_onehot, table_low, preferred_element_type=F32)
    mask_rows = edge_mask.astype(F32).T
    count_row = jnp.sum(mask_rows, axis=0)
    count_block = jnp.zeros((8, width), F32).at[0, :row_count].set(count_row)
    packed = lax.all_gather(jnp.concatenate([state, d_nodes, count_block], axis=0), "nbr", axis=0)
    h0 = packed[:, :own_rows].reshape(row_count, width).T
    dh = packed[:, own_rows : 2 * own_rows].reshape(row_count, width).T
    counts = jnp.sum(packed[:, 2 * own_rows, :row_count], axis=0)[None, :]
    base_row = lax.axis_index("res") * row_count - row_count
    idx = (neighbors - base_row).T

    pad_edge = lambda a: jnp.pad(a, ((0, 0), (0, 0), (0, width - ew)))
    own_bias = lax.dynamic_slice_in_dim(ffn_bias, n_at * ff, ff, axis=1)
    table = jnp.concatenate(
        [
            node_biases,
            node_gains,
            jnp.pad(own_bias, ((0, 0), (0, width - ff)))[:, None],
            pad_edge(edge_biases),
            pad_edge(edge_gains[:, None]),
        ],
        axis=1,
    )
    vectors = jnp.pad(table.reshape(layers * VECTORS, width), ((0, 32 - layers * VECTORS), (0, 0))).T

    results = run_whole(
        h0,
        dh,
        idx,
        mask_rows,
        counts,
        jnp.transpose(edges, (1, 2, 0)),
        jnp.transpose(d_edges, (1, 2, 0)),
        vectors,
        weights,
        res_total,
        nbr_total,
    )
    nodes_all, edges_t, g_nodes_all, g_edges_t, g_in, g_mid, g_out, g_fin, g_foutt, g_eint, g_ehid, g_vec = results
    mine = lambda a: lax.dynamic_slice_in_dim(a, n_at * own_rows, own_rows, axis=0)
    g_nodes = mine(g_nodes_all)
    g_table_full = lax.dot_general(
        step_onehot.astype(F32),
        g_nodes,
        (((0,), (0,)), ((), ())),
        precision=lax.Precision.HIGHEST,
        preferred_element_type=F32,
    )
    g_rows = g_vec.T[: layers * VECTORS].reshape(layers, VECTORS, width)
    shared = g_rows[:, B3 : GN2 + 1] * (1.0 / nbr_total)
    g_bias_ffn = lax.dynamic_update_slice_in_dim(
        jnp.zeros_like(ffn_bias), g_rows[:, FB, :ff], n_at * ff, axis=1
    )
    g_node_biases, g_node_gains, g_ffn_bias, g_edge_biases, g_edge_gains = lax.psum(
        (
            jnp.concatenate([g_rows[:, : B3], shared[:, : SH2 + 1 - B3]], axis=1),
            shared[:, GN1 - B3 :],
            g_bias_ffn,
            g_rows[:, C1 : C4 + 1, :ew],
            g_rows[:, GE, :ew],
        ),
        ("res", "nbr"),
    )
    return (
        mine(nodes_all),
        jnp.transpose(edges_t, (2, 0, 1)),
        g_nodes,
        jnp.transpose(g_edges_t, (2, 0, 1)),
        scatter_sum(low(g_table_full), 0, 1),
        scatter_sum(g_in, 1, 2),
        scatter_sum(g_mid, 1, 2),
        scatter_sum(g_out, 1, 2),
        lax.psum_scatter(g_fin, "res", scatter_dimension=1, tiled=True).astype(F32),
        jnp.swapaxes(
            lax.psum_scatter(g_foutt, "res", scatter_dimension=1, tiled=True), 1, 2
        ).astype(F32),
        jnp.swapaxes(scatter_sum(g_eint, 2, 1), 1, 2),
        scatter_sum(g_ehid, 2, 3),
        g_node_gains,
        g_node_biases,
        g_ffn_bias,
        g_edge_gains,
        g_edge_biases,
    )


def solution(mesh):
    return jax.shard_map(
        per_device,
        mesh=mesh,
        in_specs=(
            P(("res", "nbr"), None),
            P("res", "nbr", None),
            P(("res", "nbr")),
            P(),
            P("res", "nbr"),
            P("res", "nbr"),
            P("res", "nbr"),
            P(None, "res", "nbr"),
            P(None, "res", "nbr"),
            P(None, "res", "nbr"),
            P(None, "res", "nbr"),
            P(None, "nbr", "res"),
            P(None, "res", "nbr"),
            P(None, None, "res", "nbr"),
            P(),
            P(),
            P(),
            P(),
            P(),
            P(("res", "nbr"), None),
            P("res", "nbr", None),
        ),
        out_specs=(
            P(("res", "nbr"), None),
            P("res", "nbr", None),
            P(("res", "nbr"), None),
            P("res", "nbr", None),
            P("res", "nbr"),
            P(None, "res", "nbr"),
            P(None, "res", "nbr"),
            P(None, "res", "nbr"),
            P(None, "res", "nbr"),
            P(None, "nbr", "res"),
            P(None, "res", "nbr"),
            P(None, None, "res", "nbr"),
            P(),
            P(),
            P(),
            P(),
            P(),
        ),
        check_vma=False,
    )
```

```python
import functools

import jax
import jax.numpy as jnp
from jax import lax
from jax.experimental import pallas as pl
from jax.experimental.pallas import tpu as pltpu
from jax.sharding import PartitionSpec as P

NORM_EPS = 1e-05
F32 = jnp.float32
BF16 = jnp.bfloat16
MESH = pl.DeviceIdType.MESH
LANES = 128
CHUNK = 5
TANH_A = 0.7978845608028654
TANH_B = 0.044715
B1, B2, B3, B5, SH1, SH2, GN1, GN2, FB, C1, C2, C3, C4, GE = range(14)
VECTORS = 14
VEC_ROWS = {B1: 0, B2: 1, B3: 2, B5: 3, SH1: 4, SH2: 5, GN1: 6, GN2: 7, FB: 8, C1: 12, C2: 13, C3: 14, C4: 15, GE: 16}
VEC_PER_LAYER = 20
IN0, TB, MO0, FF0, ED, IN1, MO1, FF1 = range(8)
IN, MO, FF = (IN0, IN1), (MO0, MO1), (FF0, FF1)
BY_CORE, BY_X, BY_Y, BY_Z = range(4)


def nn(left, right):
    return jnp.dot(left, right, preferred_element_type=F32)


def nt(left, right):
    return lax.dot_general(left, right, (((1,), (1,)), ((), ())), preferred_element_type=F32)


def tn(left, right):
    return lax.dot_general(left, right, (((0,), (0,)), ((), ())), preferred_element_type=F32)


def gelu_pair(z):
    sq = z * z
    half = 0.5 + 0.5 * jnp.tanh(z * (TANH_A + (TANH_A * TANH_B) * sq))
    value = z * half
    slope = half + (value * (1.0 - half)) * (2.0 * TANH_A + (6.0 * TANH_A * TANH_B) * sq)
    return value.astype(BF16), slope.astype(BF16)


def norm_parts(value):
    scale = 1.0 / value.shape[0]
    centre = jnp.sum(value, axis=0, keepdims=True) * scale
    offset = value - centre
    spread = jnp.sum(offset * offset, axis=0, keepdims=True) * scale
    rstd = lax.rsqrt(spread + NORM_EPS)
    return offset * rstd, rstd


def norm_back(hat, rstd, gain, grad):
    scale = 1.0 / hat.shape[0]
    weighted = grad * gain
    first = jnp.sum(weighted, axis=0, keepdims=True) * scale
    second = jnp.sum(weighted * hat, axis=0, keepdims=True) * scale
    return rstd * (weighted - first - hat * second)


class Refs:
    def __init__(self, names, values):
        self.__dict__.update(zip(names, values, strict=True))


def up_to(value, step):
    return (value + step - 1) // step * step


class Plan:
    def __init__(self, res_total, nbr_total, slots, width, ew, ff, layers, shards):
        self.res_total, self.nbr_total = res_total, nbr_total
        self.slots, self.width, self.ew, self.ff, self.layers = slots, width, ew, ff, layers
        self.k_in, self.k_mid, self.k_hid, self.k_time = shards
        self.fast = (res_total, nbr_total) == (8, 4) and self.k_in % 8 == 0 and self.k_mid % 16 == 0
        acts = slots * width
        self.acts = [0, 3 * acts]
        self.act_rows = acts
        edge_rows = (slots + CHUNK) * ew
        self.pool_rows = 6 * acts + 4 * edge_rows
        self.edge_at = 6 * acts
        self.edge_rows = edge_rows
        if not self.fast:
            return
        self.in_pad = up_to(self.k_in, 16)
        self.hid_pad = up_to(self.k_hid, 16)
        self.in_rows = self.in_pad
        self.mo_rows = 2 * self.k_mid
        self.ed_rows = self.in_pad + 2 * self.hid_pad
        self.tb_rows = self.k_time
        self.ff_rows = 2 * self.k_mid * (ff // LANES)
        one = 3 * acts
        sizes = {IN0: self.in_rows, MO0: self.mo_rows, ED: self.ed_rows, IN1: self.in_rows,
                 MO1: self.mo_rows, TB: self.tb_rows, FF0: self.ff_rows, FF1: self.ff_rows}
        self.sizes = sizes
        self.stage = {}
        at = 0
        for item in (IN0, TB, MO0):
            self.stage[item] = at
            at += 32 * sizes[item]
        at = one
        for item in (IN1, MO1, ED):
            self.stage[item] = at
            at += 32 * sizes[item]
        for item in (FF0, FF1):
            self.stage[item] = at
            at += 8 * sizes[item]
        top = at
        self.source, self.recv = {}, {}
        at = 0
        for item in (IN0, MO0):
            self.source[item] = at
            at += 32 * sizes[item]
        at = one
        for item in (IN1, MO1, ED):
            self.source[item] = at
            at += 32 * sizes[item]
        for stage, count in ((BY_CORE, 16), (BY_X, 8), (BY_Y, 4)):
            self.recv[ED, stage] = at
            at += count * sizes[ED]
        at = max(at, 2 * one)
        self.source[FF1] = at
        self.recv[FF1, BY_Y] = at + 8 * sizes[FF1]
        at += 12 * sizes[FF1]
        for stage, count in ((BY_CORE, 16), (BY_X, 8), (BY_Y, 4)):
            for item, twin in ((IN1, IN0), (MO1, MO0)):
                self.recv[item, stage] = self.recv[twin, stage] = at
                at += count * sizes[item]
        top = max(top, at)
        self.edge_at = top
        self.source[FF0] = top
        self.recv[FF0, BY_Y] = top + 8 * sizes[FF0]
        at = top + max(4 * edge_rows, 12 * sizes[FF0])
        self.source[TB] = at
        at += 32 * sizes[TB]
        for stage, count in ((BY_CORE, 16), (BY_X, 8), (BY_Y, 4)):
            self.recv[TB, stage] = at
            at += count * sizes[TB]
        for item in sizes:
            self.recv[item, BY_Z] = at
            at += 3 * sizes[item]
        self.pool_rows = at


def whole_kernel(plan, names, *values):
    refs = Refs(names, values)
    fast = plan.fast
    mask_ref, vec_ref = refs.mask_rows, refs.vectors
    onehot, eb, pool, psum, proj, proj_e = refs.onehot, refs.eb, refs.pool, refs.psum, refs.proj, refs.proj_e
    own, own_e, state, ext = refs.own, refs.own_e, refs.state, refs.ext
    joined_a, joined_c, h1b, act = refs.joined_a, refs.joined_c, refs.h1b, refs.act
    slope_f, ubar, ds_ref = refs.slope_f, refs.ubar, refs.ds
    acc_mid, acc_e, acc_z, acc_zs, acc_b2 = refs.acc_mid, refs.acc_e, refs.acc_z, refs.acc_zs, refs.acc_b2
    acc_h2, acc_h3, acc_ee = refs.acc_h2, refs.acc_h3, refs.acc_ee
    acc_t, acc_ts, acc_c = refs.acc_t, refs.acc_ts, refs.acc_c
    wide, vrow, dcur, g_part = refs.wide, refs.vrow, refs.dcur, refs.g_part
    halo_send, halo_recv = refs.halo_send, refs.halo_recv
    ar_part, ar_one, ar_two, ar_three = refs.ar_part, refs.ar_one, refs.ar_two, refs.ar_three
    ar_tot = refs.ar_tot
    w_in, w_et, w_mid, w_midt, w_out = refs.w_in, refs.w_et, refs.w_mid, refs.w_midt, refs.w_out
    f_in, f_outt, e_int, e_e = refs.f_in, refs.f_outt, refs.e_int, refs.e_e
    e_hid, e_hidt = refs.e_hid, refs.e_hidt
    nodes_out, edges_out, g_nodes, g_edges = refs.nodes_out, refs.edges_out, refs.g_nodes, refs.g_edges
    cnt_ref = refs.counts
    res_total = plan.res_total
    slots, width, ew, ff = plan.slots, plan.width, plan.ew, plan.ff
    r = lax.axis_index("res")
    n = lax.axis_index("nbr")
    core = lax.rem(n, 2)
    xx = n // 2
    yy = lax.rem(r, 2)
    zz = r // 2
    buddy = n + 1 - 2 * core
    across = lax.rem(n + 2, 4)
    chunks = slots // CHUNK
    half_rows = width // 2
    has_prev = r > 0
    has_next = r < res_total - 1
    sem_at = [0]
    ar_at = [0]

    greeted = [(r, buddy), (r, across)]
    z_peers = []
    if fast:
        greeted.append((r, lax.rem(buddy + 2, 4)))
        y_peer = (r + 1 - 2 * yy, n)
        z_peers = [(2 * lax.rem(zz + k, 4) + yy, n) for k in (1, 2, 3)]
        greeted += [y_peer, *z_peers]
        up_too = jnp.logical_and(yy == 0, has_prev)
        down_too = jnp.logical_and(yy == 1, has_next)
    else:
        up_too, down_too = has_prev, has_next
    barrier = pltpu.get_barrier_semaphore()
    for device in greeted:
        pl.semaphore_signal(barrier, inc=1, device_id=device, device_id_type=MESH)

    @pl.when(up_too)
    def _():
        pl.semaphore_signal(barrier, inc=1, device_id=(r - 1, n), device_id_type=MESH)

    @pl.when(down_too)
    def _():
        pl.semaphore_signal(barrier, inc=1, device_id=(r + 1, n), device_id_type=MESH)

    greetings = (len(greeted) + up_too.astype(jnp.int32) + down_too.astype(jnp.int32))

    zero_tile = jnp.zeros((width, LANES), BF16)

    @pl.when(jnp.logical_not(has_prev))
    def _():
        for b in range(3):
            ext[b, 0] = zero_tile
            halo_recv[b, 0] = zero_tile

    @pl.when(jnp.logical_not(has_next))
    def _():
        for b in range(3):
            ext[b, 2] = zero_tile
            halo_recv[b, 1] = zero_tile

    def next_sem():
        at = sem_at[0]
        sem_at[0] = at + 1
        return refs.send_sem.at[at], refs.recv_sem.at[at]

    def remote(src, dst, device):
        ss, rs = next_sem()
        return pltpu.make_async_remote_copy(
            src_ref=src, dst_ref=dst, send_sem=ss, recv_sem=rs, device_id=device, device_id_type=MESH
        )

    def start(copies):
        for copy in copies:
            copy.start()

    def wait(copies):
        for copy in copies:
            copy.wait()

    def rows_of(at, count):
        return pool.at[pl.ds(at, count)]

    def aligned(at):
        return pl.multiple_of(at, 16)

    def vec(layer, which, rows=None):
        at = layer * VECTORS + which
        return vec_ref[0 : (width if rows is None else rows), at : at + 1]

    def put_vec(layer, which, value):
        at = layer * VECTORS + which
        refs.g_vec[0 : value.shape[0], at : at + 1] = jnp.sum(value, axis=1, keepdims=True)

    load_edges = pltpu.make_async_copy(refs.edges, g_edges, refs.local_sem.at[0])
    load_edges.start()

    def two_way(to_prev, at_prev, to_next, at_next):
        up = remote(to_prev, at_prev, (r - 1, n))
        down = remote(to_next, at_next, (r + 1, n))

        def begin():
            pl.when(has_prev)(up.start)
            pl.when(has_next)(down.start)

        def finish():
            @pl.when(has_prev)
            def _():
                up.wait_send()
                down.wait_recv()

            @pl.when(has_next)
            def _():
                down.wait_send()
                up.wait_recv()

        return begin, finish

    def all_reduce(value, short=False):
        at = ar_at[0] % 2
        ar_at[0] += 1
        mine = pl.multiple_of(core * half_rows, half_rows)
        theirs = pl.multiple_of(half_rows - mine, half_rows)
        ar_part[at] = value
        one = remote(ar_part.at[at, pl.ds(theirs, half_rows)], ar_one.at[at], (r, buddy))
        one.start()
        one.wait()
        sent, got = (refs.ar_two_low, refs.ar_three_low) if short else (ar_two, ar_three)
        sent[at] = (ar_part[at, pl.ds(mine, half_rows)] + ar_one[at]).astype(sent.dtype)
        two = remote(sent.at[at], got.at[at], (r, across))
        two.start()
        two.wait()
        ar_tot[at, pl.ds(mine, half_rows)] = sent[at].astype(F32) + got[at].astype(F32)
        span = ar_tot.at[at, pl.ds(mine, half_rows)]
        three = remote(span, span, (r, buddy))
        three.start()
        three.wait()
        return ar_tot.at[at]

    def extended(b):
        return jnp.concatenate([ext[b, 0], ext[b, 1], ext[b, 2]], axis=1)

    def halo(b, value):
        ext[b, 1] = value
        begin, finish = two_way(ext.at[b, 1], ext.at[b, 2], ext.at[b, 1], ext.at[b, 0])
        begin()
        return finish

    def halo_back(b, g_ext, g_own):
        halo_send[0] = g_ext[:, :LANES].astype(BF16)
        halo_send[1] = g_ext[:, 2 * LANES :].astype(BF16)
        g_part[...] = g_ext[:, LANES : 2 * LANES] + g_own
        begin, finish = two_way(halo_send.at[0], halo_recv.at[b, 1], halo_send.at[1], halo_recv.at[b, 0])
        begin()
        finish()
        total = g_part[...] + halo_recv[b, 0].astype(F32) + halo_recv[b, 1].astype(F32)
        return all_reduce(total, short=True)

    FULL = (IN0, MO0, TB, ED, IN1, MO1)
    shard_at = ((core * 2 + xx) * 2 + yy) * 4 + zz
    short_at = yy * 4 + zz

    def my_shard(item):
        at = shard_at if item in FULL else short_at
        return aligned(plan.stage[item] + at * plan.sizes[item])

    def gather_z(item):
        size = plan.sizes[item]
        span = rows_of(my_shard(item), size)
        return [remote(span, span, peer) for peer in z_peers]

    def gather_span(item, count, device):
        size = plan.sizes[item]
        at = shard_at if item in FULL else short_at
        span = rows_of(aligned(plan.stage[item] + (at // count) * (count * size)), count * size)
        return [remote(span, span, device)]

    def gather_y(item):
        return gather_span(item, 4, y_peer)

    def gather_x(item):
        return gather_span(item, 8, (r, across))

    def gather_c(item):
        return gather_span(item, 16, (r, buddy))

    def add_rows(at, other, count):
        block = next(b for b in (512, 256, 128, 64, 32, 16) if count % b == 0)

        def step(i, _):
            to = pl.ds(aligned(at + i * block), block)
            pool[to] = (pool[to].astype(F32) + pool[pl.ds(aligned(other + i * block), block)].astype(F32)).astype(BF16)
            return 0

        lax.fori_loop(0, count // block, step, 0)

    def reduce_pairs(item, stage):
        size, source = plan.sizes[item], plan.source[item]
        if stage == BY_CORE:
            count, mine, theirs, device = 16, core, 1 - core, (r, buddy)
        elif stage == BY_X:
            count, mine, theirs, device = 8, core * 2 + xx, core * 2 + 1 - xx, (r, across)
        else:
            base = (core * 2 + xx) * 2 if item in FULL else 0
            count, mine, theirs, device = 4, base + yy, base + 1 - yy, y_peer
        arrived = plan.recv[item, stage]
        copy = remote(
            rows_of(aligned(source + theirs * (count * size)), count * size),
            rows_of(arrived, count * size),
            device,
        )
        return [copy], lambda: add_rows(aligned(source + mine * (count * size)), arrived, count * size)

    def reduce_z(item):
        size, source = plan.sizes[item], plan.source[item]
        base = ((core * 2 + xx) * 2 + yy) * 4 if item in FULL else yy * 4
        copies = []
        for k in (1, 2, 3):
            to = lax.rem(zz + k, 4)
            copies.append(
                remote(
                    rows_of(aligned(source + (base + to) * size), size),
                    rows_of(plan.recv[item, BY_Z] + (k - 1) * size, size),
                    z_peers[k - 1],
                )
            )

        def total(first, count):
            value = pool[pl.ds(aligned(source + (base + zz) * size + first), count)].astype(F32)
            for k in range(3):
                value += pool[pl.ds(plan.recv[item, BY_Z] + k * size + first, count)].astype(F32)
            return value

        return copies, total

    def blocks():
        for at in range(32):
            c, x, y, z = at // 16, at // 8 % 2, at // 4 % 2, at % 4
            yield at, 2 * z + y, 2 * x + c

    def assemble_in(layer):
        at = plan.stage[IN[layer]]
        for k, rr, nn_ in blocks():
            wide[rr * plan.k_in : (rr + 1) * plan.k_in, nn_ * LANES : (nn_ + 1) * LANES] = pool[
                at + k * plan.in_rows : at + k * plan.in_rows + plan.k_in
            ].astype(F32)
        w_in[layer] = wide[: w_in.shape[1], :width].astype(BF16)
        turned = wide[2 * width : 2 * width + 2 * LANES, :width].T
        w_et[layer] = turned[:, :ew].astype(BF16)

    def assemble_mo(layer):
        at = plan.stage[MO[layer]]
        k_mid = plan.k_mid
        for k, rr, nn_ in blocks():
            to = (layer, slice(rr * k_mid, (rr + 1) * k_mid), slice(nn_ * LANES, (nn_ + 1) * LANES))
            first = at + k * plan.mo_rows
            w_mid[to] = pool[first : first + k_mid]
            w_out[to] = pool[first + k_mid : first + 2 * k_mid]
        w_midt[layer] = w_mid[layer].astype(F32).T.astype(BF16)

    def turn_square(value):
        wide[:ew, :ew] = value
        return wide[: 2 * LANES, : 2 * LANES].T[:ew, :ew]

    def assemble_edge():
        at, cols = plan.stage[ED], ew // 4
        long = up_to(w_in.shape[1], LANES)
        for k, rr, nn_ in blocks():
            first = at + k * plan.ed_rows
            wide[rr * plan.k_in : (rr + 1) * plan.k_in, nn_ * LANES : (nn_ + 1) * LANES] = pool[
                first : first + plan.k_in
            ].astype(F32)
        for nn_ in range(4):
            turned = wide[:long, nn_ * LANES : (nn_ + 1) * LANES].T
            for layer in range(2):
                e_int[layer, nn_ * cols : (nn_ + 1) * cols] = turned[
                    layer * cols : (layer + 1) * cols, : w_in.shape[1]
                ].astype(BF16)
        for layer in range(2):
            for k, rr, nn_ in blocks():
                first = at + k * plan.ed_rows + plan.in_pad + layer * plan.hid_pad
                wide[rr * plan.k_hid : (rr + 1) * plan.k_hid, nn_ * LANES : (nn_ + 1) * LANES] = pool[
                    first : first + plan.k_hid
                ].astype(F32)
            for nn_ in range(4):
                turned = wide[: 2 * LANES, nn_ * LANES : (nn_ + 1) * LANES].T
                for m in range(2):
                    e_hidt[layer, m, nn_ * cols : (nn_ + 1) * cols] = turned[
                        m * cols : (m + 1) * cols, :ew
                    ].astype(BF16)
        for layer in range(2):
            e_e[layer] = turn_square(e_int[layer, :, 2 * width :].astype(F32)).astype(BF16)
            for m in range(2):
                e_hid[layer, m] = turn_square(e_hidt[layer, m].astype(F32)).astype(BF16)

    def assemble_ffn(layer):
        at, k_mid = plan.stage[FF[layer]], plan.k_mid
        for y in range(2):
            for z in range(4):
                rr = 2 * z + y
                for j in range(ff // LANES):
                    for m, ref in enumerate((f_in, f_outt)):
                        first = at + (y * 4 + z) * plan.ff_rows + (m * (ff // LANES) + j) * k_mid
                        ref[layer, rr * k_mid : (rr + 1) * k_mid, j * LANES : (j + 1) * LANES] = pool[
                            first : first + k_mid
                        ]

    def emit_ffn(layer, g_fin, g_foutt):
        if not fast:
            refs.g_fin[layer] = g_fin.astype(BF16)
            refs.g_foutt[layer] = g_foutt.astype(BF16)
            return
        at, k_mid = plan.source[FF[layer]], plan.k_mid
        for m, value in enumerate((g_fin.astype(BF16), g_foutt.astype(BF16))):
            for y in range(2):
                for z in range(4):
                    rr = 2 * z + y
                    for j in range(ff // LANES):
                        first = at + (y * 4 + z) * plan.ff_rows + (m * (ff // LANES) + j) * k_mid
                        pool[first : first + k_mid] = value[
                            rr * k_mid : (rr + 1) * k_mid, j * LANES : (j + 1) * LANES
                        ]

    def emit_message(layer, g_own_rows, g_other_rows, g_edge_rows, g_mid, g_out):
        if not fast:
            refs.g_in[layer, :width] = g_own_rows.astype(BF16)
            refs.g_in[layer, width : 2 * width] = g_other_rows.astype(BF16)
            refs.g_in[layer, 2 * width :] = g_edge_rows.astype(BF16)
            refs.g_mid[layer] = g_mid.astype(BF16)
            refs.g_out[layer] = g_out.astype(BF16)
            return
        wide[:width, :width] = g_own_rows
        wide[width : 2 * width, :width] = g_other_rows
        wide[2 * width : 2 * width + ew, :width] = g_edge_rows
        at = plan.source[IN[layer]]
        for k, rr, nn_ in blocks():
            first = at + k * plan.in_rows
            pool[first : first + plan.k_in] = wide[
                rr * plan.k_in : (rr + 1) * plan.k_in, nn_ * LANES : (nn_ + 1) * LANES
            ].astype(BF16)
        at, k_mid = plan.source[MO[layer]], plan.k_mid
        for m, value in enumerate((g_mid.astype(BF16), g_out.astype(BF16))):
            for k, rr, nn_ in blocks():
                first = at + k * plan.mo_rows + m * k_mid
                pool[first : first + k_mid] = value[
                    rr * k_mid : (rr + 1) * k_mid, nn_ * LANES : (nn_ + 1) * LANES
                ]

    def emit_edge_all():
        at, cols = plan.source[ED], ew // 4
        long = up_to(w_in.shape[1], LANES)
        fill = LANES - 2 * cols
        for nn_ in range(4):
            span = slice(nn_ * cols, (nn_ + 1) * cols)
            tall = jnp.concatenate(
                [refs.g_eint[0, span].astype(F32), refs.g_eint[1, span].astype(F32), jnp.zeros((fill, long), F32)],
                axis=0,
            ).T
            wide[:long, nn_ * LANES : (nn_ + 1) * LANES] = tall
        for k, rr, nn_ in blocks():
            first = at + k * plan.ed_rows
            pool[first : first + plan.k_in] = wide[
                rr * plan.k_in : (rr + 1) * plan.k_in, nn_ * LANES : (nn_ + 1) * LANES
            ].astype(BF16)
        for layer in range(2):
            for nn_ in range(4):
                span = slice(nn_ * cols, (nn_ + 1) * cols)
                tall = jnp.concatenate(
                    [refs.g_ehid[layer, m, span].astype(F32) for m in range(2)]
                    + [jnp.zeros((fill, 2 * LANES), F32)],
                    axis=0,
                ).T
                wide[: 2 * LANES, nn_ * LANES : (nn_ + 1) * LANES] = tall
            for k, rr, nn_ in blocks():
                first = at + k * plan.ed_rows + plan.in_pad + layer * plan.hid_pad
                pool[first : first + plan.k_hid] = wide[
                    rr * plan.k_hid : (rr + 1) * plan.k_hid, nn_ * LANES : (nn_ + 1) * LANES
                ].astype(BF16)

    def act_at(kind, layer, slot):
        return pl.ds(aligned(plan.acts[layer] + kind * plan.act_rows + slot * width), width)

    U1, S1, S2 = 0, 1, 2
    W1, T1, W2, T2 = 0, 1, 2, 3

    def edge_act(kind, layer, base, j):
        slot = base + j if layer == 0 else slots + j
        return pl.ds(aligned(plan.edge_at + kind * plan.edge_rows + slot * ew), ew)

    def acts(kind, layer, base):
        return jnp.concatenate([pool[act_at(kind, layer, base + j)] for j in range(CHUNK)], axis=1)

    def edge_acts(kind, layer, base):
        return jnp.concatenate([pool[edge_act(kind, layer, base, j)] for j in range(CHUNK)], axis=1)

    def lanes_of(ref, base, *lead):
        return jnp.concatenate([ref[(*lead, base + j)] for j in range(CHUNK)], axis=1)

    def make_vectors():
        refs.g_vec[...] = jnp.zeros_like(refs.g_vec)
        mask_ref[...] = refs.mask[...].astype(F32)
        for layer in range(plan.layers):
            at = layer * VECTORS
            for k in range(6):
                wide[at + k : at + k + 1, :width] = refs.node_biases[k, layer : layer + 1]
            wide[at + GN1 : at + GN2 + 1, :width] = refs.node_gains[layer]
            first = pl.multiple_of(n * ff, ff)
            wide[at + FB : at + FB + 1, :ff] = refs.ffn_bias[layer : layer + 1, pl.ds(first, ff)]
            wide[at + C1 : at + C4 + 1, :ew] = refs.edge_biases[layer]
            wide[at + GE : at + GE + 1, :ew] = refs.edge_gains[layer : layer + 1]
        vec_ref[...] = wide[:LANES, :width].T

    def make_onehot():
        cells = lax.broadcasted_iota(jnp.int32, (3 * LANES, LANES), 0) + (r - 1) * LANES

        def step(s, _):
            onehot[s] = jnp.where(cells == refs.neighbors[pl.ds(s, 1), :], 1.0, 0.0).astype(BF16)
            eb[0, s] = g_edges[s].astype(BF16)
            return 0

        load_edges.wait()
        lax.fori_loop(0, slots, step, 0)

    def prepare_message(layer):
        proj[:, : 3 * LANES] = tn(w_in[layer, width : 2 * width, :], extended(layer)).astype(BF16)
        proj[:, 3 * LANES :] = w_et[layer]
        own[...] = tn(w_in[layer, :width, :], ext[layer, 1]) + vec(layer, B1)
        ubar[layer] = jnp.zeros((width, LANES), F32)

    def prepare_edge(layer):
        proj_e[:, : 3 * LANES] = nn(e_int[layer, :, width : 2 * width], extended(layer + 1)).astype(BF16)
        proj_e[:, 3 * LANES :] = e_int[layer, :, 2 * width :]
        own_e[...] = nn(e_int[layer, :, :width], ext[layer + 1, 1]) + vec(layer, C1, ew)

    def message_forward(layer, base):
        rows = jnp.concatenate([lanes_of(onehot, base), lanes_of(eb, base, layer)], axis=0)
        wide[:width, :] = nn(proj[...], rows)
        for j in range(CHUNK):
            z = wide[:width, j * LANES : (j + 1) * LANES] + own[...]
            pool[act_at(U1, layer, base + j)], pool[act_at(S1, layer, base + j)] = gelu_pair(z)
        wide[:width, :] = nn(w_midt[layer], acts(U1, layer, base))
        for j in range(CHUNK):
            z = wide[:width, j * LANES : (j + 1) * LANES] + vec(layer, B2)
            u2, pool[act_at(S2, layer, base + j)] = gelu_pair(z)
            ubar[layer] += u2.astype(F32) * mask_ref[pl.ds(base + j, 1), :]

    def edge_forward(layer, base, edge_ref, save):
        rows = jnp.concatenate([lanes_of(onehot, base), lanes_of(eb, base, layer)], axis=0)
        z = nn(proj_e[...], rows)
        for j in range(CHUNK):
            zj = z[:, j * LANES : (j + 1) * LANES] + own_e[...]
            pool[edge_act(W1, layer, base, j)], pool[edge_act(T1, layer, base, j)] = gelu_pair(zj)
        z = nn(e_hidt[layer, 0], edge_acts(W1, layer, base))
        for j in range(CHUNK):
            zj = z[:, j * LANES : (j + 1) * LANES] + vec(layer, C2, ew)
            pool[edge_act(W2, layer, base, j)], pool[edge_act(T2, layer, base, j)] = gelu_pair(zj)
        z = nn(e_hidt[layer, 1], edge_acts(W2, layer, base))
        for j in range(CHUNK):
            p = edge_ref[base + j] + z[:, j * LANES : (j + 1) * LANES] + vec(layer, C3, ew)
            hat, rstd = norm_parts(p)
            save(j, hat, rstd, p, hat * vec(layer, GE, ew) + vec(layer, C4, ew))

    def node_update(layer, before_ffn=lambda: None):
        total = all_reduce(ubar[layer])[...]
        high = total.astype(BF16)
        low = (total - high.astype(F32)).astype(BF16)
        counts = cnt_ref[...]
        sums = tn(w_out[layer], high) + tn(w_out[layer], low) + counts * vec(layer, B3)
        merged = state[layer] + sums * (1.0 / counts)
        joined_a[layer] = merged
        hat, _ = norm_parts(merged)
        hidden = hat * vec(layer, GN1) + vec(layer, SH1)
        h1b[layer] = hidden.astype(BF16)
        before_ffn()
        pre = tn(f_in[layer], h1b[layer]) + vec(layer, FB)
        act[layer], slope_f[layer] = gelu_pair(pre)
        branch = all_reduce(nn(f_outt[layer], act[layer]))[...]
        joined = hidden + (branch + vec(layer, B5))
        joined_c[layer] = joined
        hat, _ = norm_parts(joined)
        state[layer + 1] = hat * vec(layer, GN2) + vec(layer, SH2)
        return halo(layer + 1, state[layer + 1].astype(BF16))

    def clear_edge():
        for ref in (acc_h2, acc_h3, acc_ee, acc_t, acc_ts, acc_c):
            ref[...] = jnp.zeros_like(ref)

    def clear_message():
        for ref in (acc_mid, acc_e, acc_z, acc_zs, acc_b2):
            ref[...] = jnp.zeros_like(ref)

    def edge_backward(layer, base, parts):
        lows = []
        for j in range(CHUNK):
            hat, rstd, grad = parts(j)
            acc_c[0] += grad * hat
            acc_c[1] += grad
            dp = norm_back(hat, rstd, vec(layer, GE, ew), grad)
            g_edges[base + j] = dp
            low = dp.astype(BF16)
            acc_c[2] += low.astype(F32)
            lows.append(low)
        out = jnp.concatenate(lows, axis=1)
        acc_h3[...] += nt(out, edge_acts(W2, layer, base))
        grad_two = (nn(e_hid[layer, 1], out) * edge_acts(T2, layer, base).astype(F32)).astype(BF16)
        for j in range(CHUNK):
            acc_c[3] += grad_two[:, j * LANES : (j + 1) * LANES].astype(F32)
        acc_h2[...] += nt(grad_two, edge_acts(W1, layer, base))
        grad_one = (nn(e_hid[layer, 0], grad_two) * edge_acts(T1, layer, base).astype(F32)).astype(BF16)
        for j in range(CHUNK):
            acc_ts[...] += grad_one[:, j * LANES : (j + 1) * LANES].astype(F32)
        acc_t[...] += nt(grad_one, lanes_of(onehot, base))
        acc_ee[...] += nt(grad_one, lanes_of(eb, base, layer))
        back = nn(e_e[layer], grad_one)
        for j in range(CHUNK):
            g_edges[base + j] += back[:, j * LANES : (j + 1) * LANES]

    def edge_finish(layer):
        put_vec(layer, GE, acc_c[0])
        put_vec(layer, C4, acc_c[1])
        put_vec(layer, C3, acc_c[2])
        put_vec(layer, C2, acc_c[3])
        put_vec(layer, C1, acc_ts[...])
        refs.g_ehid[layer, 0, :, :ew] = acc_h2[...].astype(BF16)
        refs.g_ehid[layer, 1, :, :ew] = acc_h3[...].astype(BF16)
        table = acc_t[...].astype(BF16)
        sums = acc_ts[...].astype(BF16)
        refs.g_eint[layer, :, :width] = nt(sums, ext[layer + 1, 1]).astype(BF16)
        refs.g_eint[layer, :, width : 2 * width] = nt(table, extended(layer + 1)).astype(BF16)
        refs.g_eint[layer, :, 2 * width : 2 * width + ew] = acc_ee[...].astype(BF16)
        g_ext = tn(e_int[layer, :, width : 2 * width], table)
        g_own = tn(e_int[layer, :, :width], sums)
        return g_ext, g_own

    def message_backward(layer, base, add_edge):
        grads = []
        for j in range(CHUNK):
            s = base + j
            slope = pool[act_at(S2, layer, s)].astype(F32)
            dz = (vrow[...] * mask_ref[pl.ds(s, 1), :] * slope).astype(BF16)
            acc_b2[...] += dz.astype(F32)
            grads.append(dz)
        grad_two = jnp.concatenate(grads, axis=1)
        acc_mid[...] += nt(acts(U1, layer, base), grad_two)
        wide[:width, :] = nn(w_mid[layer], grad_two)
        grads = []
        for j in range(CHUNK):
            slope = pool[act_at(S1, layer, base + j)].astype(F32)
            dz = (wide[:width, j * LANES : (j + 1) * LANES] * slope).astype(BF16)
            acc_zs[...] += dz.astype(F32)
            grads.append(dz)
        grad_one = jnp.concatenate(grads, axis=1)
        acc_z[...] += nt(grad_one, lanes_of(onehot, base))
        acc_e[...] += nt(lanes_of(eb, base, layer), grad_one)
        back = nn(w_in[layer, 2 * width :, :], grad_one)
        for j in range(CHUNK):
            add_edge(base + j, back[:, j * LANES : (j + 1) * LANES])

    def message_finish(layer):
        put_vec(layer, B2, acc_b2[...])
        put_vec(layer, B1, acc_zs[...])
        table = acc_z[...].astype(BF16)
        sums = acc_zs[...].astype(BF16)
        emit_message(
            layer,
            nt(ext[layer, 1], sums),
            nt(extended(layer), table),
            acc_e[...],
            acc_mid[...],
            nt(ubar[layer].astype(BF16), ds_ref[...]),
        )
        g_ext = nn(w_in[layer, width : 2 * width, :], table)
        g_own = nn(w_in[layer, :width, :], sums)
        return g_ext, g_own

    def node_back(layer, meanwhile=lambda: None):
        counts = cnt_ref[...]
        grad = dcur[...]
        hat, rstd = norm_parts(joined_c[layer])
        put_vec(layer, GN2, grad * hat)
        put_vec(layer, SH2, grad)
        dc = norm_back(hat, rstd, vec(layer, GN2), grad)
        dy = dc.astype(BF16)
        put_vec(layer, B5, dy.astype(F32))
        df = (tn(f_outt[layer], dy) * slope_f[layer].astype(F32)).astype(BF16)
        put_vec(layer, FB, df.astype(F32))
        part = nn(f_in[layer], df)
        meanwhile()
        total = all_reduce(part, short=True)
        emit_ffn(layer, nt(h1b[layer], df), nt(dy, act[layer]))
        grad = dc + total[...]
        hat, rstd = norm_parts(joined_a[layer])
        put_vec(layer, GN1, grad * hat)
        put_vec(layer, SH1, grad)
        da = norm_back(hat, rstd, vec(layer, GN1), grad)
        dcur[...] = da
        ds = (da * (1.0 / counts)).astype(BF16)
        ds_ref[...] = ds
        put_vec(layer, B3, ds.astype(F32) * counts)
        vrow[...] = nn(w_out[layer], ds)

    if fast:
        own_rows = refs.nodes.shape[0]
        mine = pl.multiple_of(n * own_rows, own_rows)
        k_mid = plan.k_mid

        def pack_in(layer):
            pool[pl.ds(my_shard(IN[layer]), plan.k_in)] = refs.msg_in[layer].astype(BF16)

        def pack_mo(layer):
            at = my_shard(MO[layer])
            pool[pl.ds(at, k_mid)] = refs.msg_mid[layer].astype(BF16)
            pool[pl.ds(aligned(at + k_mid), k_mid)] = refs.msg_out[layer].astype(BF16)

        def pack_ffn(layer):
            at = my_shard(FF[layer])
            for m, ref in enumerate((refs.ffn_in, refs.ffn_outt)):
                for j in range(ff // LANES):
                    to = aligned(at + (m * (ff // LANES) + j) * k_mid)
                    pool[pl.ds(to, k_mid)] = ref[layer, :, j * LANES : (j + 1) * LANES].astype(BF16)

        def pack_edge():
            cols = ew // 4
            for layer in range(2):
                wide[layer * cols : (layer + 1) * cols, : plan.k_in] = refs.edge_in_t[layer]
            turned = wide[:LANES, : 2 * LANES].T
            at = my_shard(ED)
            pool[pl.ds(at, plan.k_in)] = turned[: plan.k_in].astype(BF16)
            for layer in range(2):
                for m in range(2):
                    wide[: plan.k_hid, m * cols : (m + 1) * cols] = refs.edge_hidden[layer, m]
                to = aligned(at + plan.in_pad + layer * plan.hid_pad)
                pool[pl.ds(to, plan.k_hid)] = wide[: plan.k_hid, :LANES].astype(BF16)

        pack_in(0)
        pool[pl.ds(my_shard(TB), plan.tb_rows)] = refs.time_table[...].astype(BF16)
        refs.all_nodes[pl.ds(mine, own_rows)] = refs.nodes[...]
        refs.all_dnodes[pl.ds(mine, own_rows)] = refs.d_nodes[...]
        steps = jnp.zeros((1, own_rows), jnp.int32)
        for p in range(refs.time_index.shape[0]):
            steps += jnp.where(refs.protein_ids[...] == p, refs.time_index[p], 0)
        refs.all_misc[n, 0:1, :] = jnp.sum(refs.mask[...].astype(F32), axis=0, keepdims=True)
        refs.all_misc[n, 1:2, :own_rows] = steps.astype(F32)
        pl.semaphore_wait(barrier, greetings)

        node_copies, late_copies = [], []
        for k in (1, 2, 3):
            peer = (r, lax.rem(n + k, 4))
            for ref, group in (
                (refs.all_nodes.at[pl.ds(mine, own_rows)], node_copies),
                (refs.all_misc.at[n], node_copies),
                (refs.all_dnodes.at[pl.ds(mine, own_rows)], late_copies),
            ):
                group.append(remote(ref, ref, peer))
        every = range(FF1 + 1)
        gz = {item: gather_z(item) for item in every}
        gy = {item: gather_y(item) for item in every}
        gx = {item: gather_x(item) for item in FULL}
        gc = {item: gather_c(item) for item in FULL}

        def pass_on(before, after, *items):
            for item in items:
                wait(before[item])
                start(after[item])

        def first(stage, *items):
            for item in items:
                start(stage[item])

        first(gz, IN0, TB)
        start(node_copies)
        pack_mo(0)
        pack_edge()
        make_vectors()
        pass_on(gz, gy, IN0, TB)
        first(gz, MO0, ED)
        pack_ffn(0)
        pack_in(1)
        pack_mo(1)
        pack_ffn(1)
        make_onehot()
        pass_on(gy, gx, IN0, TB)
        pass_on(gz, gy, MO0, ED)
        first(gz, FF0, IN1, MO1)
        wait(node_copies)
        misc = refs.all_misc[0]
        for k in range(1, 4):
            misc += refs.all_misc[k]
        cnt_ref[...] = misc[0:1]
        steps = jnp.concatenate([refs.all_misc[k, 1:2, :own_rows] for k in range(4)], axis=1)
        times = lax.broadcasted_iota(jnp.int32, (8 * plan.k_time, LANES), 0).astype(F32)
        refs.time_hot[...] = jnp.where(times == steps, 1.0, 0.0).astype(BF16)
        nodes_t = refs.all_nodes[...].T
        pass_on(gx, gc, IN0, TB)
        pass_on(gy, gx, MO0)
        wait(gc[TB])
        for k, rr, nn_ in blocks():
            at = plan.stage[TB] + k * plan.tb_rows
            refs.time_rows[rr * plan.k_time : (rr + 1) * plan.k_time, nn_ * LANES : (nn_ + 1) * LANES] = pool[
                at : at + plan.tb_rows
            ]
        state[0] = nodes_t + tn(refs.time_rows[...], refs.time_hot[...])
        finish = halo(0, state[0].astype(BF16))
        wait(gc[IN0])
        assemble_in(0)
        pass_on(gx, gc, MO0)
        pass_on(gy, gx, ED)
        finish()
        wait(gc[MO0])
        assemble_mo(0)
    else:
        make_vectors()
        make_onehot()
        pl.semaphore_wait(barrier, greetings)
        state[0] = refs.h0[...]
        halo(0, state[0].astype(BF16))()

    prepare_message(0)

    def loop_a(i, _):
        message_forward(0, i * CHUNK)
        if fast:

            @pl.when(i == 1)
            def _():
                pass_on(gz, gy, FF0)

            @pl.when(i == 2)
            def _():
                pass_on(gz, gy, IN1, MO1)
                first(gz, FF1)
                start(late_copies)

        return 0

    lax.fori_loop(0, chunks, loop_a, 0)

    def need_ffn0():
        if fast:
            pass_on(gx, gc, ED)
            pass_on(gy, gx, IN1, MO1)
            wait(gy[FF0])
            assemble_ffn(0)

    finish = node_update(0, need_ffn0)
    if fast:
        pass_on(gz, gy, FF1)
        wait(gc[ED])
        assemble_edge()
        pass_on(gx, gc, IN1, MO1)
        wait(gc[IN1])
        assemble_in(1)
        wait(gc[MO1])
        assemble_mo(1)
        wait(gy[FF1])
        assemble_ffn(1)
        wait(late_copies)
    finish()
    prepare_edge(0)
    prepare_message(1)

    def loop_b(i, _):
        base = i * CHUNK

        def save(j, hat, rstd, p, value):
            psum[base + j] = p
            edges_out[base + j] = value
            eb[1, base + j] = value.astype(BF16)

        edge_forward(0, base, g_edges, save)
        message_forward(1, base)
        return 0

    lax.fori_loop(0, chunks, loop_b, 0)
    load_grads = pltpu.make_async_copy(refs.d_edges, g_edges, refs.local_sem.at[1])
    load_grads.start()
    finish = node_update(1)
    if fast:
        refs.all_nodes[...] = state[2].T
        nodes_out[...] = refs.all_nodes[pl.ds(mine, own_rows)]
    else:
        nodes_out[...] = state[2].T
    clear_edge()
    load_grads.wait()
    finish()
    prepare_edge(1)

    def loop_c(i, _):
        base = i * CHUNK
        kept = {}

        def save(j, hat, rstd, p, value):
            edges_out[base + j] = value
            kept[j] = (hat, rstd)

        edge_forward(1, base, edges_out, save)
        edge_backward(1, base, lambda j: (*kept[j], g_edges[base + j]))
        return 0

    lax.fori_loop(0, chunks, loop_c, 0)
    g_ext, g_own = edge_finish(1)
    dh = refs.all_dnodes[...].T if fast else refs.dh[...]
    dcur[...] = dh + halo_back(0, g_ext, g_own)[...]
    node_back(1)
    clear_message()
    clear_edge()
    reduce_c, reduce_x, reduce_y, reduce_last = {}, {}, {}, {}
    if fast:
        for item in range(FF1 + 1):
            if item in FULL:
                reduce_c[item] = reduce_pairs(item, BY_CORE)
                reduce_x[item] = reduce_pairs(item, BY_X)
            reduce_y[item] = reduce_pairs(item, BY_Y)
            reduce_last[item] = reduce_z(item)

    def reduce_on(before, after, *items):
        for item in items:
            wait(before[item][0])
            before[item][1]()
            start(after[item][0])

    def put_ffn(layer):
        copies, total = reduce_last[FF[layer]]
        wait(copies)
        k_mid, parts = plan.k_mid, ff // LANES
        for m, ref in enumerate((refs.o_fin, refs.o_foutt)):
            for j in range(parts):
                ref[layer, :, j * LANES : (j + 1) * LANES] = total((m * parts + j) * k_mid, k_mid)

    def put_message(layer):
        copies, total = reduce_last[IN[layer]]
        wait(copies)
        refs.o_in[layer] = total(0, plan.k_in)
        copies, total = reduce_last[MO[layer]]
        wait(copies)
        refs.o_mid[layer] = total(0, plan.k_mid)
        refs.o_out[layer] = total(plan.k_mid, plan.k_mid)

    def put_edge():
        copies, total = reduce_last[ED]
        wait(copies)
        cols = ew // 4
        wide[: plan.in_pad, :LANES] = total(0, plan.in_pad)
        turned = wide[: 2 * LANES, :LANES].T
        hidden = total(plan.in_pad, 2 * plan.hid_pad)
        for layer in range(2):
            refs.o_edge[layer] = turned[layer * cols : (layer + 1) * cols, : plan.k_in]
            first = layer * plan.hid_pad
            for m in range(2):
                refs.o_hid[layer, m] = hidden[first : first + plan.k_hid, m * cols : (m + 1) * cols]

    if fast:
        start(reduce_y[FF1][0])

    def loop_d1(i, _):
        base = i * CHUNK

        def add_edge(s, value):
            g_edges[s] += value

        message_backward(1, base, add_edge)
        return 0

    lax.fori_loop(0, chunks, loop_d1, 0)
    m_ext, m_own = message_finish(1)
    acc_z[...] = m_ext
    acc_zs[...] = m_own
    if fast:
        start(reduce_c[IN1][0])
        start(reduce_c[MO1][0])
        reduce_on(reduce_y, reduce_last, FF1)

    def loop_d2(i, _):
        base = i * CHUNK
        edge_backward(0, base, lambda j: (*norm_parts(psum[base + j]), g_edges[base + j]))
        if fast:

            @pl.when(i == 0)
            def _():
                reduce_on(reduce_c, reduce_x, IN1, MO1)

        return 0

    lax.fori_loop(0, chunks, loop_d2, 0)
    e_ext, e_own = edge_finish(0)
    if fast:
        emit_edge_all()
        start(reduce_c[ED][0])
    dcur[...] += halo_back(1, acc_z[...] + e_ext, acc_zs[...] + e_own)[...]
    if fast:
        put_ffn(1)
        reduce_on(reduce_x, reduce_y, IN1, MO1)
    node_back(0)
    clear_message()
    if fast:
        reduce_on(reduce_c, reduce_x, ED)
        start(reduce_y[FF0][0])

    def loop_e(i, _):
        base = i * CHUNK

        def add_edge(s, value):
            g_edges[s] += value

        message_backward(0, base, add_edge)
        if fast:

            @pl.when(i == 2)
            def _():
                reduce_on(reduce_y, reduce_last, IN1, MO1)

        return 0

    lax.fori_loop(0, chunks, loop_e, 0)
    m_ext, m_own = message_finish(0)
    if fast:
        start(reduce_c[IN0][0])
        start(reduce_c[MO0][0])
        reduce_on(reduce_x, reduce_y, ED)
        reduce_on(reduce_c, reduce_x, IN0)
        reduce_on(reduce_y, reduce_last, FF0)
    final = dcur[...] + halo_back(2, m_ext, m_own)[...]
    if not fast:
        g_nodes[...] = final.T
        return
    refs.all_dnodes[...] = final.T
    g_nodes[...] = refs.all_dnodes[pl.ds(mine, own_rows)]

    high = final.astype(BF16)
    low = (final - high.astype(F32)).astype(BF16)
    g_times = (nt(refs.time_hot[...], high) + nt(refs.time_hot[...], low)) * (1.0 / plan.nbr_total)
    for k, rr, nn_ in blocks():
        at = plan.source[TB] + k * plan.tb_rows
        pool[at : at + plan.tb_rows] = g_times[
            rr * plan.k_time : (rr + 1) * plan.k_time, nn_ * LANES : (nn_ + 1) * LANES
        ].astype(BF16)
    start(reduce_c[TB][0])
    table = refs.g_vec[...].T
    sums = refs.vec_sums
    sums[0] = jnp.zeros_like(sums[0])
    for layer in range(2):
        for which, row in VEC_ROWS.items():
            value = table[layer * VECTORS + which : layer * VECTORS + which + 1]
            at = layer * VEC_PER_LAYER + row
            if which == FB:
                sums[0, pl.ds(at + n, 1)] = value
            else:
                scale = 1.0 / plan.nbr_total if B3 <= which <= GN2 else 1.0
                sums[0, at : at + 1] = value * scale
    partners = [(r, buddy), (r, across), y_peer]
    partners += [(2 * (zz + 1 - 2 * lax.rem(zz, 2)) + yy, n), (2 * lax.rem(zz + 2, 4) + yy, n)]
    rounds = [remote(sums.at[2 * k], sums.at[2 * k + 1], partners[k]) for k in range(5)]

    def vec_round(k):
        rounds[k].wait()
        sums[2 * k + 2] = sums[2 * k] + sums[2 * k + 1]
        if k < 4:
            rounds[k + 1].start()

    rounds[0].start()
    reduce_on(reduce_x, reduce_y, IN0)
    reduce_on(reduce_c, reduce_x, MO0, TB)
    vec_round(0)
    reduce_on(reduce_y, reduce_last, ED)
    put_message(1)
    vec_round(1)
    reduce_on(reduce_y, reduce_last, IN0)
    reduce_on(reduce_x, reduce_y, TB, MO0)
    vec_round(2)
    reduce_on(reduce_y, reduce_last, TB, MO0)
    vec_round(3)
    put_ffn(0)
    put_edge()
    vec_round(4)
    for layer in range(2):
        at = layer * VEC_PER_LAYER
        for k in range(6):
            refs.o_node_biases[k, layer : layer + 1] = sums[10, at + k : at + k + 1]
        refs.o_node_gains[layer] = sums[10, at + VEC_ROWS[GN1] : at + VEC_ROWS[GN2] + 1]
        for k in range(4):
            first = at + VEC_ROWS[FB] + k
            refs.o_ffn_bias[layer : layer + 1, k * ff : (k + 1) * ff] = sums[10, first : first + 1, :ff]
        first = at + VEC_ROWS[C1]
        refs.o_edge_biases[layer] = sums[10, first : first + 4, :ew]
        refs.o_edge_gains[layer : layer + 1] = sums[10, first + 4 : first + 5, :ew]
    put_message(0)
    copies, total = reduce_last[TB]
    wait(copies)
    refs.o_time[...] = total(0, plan.tb_rows)


def vmem(shape, dtype):
    return pltpu.VMEM(shape, dtype)


def run_whole(plan, operands):
    lanes, slots, width, ew, ff, layers = LANES, plan.slots, plan.width, plan.ew, plan.ff, plan.layers
    rows_in = 2 * width + ew
    node_rows = lanes // plan.nbr_total if plan.fast else lanes
    outs = dict(
        nodes_out=((node_rows, width), F32),
        edges_out=((slots, ew, lanes), F32),
        g_nodes=((node_rows, width), F32),
        g_edges=((slots, ew, lanes), F32),
    )
    scratch = dict(
        onehot=vmem((slots, 3 * lanes, lanes), BF16),
        eb=vmem((layers, slots, ew, lanes), BF16),
        pool=vmem((plan.pool_rows, lanes), BF16),
        psum=vmem((slots, ew, lanes), F32),
        proj=vmem((width, 3 * lanes + ew), BF16),
        proj_e=vmem((ew, 3 * lanes + ew), BF16),
        own=vmem((width, lanes), F32),
        own_e=vmem((ew, lanes), F32),
        state=vmem((3, width, lanes), F32),
        ext=vmem((3, 3, width, lanes), BF16),
        joined_a=vmem((layers, width, lanes), F32),
        joined_c=vmem((layers, width, lanes), F32),
        h1b=vmem((layers, width, lanes), BF16),
        act=vmem((layers, ff, lanes), BF16),
        slope_f=vmem((layers, ff, lanes), BF16),
        ubar=vmem((layers, width, lanes), F32),
        ds=vmem((width, lanes), BF16),
        acc_mid=vmem((width, width), F32),
        acc_e=vmem((ew, width), F32),
        acc_z=vmem((width, 3 * lanes), F32),
        acc_zs=vmem((width, lanes), F32),
        acc_b2=vmem((width, lanes), F32),
        acc_h2=vmem((ew, ew), F32),
        acc_h3=vmem((ew, ew), F32),
        acc_ee=vmem((ew, ew), F32),
        acc_t=vmem((ew, 3 * lanes), F32),
        acc_ts=vmem((ew, lanes), F32),
        acc_c=vmem((4, ew, lanes), F32),
        wide=vmem((up_to(rows_in, lanes), CHUNK * lanes), F32),
        vrow=vmem((width, lanes), F32),
        dcur=vmem((width, lanes), F32),
        g_part=vmem((width, lanes), F32),
        halo_send=vmem((2, width, lanes), BF16),
        halo_recv=vmem((3, 2, width, lanes), BF16),
        ar_part=vmem((2, width, lanes), F32),
        ar_one=vmem((2, width // 2, lanes), F32),
        ar_two=vmem((2, width // 2, lanes), F32),
        ar_three=vmem((2, width // 2, lanes), F32),
        ar_two_low=vmem((2, width // 2, lanes), BF16),
        ar_three_low=vmem((2, width // 2, lanes), BF16),
        mask_rows=vmem((slots, lanes), F32),
        vectors=vmem((width, lanes), F32),
        ar_tot=vmem((2, width, lanes), F32),
        send_sem=pltpu.SemaphoreType.DMA((160,)),
        recv_sem=pltpu.SemaphoreType.DMA((160,)),
        local_sem=pltpu.SemaphoreType.DMA((2,)),
    )
    kept = dict(
        g_eint=((layers, ew, up_to(rows_in, lanes)), BF16),
        g_ehid=((layers, 2, ew, 2 * lanes), BF16),
        g_vec=((width, lanes), F32),
    )
    if plan.fast:
        scratch.update({name: vmem(*spec) for name, spec in kept.items()})
        own_rows = lanes // plan.nbr_total
        scratch.update(
            dict(
                counts=vmem((1, lanes), F32),
                all_nodes=vmem((lanes, width), F32),
                all_dnodes=vmem((lanes, width), F32),
                all_misc=vmem((plan.nbr_total, 8, lanes), F32),
                time_hot=vmem((8 * plan.k_time, lanes), BF16),
                time_rows=vmem((8 * plan.k_time, width), BF16),
                vec_sums=vmem((11, layers * VEC_PER_LAYER, width), F32),
                w_in=vmem((layers, rows_in, width), BF16),
                w_et=vmem((layers, width, ew), BF16),
                w_mid=vmem((layers, width, width), BF16),
                w_midt=vmem((layers, width, width), BF16),
                w_out=vmem((layers, width, width), BF16),
                f_in=vmem((layers, width, ff), BF16),
                f_outt=vmem((layers, width, ff), BF16),
                e_int=vmem((layers, ew, rows_in), BF16),
                e_e=vmem((layers, ew, ew), BF16),
                e_hid=vmem((layers, 2, ew, ew), BF16),
                e_hidt=vmem((layers, 2, ew, ew), BF16),
            )
        )
        outs.update(
            dict(
                o_in=((layers, plan.k_in, lanes), F32),
                o_mid=((layers, plan.k_mid, lanes), F32),
                o_out=((layers, plan.k_mid, lanes), F32),
                o_fin=((layers, plan.k_mid, ff), F32),
                o_foutt=((layers, plan.k_mid, ff), F32),
                o_edge=((layers, ew // 4, plan.k_in), F32),
                o_hid=((layers, 2, plan.k_hid, ew // 4), F32),
                o_time=((plan.tb_rows, lanes), F32),
                o_node_biases=((6, layers, width), F32),
                o_node_gains=((layers, 2, width), F32),
                o_ffn_bias=((layers, 4 * ff), F32),
                o_edge_gains=((layers, ew), F32),
                o_edge_biases=((layers, 4, ew), F32),
            )
        )
    else:
        outs.update(
            dict(
                g_in=((layers, rows_in, width), BF16),
                g_mid=((layers, width, width), BF16),
                g_out=((layers, width, width), BF16),
                g_fin=((layers, width, ff), BF16),
                g_foutt=((layers, width, ff), BF16),
                **kept,
            )
        )
    names = (*operands, *outs, *scratch)
    in_hbm, in_smem = dict(edges=1, d_edges=1), dict(time_index=1)
    place = lambda name: pl.BlockSpec(
        memory_space=pl.ANY if name in in_hbm else pltpu.SMEM if name in in_smem else pltpu.VMEM
    )
    results = pl.pallas_call(
        functools.partial(whole_kernel, plan, names),
        out_shape=tuple(jax.ShapeDtypeStruct(*spec) for spec in outs.values()),
        in_specs=[place(name) for name in operands],
        out_specs=[pl.BlockSpec(memory_space=pltpu.VMEM)] * len(outs),
        scratch_shapes=list(scratch.values()),
        compiler_params=pltpu.CompilerParams(
            collective_id=1, has_side_effects=True, vmem_limit_bytes=62 * 1024 * 1024
        ),
    )(*operands.values())
    return Refs(outs, results)


def hand_over(values):
    def kernel(*refs):
        for source, result in zip(refs[: len(values)], refs[len(values) :], strict=True):
            result[...] = source[...]

    return pl.pallas_call(
        kernel,
        out_shape=[jax.ShapeDtypeStruct(value.shape, value.dtype) for value in values],
        in_specs=[pl.BlockSpec(memory_space=pltpu.VMEM)] * len(values),
        out_specs=[pl.BlockSpec(memory_space=pltpu.VMEM)] * len(values),
    )(*values)


def gather_all(value, res_dim, nbr_dim):
    value = lax.all_gather(value, "res", axis=res_dim, tiled=True)
    return lax.all_gather(value, "nbr", axis=nbr_dim, tiled=True)


def scatter_sum(value, res_dim, nbr_dim):
    value = lax.psum_scatter(value, "res", scatter_dimension=res_dim, tiled=True)
    return lax.psum_scatter(value, "nbr", scatter_dimension=nbr_dim, tiled=True).astype(F32)


def low(value):
    return value.astype(BF16)


def per_device(
    nodes,
    edges,
    protein_ids,
    time_index,
    neighbors,
    edge_mask,
    time_table,
    msg_in,
    msg_mid,
    msg_out,
    ffn_in,
    ffn_out,
    edge_in,
    edge_hidden,
    node_gains,
    node_biases,
    ffn_bias,
    edge_gains,
    edge_biases,
    d_nodes,
    d_edges,
):
    res_total, nbr_total = lax.axis_size("res"), lax.axis_size("nbr")
    own_rows, width = nodes.shape
    ew = edges.shape[2]
    row_count, slot_count = neighbors.shape
    layers = msg_in.shape[0]
    n_at = lax.axis_index("nbr")
    ff = ffn_bias.shape[1] // nbr_total
    shards = (msg_in.shape[1], msg_mid.shape[1], edge_hidden.shape[2], time_table.shape[0])
    plan = Plan(res_total, nbr_total, slot_count, width, ew, ff, layers, shards)

    operands = dict(
        neighbors=neighbors.T,
        mask=edge_mask.T,
        edges=jnp.transpose(edges, (1, 2, 0)),
        d_edges=jnp.transpose(d_edges, (1, 2, 0)),
        node_biases=jnp.swapaxes(node_biases, 0, 1),
        node_gains=node_gains,
        ffn_bias=ffn_bias,
        edge_gains=edge_gains,
        edge_biases=edge_biases,
    )
    if plan.fast:
        operands.update(
            nodes=nodes,
            d_nodes=d_nodes,
            protein_ids=protein_ids[None, :],
            time_index=time_index,
            msg_in=msg_in,
            msg_mid=msg_mid,
            msg_out=msg_out,
            ffn_in=ffn_in,
            ffn_outt=jnp.swapaxes(ffn_out, 1, 2),
            edge_in_t=jnp.swapaxes(edge_in, 1, 2),
            edge_hidden=edge_hidden,
            time_table=time_table,
        )
        out = run_whole(plan, operands)
        (
            nodes_out, edges_out, g_nodes, g_edges, g_time, g_in, g_mid, g_out, g_fin, g_foutt, g_edge_t,
            g_hid, g_gains, g_biases, g_ffn_bias, g_edge_gains, g_edge_biases,
        ) = hand_over(
            [
                out.nodes_out, out.edges_out, out.g_nodes, out.g_edges, out.o_time, out.o_in, out.o_mid,
                out.o_out, out.o_fin, out.o_foutt, out.o_edge, out.o_hid, out.o_node_gains,
                out.o_node_biases, out.o_ffn_bias, out.o_edge_gains, out.o_edge_biases,
            ]
        )
        return (
            nodes_out,
            jnp.transpose(edges_out, (2, 0, 1)),
            g_nodes,
            jnp.transpose(g_edges, (2, 0, 1)),
            g_time,
            g_in,
            g_mid,
            g_out,
            g_fin,
            jnp.swapaxes(g_foutt, 1, 2),
            jnp.swapaxes(g_edge_t, 1, 2),
            g_hid,
            g_gains,
            jnp.swapaxes(g_biases, 0, 1),
            g_ffn_bias,
            g_edge_gains,
            g_edge_biases,
        )

    count_row = jnp.sum(edge_mask.astype(F32), axis=1)
    matches = protein_ids[:, None] == jnp.arange(time_index.shape[0], dtype=jnp.int32)[None, :]
    step_rows = jnp.sum(jnp.where(matches, time_index[None, :], 0), axis=1)
    mine = lambda a: lax.dynamic_slice_in_dim(a, n_at * own_rows, own_rows, axis=0)
    node_vectors = lambda rows: (rows[:, : SH2 + 1], rows[:, GN1 : GN2 + 1])
    table_low = gather_all(low(time_table), 0, 1)
    w_in = gather_all(low(msg_in), 1, 2)
    w_mid = gather_all(low(msg_mid), 1, 2)
    e_in = gather_all(low(edge_in), 1, 2)
    e_hid = gather_all(low(edge_hidden), 2, 3)
    step_onehot = (
        step_rows[:, None] == jnp.arange(table_low.shape[0], dtype=jnp.int32)[None, :]
    ).astype(BF16)
    state = nodes + jnp.dot(step_onehot, table_low, preferred_element_type=F32)
    count_block = jnp.zeros((8, width), F32).at[0, :row_count].set(count_row)
    packed = lax.all_gather(jnp.concatenate([state, d_nodes, count_block], axis=0), "nbr", axis=0)
    operands.update(
        dict(
            h0=packed[:, :own_rows].reshape(row_count, width).T,
            dh=packed[:, own_rows : 2 * own_rows].reshape(row_count, width).T,
            counts=jnp.sum(packed[:, 2 * own_rows, :row_count], axis=0)[None, :],
            w_in=w_in,
            w_et=jnp.swapaxes(w_in[:, 2 * width :], 1, 2),
            w_mid=w_mid,
            w_midt=jnp.swapaxes(w_mid, 1, 2),
            w_out=gather_all(low(msg_out), 1, 2),
            f_in=lax.all_gather(low(ffn_in), "res", axis=1, tiled=True),
            f_outt=lax.all_gather(jnp.swapaxes(low(ffn_out), 1, 2), "res", axis=1, tiled=True),
            e_int=jnp.swapaxes(e_in, 1, 2),
            e_e=e_in[:, 2 * width :],
            e_hid=e_hid,
            e_hidt=jnp.swapaxes(e_hid, 2, 3),
        )
    )
    out = run_whole(plan, operands)
    g_nodes = mine(out.g_nodes)
    g_table_full = lax.dot_general(
        step_onehot.astype(F32),
        g_nodes,
        (((0,), (0,)), ((), ())),
        precision=lax.Precision.HIGHEST,
        preferred_element_type=F32,
    )
    rows = out.g_vec.T[: layers * VECTORS].reshape(layers, VECTORS, width)
    shared = rows[:, B3 : GN2 + 1] * (1.0 / nbr_total)
    g_bias_ffn = lax.dynamic_update_slice_in_dim(
        jnp.zeros_like(ffn_bias), rows[:, FB, :ff], n_at * ff, axis=1
    )
    vectors, g_ffn_bias, g_edge_biases, g_edge_gains = lax.psum(
        (
            jnp.concatenate([rows[:, :B3], shared], axis=1),
            g_bias_ffn,
            rows[:, C1 : C4 + 1, :ew],
            rows[:, GE, :ew],
        ),
        ("res", "nbr"),
    )
    g_node_biases, g_node_gains = node_vectors(vectors)
    scatter_res = lambda a: lax.psum_scatter(a, "res", scatter_dimension=1, tiled=True).astype(F32)
    return (
        mine(out.nodes_out),
        jnp.transpose(out.edges_out, (2, 0, 1)),
        g_nodes,
        jnp.transpose(out.g_edges, (2, 0, 1)),
        scatter_sum(low(g_table_full), 0, 1),
        scatter_sum(out.g_in, 1, 2),
        scatter_sum(out.g_mid, 1, 2),
        scatter_sum(out.g_out, 1, 2),
        scatter_res(out.g_fin),
        jnp.swapaxes(scatter_res(out.g_foutt), 1, 2),
        jnp.swapaxes(scatter_sum(out.g_eint[:, :, : 2 * width + ew], 2, 1), 1, 2),
        scatter_sum(jnp.swapaxes(out.g_ehid[..., :ew], 2, 3), 2, 3),
        g_node_gains,
        g_node_biases,
        g_ffn_bias,
        g_edge_gains,
        g_edge_biases,
    )


def solution(mesh):
    return jax.shard_map(
        per_device,
        mesh=mesh,
        in_specs=(
            P(("res", "nbr"), None),
            P("res", "nbr", None),
            P(("res", "nbr")),
            P(),
            P("res", "nbr"),
            P("res", "nbr"),
            P("res", "nbr"),
            P(None, "res", "nbr"),
            P(None, "res", "nbr"),
            P(None, "res", "nbr"),
            P(None, "res", "nbr"),
            P(None, "nbr", "res"),
            P(None, "res", "nbr"),
            P(None, None, "res", "nbr"),
            P(),
            P(),
            P(),
            P(),
            P(),
            P(("res", "nbr"), None),
            P("res", "nbr", None),
        ),
        out_specs=(
            P(("res", "nbr"), None),
            P("res", "nbr", None),
            P(("res", "nbr"), None),
            P("res", "nbr", None),
            P("res", "nbr"),
            P(None, "res", "nbr"),
            P(None, "res", "nbr"),
            P(None, "res", "nbr"),
            P(None, "res", "nbr"),
            P(None, "nbr", "res"),
            P(None, "res", "nbr"),
            P(None, None, "res", "nbr"),
            P(),
            P(),
            P(),
            P(),
            P(),
        ),
        check_vma=False,
    )
```

```python
import functools

import jax
import jax.numpy as jnp
from jax import lax
from jax.experimental import pallas as pl
from jax.experimental.pallas import tpu as pltpu
from jax.sharding import PartitionSpec as P

NORM_EPS = 1e-05
F32 = jnp.float32
BF16 = jnp.bfloat16
MESH = pl.DeviceIdType.MESH
LANES = 128
CHUNK = 5
TANH_A = 0.7978845608028654
TANH_B = 0.044715
B1, B2, B3, B5, SH1, SH2, GN1, GN2, FB, C1, C2, C3, C4, GE = range(14)
VECTORS = 14
VEC_ROWS = {B1: 0, B2: 1, B3: 2, B5: 3, SH1: 4, SH2: 5, GN1: 6, GN2: 7, FB: 8, C1: 12, C2: 13, C3: 14, C4: 15, GE: 16}
VEC_PER_LAYER = 20
IN0, TB, MO0, FF0, ED, IN1, MO1, FF1 = range(8)
IN, MO, FF = (IN0, IN1), (MO0, MO1), (FF0, FF1)
BY_CORE, BY_X, BY_Y, BY_Z = range(4)


def nn(left, right):
    return jnp.dot(left, right, preferred_element_type=F32)


def nt(left, right):
    return lax.dot_general(left, right, (((1,), (1,)), ((), ())), preferred_element_type=F32)


def tn(left, right):
    return lax.dot_general(left, right, (((0,), (0,)), ((), ())), preferred_element_type=F32)


def gelu_pair(z):
    sq = z * z
    half = 0.5 + 0.5 * jnp.tanh(z * (TANH_A + (TANH_A * TANH_B) * sq))
    value = z * half
    slope = half + (value * (1.0 - half)) * (2.0 * TANH_A + (6.0 * TANH_A * TANH_B) * sq)
    return value.astype(BF16), slope.astype(BF16)


def norm_parts(value):
    scale = 1.0 / value.shape[0]
    centre = jnp.sum(value, axis=0, keepdims=True) * scale
    offset = value - centre
    spread = jnp.sum(offset * offset, axis=0, keepdims=True) * scale
    rstd = lax.rsqrt(spread + NORM_EPS)
    return offset * rstd, rstd


def norm_back(hat, rstd, gain, grad):
    scale = 1.0 / hat.shape[0]
    weighted = grad * gain
    first = jnp.sum(weighted, axis=0, keepdims=True) * scale
    second = jnp.sum(weighted * hat, axis=0, keepdims=True) * scale
    return rstd * (weighted - first - hat * second)


class Refs:
    def __init__(self, names, values):
        self.__dict__.update(zip(names, values, strict=True))


def up_to(value, step):
    return (value + step - 1) // step * step


class Plan:
    def __init__(self, res_total, nbr_total, slots, width, ew, ff, layers, shards):
        self.res_total, self.nbr_total = res_total, nbr_total
        self.slots, self.width, self.ew, self.ff, self.layers = slots, width, ew, ff, layers
        self.k_in, self.k_mid, self.k_hid, self.k_time = shards
        self.fast = (res_total, nbr_total) == (8, 4) and self.k_in % 8 == 0 and self.k_mid % 16 == 0
        acts = slots * width
        self.acts = [0, 3 * acts]
        self.act_rows = acts
        edge_rows = (slots + CHUNK) * ew
        self.pool_rows = 6 * acts + 4 * edge_rows
        self.edge_at = 6 * acts
        self.edge_rows = edge_rows
        if not self.fast:
            return
        self.in_pad = up_to(self.k_in, 16)
        self.hid_pad = up_to(self.k_hid, 16)
        self.in_rows = self.in_pad
        self.mo_rows = 2 * self.k_mid
        self.ed_rows = self.in_pad + 2 * self.hid_pad
        self.tb_rows = self.k_time
        self.ff_rows = 2 * self.k_mid * (ff // LANES)
        one = 3 * acts
        sizes = {IN0: self.in_rows, MO0: self.mo_rows, ED: self.ed_rows, IN1: self.in_rows,
                 MO1: self.mo_rows, TB: self.tb_rows, FF0: self.ff_rows, FF1: self.ff_rows}
        self.sizes = sizes
        self.stage = {}
        at = 0
        for item in (IN0, TB, MO0):
            self.stage[item] = at
            at += 32 * sizes[item]
        at = one
        for item in (IN1, MO1, ED):
            self.stage[item] = at
            at += 32 * sizes[item]
        top = at
        at = 2 * one
        for item in (FF0, FF1):
            self.stage[item] = at
            at += 8 * sizes[item]
        top = max(top, at)
        self.source, self.recv = {}, {}
        at = 0
        for item in (MO0, IN0):
            self.source[item] = at
            at += 32 * sizes[item]
        at = one
        for item in (IN1, MO1, ED):
            self.source[item] = at
            at += 32 * sizes[item]
        for stage, count in ((BY_CORE, 16), (BY_X, 8), (BY_Y, 4)):
            self.recv[ED, stage] = at
            at += count * sizes[ED]
        at = max(at, 2 * one)
        self.source[FF1] = at
        self.recv[FF1, BY_Y] = at + 8 * sizes[FF1]
        at += 12 * sizes[FF1]
        for stage, count in ((BY_CORE, 16), (BY_X, 8), (BY_Y, 4)):
            for item in (IN1, MO1):
                self.recv[item, stage] = at
                at += count * sizes[item]
        self.recv[IN0, BY_CORE], self.recv[MO0, BY_CORE] = self.recv[IN1, BY_CORE], self.recv[MO1, BY_CORE]
        top = max(top, at)
        self.edge_at = top
        self.source[FF0] = top
        self.recv[FF0, BY_Y] = top + 8 * sizes[FF0]
        at = top + 12 * sizes[FF0]
        for stage, count in ((BY_X, 8), (BY_Y, 4)):
            for item in (IN0, MO0):
                self.recv[item, stage] = at
                at += count * sizes[item]
        at = max(at, top + 4 * edge_rows)
        self.source[TB] = at
        at += 32 * sizes[TB]
        for stage, count in ((BY_CORE, 16), (BY_X, 8), (BY_Y, 4)):
            self.recv[TB, stage] = at
            at += count * sizes[TB]
        for item in sizes:
            self.recv[item, BY_Z] = at
            at += 3 * sizes[item]
        self.pool_rows = at


def whole_kernel(plan, names, *values):
    refs = Refs(names, values)
    fast = plan.fast
    mask_ref, vec_ref = refs.mask_rows, refs.vectors
    onehot, eb, pool, psum, proj, proj_e = refs.onehot, refs.eb, refs.pool, refs.psum, refs.proj, refs.proj_e
    own, own_e, state, ext = refs.own, refs.own_e, refs.state, refs.ext
    joined_a, joined_c, h1b, act = refs.joined_a, refs.joined_c, refs.h1b, refs.act
    slope_f, ubar, ds_ref = refs.slope_f, refs.ubar, refs.ds
    acc_mid, acc_e, acc_z, acc_zs, acc_b2 = refs.acc_mid, refs.acc_e, refs.acc_z, refs.acc_zs, refs.acc_b2
    acc_h2, acc_h3, acc_ee = refs.acc_h2, refs.acc_h3, refs.acc_ee
    acc_t, acc_ts, acc_c = refs.acc_t, refs.acc_ts, refs.acc_c
    wide, vrow, dcur, g_part = refs.wide, refs.vrow, refs.dcur, refs.g_part
    halo_send, halo_recv = refs.halo_send, refs.halo_recv
    ar_part, ar_one, ar_two, ar_three = refs.ar_part, refs.ar_one, refs.ar_two, refs.ar_three
    ar_tot = refs.ar_tot
    w_in, w_et, w_mid, w_midt, w_out = refs.w_in, refs.w_et, refs.w_mid, refs.w_midt, refs.w_out
    f_in, f_outt, e_int, e_e = refs.f_in, refs.f_outt, refs.e_int, refs.e_e
    e_hid, e_hidt = refs.e_hid, refs.e_hidt
    nodes_out, edges_out, g_nodes, g_edges = refs.nodes_out, refs.edges_out, refs.g_nodes, refs.g_edges
    cnt_ref = refs.counts
    res_total = plan.res_total
    slots, width, ew, ff = plan.slots, plan.width, plan.ew, plan.ff
    r = lax.axis_index("res")
    n = lax.axis_index("nbr")
    core = lax.rem(n, 2)
    xx = n // 2
    yy = lax.rem(r, 2)
    zz = r // 2
    buddy = n + 1 - 2 * core
    across = lax.rem(n + 2, 4)
    chunks = slots // CHUNK
    half_rows = width // 2
    has_prev = r > 0
    has_next = r < res_total - 1
    sem_at = [0]
    ar_at = [0]

    greeted = [(r, buddy), (r, across)]
    z_peers = []
    if fast:
        greeted.append((r, lax.rem(buddy + 2, 4)))
        y_peer = (r + 1 - 2 * yy, n)
        z_peers = [(2 * lax.rem(zz + k, 4) + yy, n) for k in (1, 2, 3)]
        greeted += [y_peer, *z_peers]
        up_too = jnp.logical_and(yy == 0, has_prev)
        down_too = jnp.logical_and(yy == 1, has_next)
    else:
        up_too, down_too = has_prev, has_next
    barrier = pltpu.get_barrier_semaphore()
    for device in greeted:
        pl.semaphore_signal(barrier, inc=1, device_id=device, device_id_type=MESH)

    def greet(device):
        pl.semaphore_signal(barrier, inc=1, device_id=device, device_id_type=MESH)

    pl.when(up_too)(lambda: greet((r - 1, n)))
    pl.when(down_too)(lambda: greet((r + 1, n)))
    pl.when(has_prev)(lambda: greet((r - 1, across)))
    pl.when(has_next)(lambda: greet((r + 1, across)))
    greetings = len(greeted)
    for there in (up_too, down_too, has_prev, has_next):
        greetings += there.astype(jnp.int32)

    zero_tile = jnp.zeros((width, LANES), BF16)

    @pl.when(jnp.logical_not(has_prev))
    def _():
        for b in range(3):
            ext[b, 0] = zero_tile
            halo_recv[b, 0:2] = jnp.zeros_like(halo_recv[b, 0:2])

    @pl.when(jnp.logical_not(has_next))
    def _():
        for b in range(3):
            ext[b, 2] = zero_tile
            halo_recv[b, 2:4] = jnp.zeros_like(halo_recv[b, 2:4])

    def next_sem():
        at = sem_at[0]
        sem_at[0] = at + 1
        return refs.send_sem.at[at], refs.recv_sem.at[at]

    def remote(src, dst, device):
        ss, rs = next_sem()
        return pltpu.make_async_remote_copy(
            src_ref=src, dst_ref=dst, send_sem=ss, recv_sem=rs, device_id=device, device_id_type=MESH
        )

    def start(copies):
        for copy in copies:
            copy.start()

    def wait(copies):
        for copy in copies:
            copy.wait()

    def rows_of(at, count):
        return pool.at[pl.ds(at, count)]

    def aligned(at):
        return pl.multiple_of(at, 16)

    def vec(layer, which, rows=None):
        at = layer * VECTORS + which
        return vec_ref[0 : (width if rows is None else rows), at : at + 1]

    def put_vec(layer, which, value):
        at = layer * VECTORS + which
        refs.g_vec[0 : value.shape[0], at : at + 1] = jnp.sum(value, axis=1, keepdims=True)

    load_edges = pltpu.make_async_copy(refs.edges, g_edges, refs.local_sem.at[0])
    load_edges.start()

    def two_way(pairs):
        ups = [remote(a, b, (r - 1, col)) for col, a, b, _, _ in pairs]
        downs = [remote(a, b, (r + 1, col)) for col, _, _, a, b in pairs]

        def begin():
            pl.when(has_prev)(lambda: start(ups))
            pl.when(has_next)(lambda: start(downs))

        def finish():
            @pl.when(has_prev)
            def _():
                for up, down in zip(ups, downs, strict=True):
                    up.wait_send()
                    down.wait_recv()

            @pl.when(has_next)
            def _():
                for up, down in zip(ups, downs, strict=True):
                    down.wait_send()
                    up.wait_recv()

        return begin, finish

    def all_reduce(value, meanwhile=lambda: None):
        at = ar_at[0] % 2
        ar_at[0] += 1
        mine = pl.multiple_of(core * half_rows, half_rows)
        theirs = pl.multiple_of(half_rows - mine, half_rows)
        ar_part[at] = value
        one = remote(ar_part.at[at, pl.ds(theirs, half_rows)], ar_one.at[at], (r, buddy))
        one.start()
        one.wait()
        ar_two[at] = (ar_part[at, pl.ds(mine, half_rows)] + ar_one[at]).astype(BF16)
        two = remote(ar_two.at[at], ar_three.at[at], (r, across))
        two.start()
        meanwhile()
        two.wait()
        ar_tot[at, pl.ds(mine, half_rows)] = ar_two[at].astype(F32) + ar_three[at].astype(F32)
        span = ar_tot.at[at, pl.ds(mine, half_rows)]
        three = remote(span, span, (r, buddy))
        three.start()
        three.wait()
        return ar_tot.at[at]

    def extended(b):
        return jnp.concatenate([ext[b, 0], ext[b, 1], ext[b, 2]], axis=1)

    def halo(b, value):
        ext[b, 1] = value
        begin, finish = two_way([(n, ext.at[b, 1], ext.at[b, 2], ext.at[b, 1], ext.at[b, 0])])
        begin()
        return finish

    def halo_back(b, g_ext, g_own, beside_core=lambda: None, beside_far=lambda: None):
        at = ar_at[0] % 2
        ar_at[0] += 1
        my_half = pl.ds(pl.multiple_of(core * half_rows, half_rows), half_rows)
        their_half = pl.ds(pl.multiple_of(half_rows - core * half_rows, half_rows), half_rows)
        for k in range(3):
            part = g_ext[:, k * LANES : (k + 1) * LANES]
            g_part[k] = part + g_own if k == 1 else part
        halo_send[...] = g_part[:, their_half].astype(BF16)
        one = remote(halo_send, refs.halo_core, (r, buddy))
        one.start()
        beside_core()
        one.wait()
        half = refs.halo_half
        half[...] = (g_part[:, my_half] + refs.halo_core[...].astype(F32)).astype(BF16)
        two = remote(half.at[1], refs.halo_x, (r, across))
        begin, finish = two_way(
            [
                (n, half.at[0], halo_recv.at[b, 2], half.at[2], halo_recv.at[b, 0]),
                (across, half.at[0], halo_recv.at[b, 3], half.at[2], halo_recv.at[b, 1]),
            ]
        )
        begin()
        two.start()
        beside_far()
        two.wait()
        finish()
        total = half[1].astype(F32) + refs.halo_x[...].astype(F32)
        for k in (0, 2):
            total += halo_recv[b, k].astype(F32) + halo_recv[b, k + 1].astype(F32)
        ar_tot[at, my_half] = total
        span = ar_tot.at[at, my_half]
        three = remote(span, span, (r, buddy))
        three.start()
        three.wait()
        return ar_tot.at[at]

    FULL = (IN0, MO0, TB, ED, IN1, MO1)
    shard_at = ((core * 2 + xx) * 2 + yy) * 4 + zz
    short_at = yy * 4 + zz

    def my_shard(item):
        at = shard_at if item in FULL else short_at
        return aligned(plan.stage[item] + at * plan.sizes[item])

    def gather_z(item):
        size = plan.sizes[item]
        span = rows_of(my_shard(item), size)
        return [remote(span, span, peer) for peer in z_peers]

    def gather_span(item, count, device):
        size = plan.sizes[item]
        at = shard_at if item in FULL else short_at
        span = rows_of(aligned(plan.stage[item] + (at // count) * (count * size)), count * size)
        return [remote(span, span, device)]

    def gather_y(item):
        return gather_span(item, 4, y_peer)

    def edge_shard(x):
        at = ((core * 2 + x) * 2 + yy) * 4 + zz
        return rows_of(aligned(plan.stage[ED] + at * plan.ed_rows), plan.ed_rows)

    def edge_x():
        span = edge_shard(xx)
        return [remote(span, span, (r, across))]

    def edge_z():
        return [remote(edge_shard(x), edge_shard(x), peer) for x in range(2) for peer in z_peers]

    def edge_y():
        copies = []
        for x in range(2):
            at = ((core * 2 + x) * 2 + yy) * 4
            span = rows_of(aligned(plan.stage[ED] + at * plan.ed_rows), 4 * plan.ed_rows)
            copies.append(remote(span, span, y_peer))
        return copies

    def gather_x(item):
        return gather_span(item, 8, (r, across))

    def gather_c(item):
        return gather_span(item, 16, (r, buddy))

    def add_rows(at, other, count):
        block = next(b for b in (512, 256, 128, 64, 32, 16) if count % b == 0)

        def step(i, _):
            to = pl.ds(aligned(at + i * block), block)
            pool[to] = (pool[to].astype(F32) + pool[pl.ds(aligned(other + i * block), block)].astype(F32)).astype(BF16)
            return 0

        lax.fori_loop(0, count // block, step, 0)

    def reduce_pairs(item, stage):
        size, source = plan.sizes[item], plan.source[item]
        if stage == BY_CORE:
            count, mine, theirs, device = 16, core, 1 - core, (r, buddy)
        elif stage == BY_X:
            count, mine, theirs, device = 8, core * 2 + xx, core * 2 + 1 - xx, (r, across)
        else:
            base = (core * 2 + xx) * 2 if item in FULL else 0
            count, mine, theirs, device = 4, base + yy, base + 1 - yy, y_peer
        arrived = plan.recv[item, stage]
        copy = remote(
            rows_of(aligned(source + theirs * (count * size)), count * size),
            rows_of(arrived, count * size),
            device,
        )
        return [copy], lambda: add_rows(aligned(source + mine * (count * size)), arrived, count * size)

    def reduce_z(item):
        size, source = plan.sizes[item], plan.source[item]
        base = ((core * 2 + xx) * 2 + yy) * 4 if item in FULL else yy * 4
        copies = []
        for k in (1, 2, 3):
            to = lax.rem(zz + k, 4)
            copies.append(
                remote(
                    rows_of(aligned(source + (base + to) * size), size),
                    rows_of(plan.recv[item, BY_Z] + (k - 1) * size, size),
                    z_peers[k - 1],
                )
            )

        def total(first, count):
            value = pool[pl.ds(aligned(source + (base + zz) * size + first), count)].astype(F32)
            for k in range(3):
                value += pool[pl.ds(plan.recv[item, BY_Z] + k * size + first, count)].astype(F32)
            return value

        return copies, total

    def blocks():
        for at in range(32):
            c, x, y, z = at // 16, at // 8 % 2, at // 4 % 2, at % 4
            yield at, 2 * z + y, 2 * x + c

    def assemble_in(layer):
        at = plan.stage[IN[layer]]
        for k, rr, nn_ in blocks():
            wide[rr * plan.k_in : (rr + 1) * plan.k_in, nn_ * LANES : (nn_ + 1) * LANES] = pool[
                at + k * plan.in_rows : at + k * plan.in_rows + plan.k_in
            ].astype(F32)
        w_in[layer] = wide[: w_in.shape[1], :width].astype(BF16)
        turned = wide[2 * width : 2 * width + 2 * LANES, :width].T
        w_et[layer] = turned[:, :ew].astype(BF16)

    def assemble_mo(layer):
        at = plan.stage[MO[layer]]
        k_mid = plan.k_mid
        for k, rr, nn_ in blocks():
            to = (layer, slice(rr * k_mid, (rr + 1) * k_mid), slice(nn_ * LANES, (nn_ + 1) * LANES))
            first = at + k * plan.mo_rows
            w_mid[to] = pool[first : first + k_mid]
            w_out[to] = pool[first + k_mid : first + 2 * k_mid]
        w_midt[layer] = w_mid[layer].astype(F32).T.astype(BF16)

    def turn_square(value):
        wide[:ew, :ew] = value
        return wide[: 2 * LANES, : 2 * LANES].T[:ew, :ew]

    def assemble_edge():
        at, cols = plan.stage[ED], ew // 4
        long = up_to(w_in.shape[1], LANES)
        for k, rr, nn_ in blocks():
            first = at + k * plan.ed_rows
            wide[rr * plan.k_in : (rr + 1) * plan.k_in, nn_ * LANES : (nn_ + 1) * LANES] = pool[
                first : first + plan.k_in
            ].astype(F32)
        for nn_ in range(4):
            turned = wide[:long, nn_ * LANES : (nn_ + 1) * LANES].T
            for layer in range(2):
                e_int[layer, nn_ * cols : (nn_ + 1) * cols] = turned[
                    layer * cols : (layer + 1) * cols, : w_in.shape[1]
                ].astype(BF16)
        for layer in range(2):
            for k, rr, nn_ in blocks():
                first = at + k * plan.ed_rows + plan.in_pad + layer * plan.hid_pad
                wide[rr * plan.k_hid : (rr + 1) * plan.k_hid, nn_ * LANES : (nn_ + 1) * LANES] = pool[
                    first : first + plan.k_hid
                ].astype(F32)
            for nn_ in range(4):
                turned = wide[: 2 * LANES, nn_ * LANES : (nn_ + 1) * LANES].T
                for m in range(2):
                    e_hidt[layer, m, nn_ * cols : (nn_ + 1) * cols] = turned[
                        m * cols : (m + 1) * cols, :ew
                    ].astype(BF16)
        for layer in range(2):
            e_e[layer] = turn_square(e_int[layer, :, 2 * width :].astype(F32)).astype(BF16)
            for m in range(2):
                e_hid[layer, m] = turn_square(e_hidt[layer, m].astype(F32)).astype(BF16)

    def assemble_ffn(layer):
        at, k_mid = plan.stage[FF[layer]], plan.k_mid
        for y in range(2):
            for z in range(4):
                rr = 2 * z + y
                for j in range(ff // LANES):
                    for m, ref in enumerate((f_in, f_outt)):
                        first = at + (y * 4 + z) * plan.ff_rows + (m * (ff // LANES) + j) * k_mid
                        ref[layer, rr * k_mid : (rr + 1) * k_mid, j * LANES : (j + 1) * LANES] = pool[
                            first : first + k_mid
                        ]

    def emit_ffn(layer, g_fin, g_foutt):
        if not fast:
            refs.g_fin[layer] = g_fin.astype(BF16)
            refs.g_foutt[layer] = g_foutt.astype(BF16)
            return
        at, k_mid = plan.source[FF[layer]], plan.k_mid
        for m, value in enumerate((g_fin.astype(BF16), g_foutt.astype(BF16))):
            for y in range(2):
                for z in range(4):
                    rr = 2 * z + y
                    for j in range(ff // LANES):
                        first = at + (y * 4 + z) * plan.ff_rows + (m * (ff // LANES) + j) * k_mid
                        pool[first : first + k_mid] = value[
                            rr * k_mid : (rr + 1) * k_mid, j * LANES : (j + 1) * LANES
                        ]

    def emit_middle(layer, g_mid, g_out):
        if not fast:
            refs.g_mid[layer] = g_mid.astype(BF16)
            refs.g_out[layer] = g_out.astype(BF16)
            return
        at, k_mid = plan.source[MO[layer]], plan.k_mid
        for m, value in enumerate((g_mid.astype(BF16), g_out.astype(BF16))):
            for k, rr, nn_ in blocks():
                first = at + k * plan.mo_rows + m * k_mid
                pool[first : first + k_mid] = value[
                    rr * k_mid : (rr + 1) * k_mid, nn_ * LANES : (nn_ + 1) * LANES
                ]

    def emit_input(layer, g_own_rows, g_other_rows, g_edge_rows):
        if not fast:
            refs.g_in[layer, :width] = g_own_rows.astype(BF16)
            refs.g_in[layer, width : 2 * width] = g_other_rows.astype(BF16)
            refs.g_in[layer, 2 * width :] = g_edge_rows.astype(BF16)
            return
        wide[:width, :width] = g_own_rows
        wide[width : 2 * width, :width] = g_other_rows
        wide[2 * width : 2 * width + ew, :width] = g_edge_rows
        at = plan.source[IN[layer]]
        for k, rr, nn_ in blocks():
            first = at + k * plan.in_rows
            pool[first : first + plan.k_in] = wide[
                rr * plan.k_in : (rr + 1) * plan.k_in, nn_ * LANES : (nn_ + 1) * LANES
            ].astype(BF16)

    def emit_edge_all():
        at, cols = plan.source[ED], ew // 4
        long = up_to(w_in.shape[1], LANES)
        fill = LANES - 2 * cols
        for nn_ in range(4):
            span = slice(nn_ * cols, (nn_ + 1) * cols)
            tall = jnp.concatenate(
                [refs.g_eint[0, span].astype(F32), refs.g_eint[1, span].astype(F32), jnp.zeros((fill, long), F32)],
                axis=0,
            ).T
            wide[:long, nn_ * LANES : (nn_ + 1) * LANES] = tall
        for k, rr, nn_ in blocks():
            first = at + k * plan.ed_rows
            pool[first : first + plan.k_in] = wide[
                rr * plan.k_in : (rr + 1) * plan.k_in, nn_ * LANES : (nn_ + 1) * LANES
            ].astype(BF16)
        for layer in range(2):
            for nn_ in range(4):
                span = slice(nn_ * cols, (nn_ + 1) * cols)
                tall = jnp.concatenate(
                    [refs.g_ehid[layer, m, span].astype(F32) for m in range(2)]
                    + [jnp.zeros((fill, 2 * LANES), F32)],
                    axis=0,
                ).T
                wide[: 2 * LANES, nn_ * LANES : (nn_ + 1) * LANES] = tall
            for k, rr, nn_ in blocks():
                first = at + k * plan.ed_rows + plan.in_pad + layer * plan.hid_pad
                pool[first : first + plan.k_hid] = wide[
                    rr * plan.k_hid : (rr + 1) * plan.k_hid, nn_ * LANES : (nn_ + 1) * LANES
                ].astype(BF16)

    def act_at(kind, layer, slot):
        return pl.ds(aligned(plan.acts[layer] + kind * plan.act_rows + slot * width), width)

    U1, S1, S2 = 0, 1, 2
    W1, T1, W2, T2 = 0, 1, 2, 3

    def edge_act(kind, layer, base, j):
        slot = base + j if layer == 0 else slots + j
        return pl.ds(aligned(plan.edge_at + kind * plan.edge_rows + slot * ew), ew)

    def acts(kind, layer, base):
        return jnp.concatenate([pool[act_at(kind, layer, base + j)] for j in range(CHUNK)], axis=1)

    def edge_acts(kind, layer, base):
        return jnp.concatenate([pool[edge_act(kind, layer, base, j)] for j in range(CHUNK)], axis=1)

    def lanes_of(ref, base, *lead):
        return jnp.concatenate([ref[(*lead, base + j)] for j in range(CHUNK)], axis=1)

    def make_vectors():
        refs.g_vec[...] = jnp.zeros_like(refs.g_vec)
        mask_ref[...] = refs.mask[...].astype(F32)
        for layer in range(plan.layers):
            at = layer * VECTORS
            for k in range(6):
                wide[at + k : at + k + 1, :width] = refs.node_biases[k, layer : layer + 1]
            wide[at + GN1 : at + GN2 + 1, :width] = refs.node_gains[layer]
            first = pl.multiple_of(n * ff, ff)
            wide[at + FB : at + FB + 1, :ff] = refs.ffn_bias[layer : layer + 1, pl.ds(first, ff)]
            wide[at + C1 : at + C4 + 1, :ew] = refs.edge_biases[layer]
            wide[at + GE : at + GE + 1, :ew] = refs.edge_gains[layer : layer + 1]
        vec_ref[...] = wide[:LANES, :width].T

    def make_onehot():
        cells = lax.broadcasted_iota(jnp.int32, (3 * LANES, LANES), 0) + (r - 1) * LANES

        def step(s, _):
            onehot[s] = jnp.where(cells == refs.neighbors[pl.ds(s, 1), :], 1.0, 0.0).astype(BF16)
            eb[0, s] = g_edges[s].astype(BF16)
            return 0

        load_edges.wait()
        lax.fori_loop(0, slots, step, 0)

    def prepare_message(layer):
        proj[:, : 3 * LANES] = tn(w_in[layer, width : 2 * width, :], extended(layer)).astype(BF16)
        proj[:, 3 * LANES :] = w_et[layer]
        own[...] = tn(w_in[layer, :width, :], ext[layer, 1]) + vec(layer, B1)
        ubar[layer] = jnp.zeros((width, LANES), F32)

    def prepare_edge(layer):
        proj_e[:, : 3 * LANES] = nn(e_int[layer, :, width : 2 * width], extended(layer + 1)).astype(BF16)
        proj_e[:, 3 * LANES :] = e_int[layer, :, 2 * width :]
        own_e[...] = nn(e_int[layer, :, :width], ext[layer + 1, 1]) + vec(layer, C1, ew)

    def message_forward(layer, base):
        rows = jnp.concatenate([lanes_of(onehot, base), lanes_of(eb, base, layer)], axis=0)
        wide[:width, :] = nn(proj[...], rows)
        for j in range(CHUNK):
            z = wide[:width, j * LANES : (j + 1) * LANES] + own[...]
            pool[act_at(U1, layer, base + j)], pool[act_at(S1, layer, base + j)] = gelu_pair(z)
        wide[:width, :] = nn(w_midt[layer], acts(U1, layer, base))
        for j in range(CHUNK):
            z = wide[:width, j * LANES : (j + 1) * LANES] + vec(layer, B2)
            u2, pool[act_at(S2, layer, base + j)] = gelu_pair(z)
            ubar[layer] += u2.astype(F32) * mask_ref[pl.ds(base + j, 1), :]

    def edge_forward(layer, base, edge_ref, save):
        rows = jnp.concatenate([lanes_of(onehot, base), lanes_of(eb, base, layer)], axis=0)
        z = nn(proj_e[...], rows)
        for j in range(CHUNK):
            zj = z[:, j * LANES : (j + 1) * LANES] + own_e[...]
            pool[edge_act(W1, layer, base, j)], pool[edge_act(T1, layer, base, j)] = gelu_pair(zj)
        z = nn(e_hidt[layer, 0], edge_acts(W1, layer, base))
        for j in range(CHUNK):
            zj = z[:, j * LANES : (j + 1) * LANES] + vec(layer, C2, ew)
            pool[edge_act(W2, layer, base, j)], pool[edge_act(T2, layer, base, j)] = gelu_pair(zj)
        z = nn(e_hidt[layer, 1], edge_acts(W2, layer, base))
        for j in range(CHUNK):
            p = edge_ref[base + j] + z[:, j * LANES : (j + 1) * LANES] + vec(layer, C3, ew)
            hat, rstd = norm_parts(p)
            save(j, hat, rstd, p, hat * vec(layer, GE, ew) + vec(layer, C4, ew))

    def node_update(layer, before_ffn=lambda: None, beside_branch=lambda: None):
        total = all_reduce(ubar[layer])[...]
        high = total.astype(BF16)
        low = (total - high.astype(F32)).astype(BF16)
        counts = cnt_ref[...]
        sums = tn(w_out[layer], high) + tn(w_out[layer], low) + counts * vec(layer, B3)
        merged = state[layer] + sums * (1.0 / counts)
        joined_a[layer] = merged
        hat, _ = norm_parts(merged)
        hidden = hat * vec(layer, GN1) + vec(layer, SH1)
        h1b[layer] = hidden.astype(BF16)
        before_ffn()
        pre = tn(f_in[layer], h1b[layer]) + vec(layer, FB)
        act[layer], slope_f[layer] = gelu_pair(pre)
        branch = all_reduce(nn(f_outt[layer], act[layer]), beside_branch)[...]
        joined = hidden + (branch + vec(layer, B5))
        joined_c[layer] = joined
        hat, _ = norm_parts(joined)
        state[layer + 1] = hat * vec(layer, GN2) + vec(layer, SH2)
        return halo(layer + 1, state[layer + 1].astype(BF16))

    def clear_edge():
        for ref in (acc_h2, acc_h3, acc_ee, acc_t, acc_ts, acc_c):
            ref[...] = jnp.zeros_like(ref)

    def clear_message():
        for ref in (acc_mid, acc_e, acc_z, acc_zs, acc_b2):
            ref[...] = jnp.zeros_like(ref)

    def edge_backward(layer, base, parts):
        lows = []
        for j in range(CHUNK):
            hat, rstd, grad = parts(j)
            acc_c[0] += grad * hat
            acc_c[1] += grad
            dp = norm_back(hat, rstd, vec(layer, GE, ew), grad)
            g_edges[base + j] = dp
            low = dp.astype(BF16)
            acc_c[2] += low.astype(F32)
            lows.append(low)
        out = jnp.concatenate(lows, axis=1)
        acc_h3[...] += nt(out, edge_acts(W2, layer, base))
        grad_two = (nn(e_hid[layer, 1], out) * edge_acts(T2, layer, base).astype(F32)).astype(BF16)
        for j in range(CHUNK):
            acc_c[3] += grad_two[:, j * LANES : (j + 1) * LANES].astype(F32)
        acc_h2[...] += nt(grad_two, edge_acts(W1, layer, base))
        grad_one = (nn(e_hid[layer, 0], grad_two) * edge_acts(T1, layer, base).astype(F32)).astype(BF16)
        for j in range(CHUNK):
            acc_ts[...] += grad_one[:, j * LANES : (j + 1) * LANES].astype(F32)
        acc_t[...] += nt(grad_one, lanes_of(onehot, base))
        acc_ee[...] += nt(grad_one, lanes_of(eb, base, layer))
        back = nn(e_e[layer], grad_one)
        for j in range(CHUNK):
            g_edges[base + j] += back[:, j * LANES : (j + 1) * LANES]

    def edge_terms(layer):
        table = acc_t[...].astype(BF16)
        sums = acc_ts[...].astype(BF16)
        g_ext = tn(e_int[layer, :, width : 2 * width], table)
        g_own = tn(e_int[layer, :, :width], sums)
        return g_ext, g_own

    def edge_finish(layer):
        put_vec(layer, GE, acc_c[0])
        put_vec(layer, C4, acc_c[1])
        put_vec(layer, C3, acc_c[2])
        put_vec(layer, C2, acc_c[3])
        put_vec(layer, C1, acc_ts[...])
        refs.g_ehid[layer, 0, :, :ew] = acc_h2[...].astype(BF16)
        refs.g_ehid[layer, 1, :, :ew] = acc_h3[...].astype(BF16)
        table = acc_t[...].astype(BF16)
        sums = acc_ts[...].astype(BF16)
        refs.g_eint[layer, :, :width] = nt(sums, ext[layer + 1, 1]).astype(BF16)
        refs.g_eint[layer, :, width : 2 * width] = nt(table, extended(layer + 1)).astype(BF16)
        refs.g_eint[layer, :, 2 * width : 2 * width + ew] = acc_ee[...].astype(BF16)

    def message_back_two(layer, base):
        grads = []
        for j in range(CHUNK):
            s = base + j
            slope = pool[act_at(S2, layer, s)].astype(F32)
            dz = (vrow[...] * mask_ref[pl.ds(s, 1), :] * slope).astype(BF16)
            acc_b2[...] += dz.astype(F32)
            pool[act_at(S2, layer, s)] = dz
            grads.append(dz)
        acc_mid[...] += nt(acts(U1, layer, base), jnp.concatenate(grads, axis=1))

    def message_back_one(layer, base, add_edge):
        wide[:width, :] = nn(w_mid[layer], acts(S2, layer, base))
        grads = []
        for j in range(CHUNK):
            slope = pool[act_at(S1, layer, base + j)].astype(F32)
            dz = (wide[:width, j * LANES : (j + 1) * LANES] * slope).astype(BF16)
            acc_zs[...] += dz.astype(F32)
            grads.append(dz)
        grad_one = jnp.concatenate(grads, axis=1)
        acc_z[...] += nt(grad_one, lanes_of(onehot, base))
        acc_e[...] += nt(lanes_of(eb, base, layer), grad_one)
        back = nn(w_in[layer, 2 * width :, :], grad_one)
        for j in range(CHUNK):
            add_edge(base + j, back[:, j * LANES : (j + 1) * LANES])

    def middle_finish(layer):
        put_vec(layer, B2, acc_b2[...])
        emit_middle(layer, acc_mid[...], nt(ubar[layer].astype(BF16), ds_ref[...]))

    def message_terms(layer):
        table = acc_z[...].astype(BF16)
        sums = acc_zs[...].astype(BF16)
        g_ext = nn(w_in[layer, width : 2 * width, :], table)
        g_own = nn(w_in[layer, :width, :], sums)
        return g_ext, g_own

    def message_finish(layer):
        table = acc_z[...].astype(BF16)
        sums = acc_zs[...].astype(BF16)
        emit_input(layer, nt(ext[layer, 1], sums), nt(extended(layer), table), acc_e[...])
        put_vec(layer, B1, acc_zs[...])

    def node_back(layer, meanwhile=lambda: None):
        counts = cnt_ref[...]
        grad = dcur[...]
        hat, rstd = norm_parts(joined_c[layer])
        put_vec(layer, GN2, grad * hat)
        put_vec(layer, SH2, grad)
        dc = norm_back(hat, rstd, vec(layer, GN2), grad)
        dy = dc.astype(BF16)
        put_vec(layer, B5, dy.astype(F32))
        df = (tn(f_outt[layer], dy) * slope_f[layer].astype(F32)).astype(BF16)
        put_vec(layer, FB, df.astype(F32))
        part = nn(f_in[layer], df)
        total = all_reduce(part, meanwhile)
        emit_ffn(layer, nt(h1b[layer], df), nt(dy, act[layer]))
        grad = dc + total[...]
        hat, rstd = norm_parts(joined_a[layer])
        put_vec(layer, GN1, grad * hat)
        put_vec(layer, SH1, grad)
        da = norm_back(hat, rstd, vec(layer, GN1), grad)
        dcur[...] = da
        ds = (da * (1.0 / counts)).astype(BF16)
        ds_ref[...] = ds
        put_vec(layer, B3, ds.astype(F32) * counts)
        vrow[...] = nn(w_out[layer], ds)

    if fast:
        own_rows = refs.nodes.shape[0]
        mine = pl.multiple_of(n * own_rows, own_rows)
        k_mid = plan.k_mid

        def pack_in(layer):
            pool[pl.ds(my_shard(IN[layer]), plan.k_in)] = refs.msg_in[layer].astype(BF16)

        def pack_mo(layer):
            at = my_shard(MO[layer])
            pool[pl.ds(at, k_mid)] = refs.msg_mid[layer].astype(BF16)
            pool[pl.ds(aligned(at + k_mid), k_mid)] = refs.msg_out[layer].astype(BF16)

        def pack_ffn(layer):
            at = my_shard(FF[layer])
            for m, ref in enumerate((refs.ffn_in, refs.ffn_outt)):
                for j in range(ff // LANES):
                    to = aligned(at + (m * (ff // LANES) + j) * k_mid)
                    pool[pl.ds(to, k_mid)] = ref[layer, :, j * LANES : (j + 1) * LANES].astype(BF16)

        def pack_edge():
            cols = ew // 4
            for layer in range(2):
                wide[layer * cols : (layer + 1) * cols, : plan.k_in] = refs.edge_in_t[layer]
            turned = wide[:LANES, : 2 * LANES].T
            at = my_shard(ED)
            pool[pl.ds(at, plan.k_in)] = turned[: plan.k_in].astype(BF16)
            for layer in range(2):
                for m in range(2):
                    wide[: plan.k_hid, m * cols : (m + 1) * cols] = refs.edge_hidden[layer, m]
                to = aligned(at + plan.in_pad + layer * plan.hid_pad)
                pool[pl.ds(to, plan.k_hid)] = wide[: plan.k_hid, :LANES].astype(BF16)

        pack_in(0)
        pool[pl.ds(my_shard(TB), plan.tb_rows)] = refs.time_table[...].astype(BF16)
        refs.all_nodes[pl.ds(mine, own_rows)] = refs.nodes[...]
        refs.all_dnodes[pl.ds(mine, own_rows)] = refs.d_nodes[...]
        steps = jnp.zeros((1, own_rows), jnp.int32)
        for p in range(refs.time_index.shape[0]):
            steps += jnp.where(refs.protein_ids[...] == p, refs.time_index[p], 0)
        refs.all_misc[n, 0:1, :] = jnp.sum(refs.mask[...].astype(F32), axis=0, keepdims=True)
        refs.all_misc[n, 1:2, :own_rows] = steps.astype(F32)
        pl.semaphore_wait(barrier, greetings)

        node_copies, late_copies = [], []
        for k in (1, 2, 3):
            peer = (r, lax.rem(n + k, 4))
            for ref, group in (
                (refs.all_nodes.at[pl.ds(mine, own_rows)], node_copies),
                (refs.all_misc.at[n], node_copies),
                (refs.all_dnodes.at[pl.ds(mine, own_rows)], late_copies),
            ):
                group.append(remote(ref, ref, peer))
        every = range(FF1 + 1)
        gz = {item: gather_z(item) for item in every if item != ED}
        gy = {item: gather_y(item) for item in every if item != ED}
        gx = {item: gather_x(item) for item in FULL if item != ED}
        gc = {item: gather_c(item) for item in FULL}
        gx[ED], gz[ED], gy[ED] = edge_x(), edge_z(), edge_y()

        def pass_on(before, after, *items):
            for item in items:
                wait(before[item])
                start(after[item])

        def first(stage, *items):
            for item in items:
                start(stage[item])

        first(gz, TB, IN0)
        start(node_copies)
        pack_mo(0)
        first(gz, MO0)
        pack_edge()
        first(gx, ED)
        pass_on(gz, gy, TB, IN0)
        pack_in(1)
        pack_mo(1)
        pass_on(gy, gx, TB)
        make_vectors()
        wait(node_copies)
        misc = refs.all_misc[0]
        for k in range(1, 4):
            misc += refs.all_misc[k]
        cnt_ref[...] = misc[0:1]
        steps = jnp.concatenate([refs.all_misc[k, 1:2, :own_rows] for k in range(4)], axis=1)
        times = lax.broadcasted_iota(jnp.int32, (8 * plan.k_time, LANES), 0).astype(F32)
        refs.time_hot[...] = jnp.where(times == steps, 1.0, 0.0).astype(BF16)
        nodes_t = refs.all_nodes[...].T
        pass_on(gx, gc, TB)
        pass_on(gy, gx, IN0)
        wait(gc[TB])
        for k, rr, nn_ in blocks():
            at = plan.stage[TB] + k * plan.tb_rows
            refs.time_rows[rr * plan.k_time : (rr + 1) * plan.k_time, nn_ * LANES : (nn_ + 1) * LANES] = pool[
                at : at + plan.tb_rows
            ]
        state[0] = nodes_t + tn(refs.time_rows[...], refs.time_hot[...])
        finish = halo(0, state[0].astype(BF16))
        pass_on(gz, gy, MO0)
        first(gz, IN1, MO1)
        pack_ffn(0)
        first(gz, FF0)
        pass_on(gx, gz, ED)
        make_onehot()
        pack_ffn(1)
        pass_on(gy, gx, MO0)
        finish()
        pass_on(gz, gy, IN1, MO1)
        pass_on(gx, gc, IN0)
        wait(gc[IN0])
        assemble_in(0)
        pass_on(gx, gc, MO0)
        pass_on(gy, gx, IN1, MO1)
        pass_on(gz, gy, FF0)
        first(gz, FF1)
        wait(gc[MO0])
        assemble_mo(0)
    else:
        make_vectors()
        make_onehot()
        pl.semaphore_wait(barrier, greetings)
        state[0] = refs.h0[...]
        halo(0, state[0].astype(BF16))()

    prepare_message(0)

    def loop_a(i, _):
        message_forward(0, i * CHUNK)
        if fast:

            @pl.when(i == 1)
            def _():
                pass_on(gz, gy, ED)

        return 0

    lax.fori_loop(0, chunks, loop_a, 0)

    def need_ffn0():
        if fast:
            wait(gy[FF0])
            assemble_ffn(0)

    def beside_branch():
        if fast:
            pass_on(gx, gc, IN1, MO1)
            pass_on(gy, gc, ED)

    finish = node_update(0, need_ffn0, beside_branch)
    if fast:
        start(late_copies)
        wait(gc[IN1])
        assemble_in(1)
        wait(gc[MO1])
        assemble_mo(1)
        wait(gc[ED])
        assemble_edge()
    finish()
    prepare_edge(0)
    if fast:
        pass_on(gz, gy, FF1)
    prepare_message(1)

    def loop_b(i, _):
        base = i * CHUNK

        def save(j, hat, rstd, p, value):
            psum[base + j] = p
            edges_out[base + j] = value
            eb[1, base + j] = value.astype(BF16)

        edge_forward(0, base, g_edges, save)
        message_forward(1, base)
        return 0

    lax.fori_loop(0, chunks, loop_b, 0)
    load_grads = pltpu.make_async_copy(refs.d_edges, g_edges, refs.local_sem.at[1])
    load_grads.start()

    def need_ffn1():
        if fast:
            wait(late_copies)
            wait(gy[FF1])
            assemble_ffn(1)

    finish = node_update(1, need_ffn1)
    if fast:
        refs.all_nodes[...] = state[2].T
        nodes_out[...] = refs.all_nodes[pl.ds(mine, own_rows)]
    else:
        nodes_out[...] = state[2].T
    clear_edge()
    load_grads.wait()
    finish()
    prepare_edge(1)

    def loop_c(i, _):
        base = i * CHUNK
        kept = {}

        def save(j, hat, rstd, p, value):
            edges_out[base + j] = value
            kept[j] = (hat, rstd)

        edge_forward(1, base, edges_out, save)
        edge_backward(1, base, lambda j: (*kept[j], g_edges[base + j]))
        return 0

    lax.fori_loop(0, chunks, loop_c, 0)
    g_ext, g_own = edge_terms(1)
    dh = refs.all_dnodes[...].T if fast else refs.dh[...]
    dcur[...] = dh + halo_back(0, g_ext, g_own, beside_far=lambda: edge_finish(1))[...]
    node_back(1)
    clear_message()
    clear_edge()
    reduce_c, reduce_x, reduce_y, reduce_last = {}, {}, {}, {}
    if fast:
        for item in range(FF1 + 1):
            if item in FULL:
                reduce_c[item] = reduce_pairs(item, BY_CORE)
                reduce_x[item] = reduce_pairs(item, BY_X)
            reduce_y[item] = reduce_pairs(item, BY_Y)
            reduce_last[item] = reduce_z(item)

    def reduce_on(before, after, *items):
        for item in items:
            wait(before[item][0])
            before[item][1]()
            start(after[item][0])

    def put_ffn(layer):
        copies, total = reduce_last[FF[layer]]
        wait(copies)
        k_mid, parts = plan.k_mid, ff // LANES
        for m, ref in enumerate((refs.o_fin, refs.o_foutt)):
            for j in range(parts):
                ref[layer, :, j * LANES : (j + 1) * LANES] = total((m * parts + j) * k_mid, k_mid)

    def put_message(layer):
        copies, total = reduce_last[IN[layer]]
        wait(copies)
        refs.o_in[layer] = total(0, plan.k_in)
        copies, total = reduce_last[MO[layer]]
        wait(copies)
        refs.o_mid[layer] = total(0, plan.k_mid)
        refs.o_out[layer] = total(plan.k_mid, plan.k_mid)

    def put_edge():
        copies, total = reduce_last[ED]
        wait(copies)
        cols = ew // 4
        wide[: plan.in_pad, :LANES] = total(0, plan.in_pad)
        turned = wide[: 2 * LANES, :LANES].T
        hidden = total(plan.in_pad, 2 * plan.hid_pad)
        for layer in range(2):
            refs.o_edge[layer] = turned[layer * cols : (layer + 1) * cols, : plan.k_in]
            first = layer * plan.hid_pad
            for m in range(2):
                refs.o_hid[layer, m] = hidden[first : first + plan.k_hid, m * cols : (m + 1) * cols]

    if fast:
        start(reduce_y[FF1][0])

    def loop_d1(i, _):
        base = i * CHUNK

        def add_edge(s, value):
            g_edges[s] += value

        message_back_two(1, base)
        message_back_one(1, base, add_edge)
        return 0

    lax.fori_loop(0, chunks, loop_d1, 0)
    middle_finish(1)
    message_finish(1)
    m_ext, m_own = message_terms(1)
    acc_z[...] = m_ext
    acc_zs[...] = m_own
    if fast:
        start(reduce_c[IN1][0])
        start(reduce_c[MO1][0])

    def loop_d2(i, _):
        base = i * CHUNK
        edge_backward(0, base, lambda j: (*norm_parts(psum[base + j]), g_edges[base + j]))
        return 0

    lax.fori_loop(0, chunks, loop_d2, 0)
    e_ext, e_own = edge_terms(0)

    def beside_edge():
        if fast:
            reduce_on(reduce_c, reduce_x, IN1, MO1)
            reduce_on(reduce_y, reduce_last, FF1)
        edge_finish(0)
        if fast:
            emit_edge_all()

    dcur[...] += halo_back(1, acc_z[...] + e_ext, acc_zs[...] + e_own, beside_far=beside_edge)[...]

    def beside_node():
        if fast:
            start(reduce_c[ED][0])

    node_back(0, beside_node)
    clear_message()
    if fast:
        reduce_on(reduce_x, reduce_y, IN1, MO1)
        start(reduce_y[FF0][0])
        reduce_on(reduce_c, reduce_x, ED)

    def loop_e1(i, _):
        message_back_two(0, i * CHUNK)
        return 0

    lax.fori_loop(0, chunks, loop_e1, 0)
    middle_finish(0)
    if fast:
        start(reduce_c[MO0][0])

    def loop_e2(i, _):
        base = i * CHUNK

        def add_edge(s, value):
            g_edges[s] += value

        message_back_one(0, base, add_edge)
        if fast:

            @pl.when(i == 0)
            def _():
                reduce_on(reduce_c, reduce_x, MO0)

            @pl.when(i == 2)
            def _():
                reduce_on(reduce_y, reduce_last, IN1, MO1)

        return 0

    lax.fori_loop(0, chunks, loop_e2, 0)
    m_ext, m_own = message_terms(0)
    if not fast:
        message_finish(0)
        final = dcur[...] + halo_back(2, m_ext, m_own)[...]
        g_nodes[...] = final.T
        return

    def beside_last_core():
        message_finish(0)
        start(reduce_c[IN0][0])

    sums = refs.vec_sums
    partners = [(r, buddy), (r, across), y_peer]
    partners += [(2 * (zz + 1 - 2 * lax.rem(zz, 2)) + yy, n), (2 * lax.rem(zz + 2, 4) + yy, n)]
    rounds = [remote(sums.at[2 * k], sums.at[2 * k + 1], partners[k]) for k in range(5)]

    def vec_round(k):
        rounds[k].wait()
        sums[2 * k + 2] = sums[2 * k] + sums[2 * k + 1]
        if k < 4:
            rounds[k + 1].start()

    def beside_last_far():
        table = refs.g_vec[...].T
        sums[0] = jnp.zeros_like(sums[0])
        for layer in range(2):
            for which, row in VEC_ROWS.items():
                value = table[layer * VECTORS + which : layer * VECTORS + which + 1]
                at = layer * VEC_PER_LAYER + row
                if which == FB:
                    sums[0, pl.ds(at + n, 1)] = value
                else:
                    scale = 1.0 / plan.nbr_total if B3 <= which <= GN2 else 1.0
                    sums[0, at : at + 1] = value * scale
        rounds[0].start()
        reduce_on(reduce_c, reduce_x, IN0)
        reduce_on(reduce_y, reduce_last, FF0)
        reduce_on(reduce_x, reduce_y, MO0, ED)
        vec_round(0)
        put_ffn(1)
        put_message(1)

    final = dcur[...] + halo_back(2, m_ext, m_own, beside_last_core, beside_last_far)[...]
    high = final.astype(BF16)
    low = (final - high.astype(F32)).astype(BF16)
    g_times = (nt(refs.time_hot[...], high) + nt(refs.time_hot[...], low)) * (1.0 / plan.nbr_total)
    for k, rr, nn_ in blocks():
        at = plan.source[TB] + k * plan.tb_rows
        pool[at : at + plan.tb_rows] = g_times[
            rr * plan.k_time : (rr + 1) * plan.k_time, nn_ * LANES : (nn_ + 1) * LANES
        ].astype(BF16)
    start(reduce_c[TB][0])
    vec_round(1)
    reduce_on(reduce_x, reduce_y, IN0)
    reduce_on(reduce_c, reduce_x, TB)
    refs.all_dnodes[...] = final.T
    g_nodes[...] = refs.all_dnodes[pl.ds(mine, own_rows)]
    reduce_on(reduce_y, reduce_last, MO0)
    vec_round(2)
    reduce_on(reduce_x, reduce_y, TB)
    reduce_on(reduce_y, reduce_last, IN0, ED)
    vec_round(3)
    put_ffn(0)
    reduce_on(reduce_y, reduce_last, TB)
    vec_round(4)
    for layer in range(2):
        at = layer * VEC_PER_LAYER
        for k in range(6):
            refs.o_node_biases[k, layer : layer + 1] = sums[10, at + k : at + k + 1]
        refs.o_node_gains[layer] = sums[10, at + VEC_ROWS[GN1] : at + VEC_ROWS[GN2] + 1]
        for k in range(4):
            first = at + VEC_ROWS[FB] + k
            refs.o_ffn_bias[layer : layer + 1, k * ff : (k + 1) * ff] = sums[10, first : first + 1, :ff]
        first = at + VEC_ROWS[C1]
        refs.o_edge_biases[layer] = sums[10, first : first + 4, :ew]
        refs.o_edge_gains[layer : layer + 1] = sums[10, first + 4 : first + 5, :ew]
    put_message(0)
    put_edge()
    copies, total = reduce_last[TB]
    wait(copies)
    refs.o_time[...] = total(0, plan.tb_rows)


def vmem(shape, dtype):
    return pltpu.VMEM(shape, dtype)


def run_whole(plan, operands):
    lanes, slots, width, ew, ff, layers = LANES, plan.slots, plan.width, plan.ew, plan.ff, plan.layers
    rows_in = 2 * width + ew
    node_rows = lanes // plan.nbr_total if plan.fast else lanes
    outs = dict(
        nodes_out=((node_rows, width), F32),
        edges_out=((slots, ew, lanes), F32),
        g_nodes=((node_rows, width), F32),
        g_edges=((slots, ew, lanes), F32),
    )
    scratch = dict(
        onehot=vmem((slots, 3 * lanes, lanes), BF16),
        eb=vmem((layers, slots, ew, lanes), BF16),
        pool=vmem((plan.pool_rows, lanes), BF16),
        psum=vmem((slots, ew, lanes), F32),
        proj=vmem((width, 3 * lanes + ew), BF16),
        proj_e=vmem((ew, 3 * lanes + ew), BF16),
        own=vmem((width, lanes), F32),
        own_e=vmem((ew, lanes), F32),
        state=vmem((3, width, lanes), F32),
        ext=vmem((3, 3, width, lanes), BF16),
        joined_a=vmem((layers, width, lanes), F32),
        joined_c=vmem((layers, width, lanes), F32),
        h1b=vmem((layers, width, lanes), BF16),
        act=vmem((layers, ff, lanes), BF16),
        slope_f=vmem((layers, ff, lanes), BF16),
        ubar=vmem((layers, width, lanes), F32),
        ds=vmem((width, lanes), BF16),
        acc_mid=vmem((width, width), F32),
        acc_e=vmem((ew, width), F32),
        acc_z=vmem((width, 3 * lanes), F32),
        acc_zs=vmem((width, lanes), F32),
        acc_b2=vmem((width, lanes), F32),
        acc_h2=vmem((ew, ew), F32),
        acc_h3=vmem((ew, ew), F32),
        acc_ee=vmem((ew, ew), F32),
        acc_t=vmem((ew, 3 * lanes), F32),
        acc_ts=vmem((ew, lanes), F32),
        acc_c=vmem((4, ew, lanes), F32),
        wide=vmem((up_to(rows_in, lanes), CHUNK * lanes), F32),
        vrow=vmem((width, lanes), F32),
        dcur=vmem((width, lanes), F32),
        g_part=vmem((3, width, lanes), F32),
        halo_send=vmem((3, width // 2, lanes), BF16),
        halo_core=vmem((3, width // 2, lanes), BF16),
        halo_half=vmem((3, width // 2, lanes), BF16),
        halo_x=vmem((width // 2, lanes), BF16),
        halo_recv=vmem((3, 4, width // 2, lanes), BF16),
        ar_part=vmem((2, width, lanes), F32),
        ar_one=vmem((2, width // 2, lanes), F32),
        ar_two=vmem((2, width // 2, lanes), BF16),
        ar_three=vmem((2, width // 2, lanes), BF16),
        mask_rows=vmem((slots, lanes), F32),
        vectors=vmem((width, lanes), F32),
        ar_tot=vmem((2, width, lanes), F32),
        send_sem=pltpu.SemaphoreType.DMA((160,)),
        recv_sem=pltpu.SemaphoreType.DMA((160,)),
        local_sem=pltpu.SemaphoreType.DMA((2,)),
    )
    kept = dict(
        g_eint=((layers, ew, up_to(rows_in, lanes)), BF16),
        g_ehid=((layers, 2, ew, 2 * lanes), BF16),
        g_vec=((width, lanes), F32),
    )
    if plan.fast:
        scratch.update({name: vmem(*spec) for name, spec in kept.items()})
        own_rows = lanes // plan.nbr_total
        scratch.update(
            dict(
                counts=vmem((1, lanes), F32),
                all_nodes=vmem((lanes, width), F32),
                all_dnodes=vmem((lanes, width), F32),
                all_misc=vmem((plan.nbr_total, 8, lanes), F32),
                time_hot=vmem((8 * plan.k_time, lanes), BF16),
                time_rows=vmem((8 * plan.k_time, width), BF16),
                vec_sums=vmem((11, layers * VEC_PER_LAYER, width), F32),
                w_in=vmem((layers, rows_in, width), BF16),
                w_et=vmem((layers, width, ew), BF16),
                w_mid=vmem((layers, width, width), BF16),
                w_midt=vmem((layers, width, width), BF16),
                w_out=vmem((layers, width, width), BF16),
                f_in=vmem((layers, width, ff), BF16),
                f_outt=vmem((layers, width, ff), BF16),
                e_int=vmem((layers, ew, rows_in), BF16),
                e_e=vmem((layers, ew, ew), BF16),
                e_hid=vmem((layers, 2, ew, ew), BF16),
                e_hidt=vmem((layers, 2, ew, ew), BF16),
            )
        )
        outs.update(
            dict(
                o_in=((layers, plan.k_in, lanes), F32),
                o_mid=((layers, plan.k_mid, lanes), F32),
                o_out=((layers, plan.k_mid, lanes), F32),
                o_fin=((layers, plan.k_mid, ff), F32),
                o_foutt=((layers, plan.k_mid, ff), F32),
                o_edge=((layers, ew // 4, plan.k_in), F32),
                o_hid=((layers, 2, plan.k_hid, ew // 4), F32),
                o_time=((plan.tb_rows, lanes), F32),
                o_node_biases=((6, layers, width), F32),
                o_node_gains=((layers, 2, width), F32),
                o_ffn_bias=((layers, 4 * ff), F32),
                o_edge_gains=((layers, ew), F32),
                o_edge_biases=((layers, 4, ew), F32),
            )
        )
    else:
        outs.update(
            dict(
                g_in=((layers, rows_in, width), BF16),
                g_mid=((layers, width, width), BF16),
                g_out=((layers, width, width), BF16),
                g_fin=((layers, width, ff), BF16),
                g_foutt=((layers, width, ff), BF16),
                **kept,
            )
        )
    names = (*operands, *outs, *scratch)
    in_hbm, in_smem = dict(edges=1, d_edges=1), dict(time_index=1)
    place = lambda name: pl.BlockSpec(
        memory_space=pl.ANY if name in in_hbm else pltpu.SMEM if name in in_smem else pltpu.VMEM
    )
    results = pl.pallas_call(
        functools.partial(whole_kernel, plan, names),
        out_shape=tuple(jax.ShapeDtypeStruct(*spec) for spec in outs.values()),
        in_specs=[place(name) for name in operands],
        out_specs=[pl.BlockSpec(memory_space=pltpu.VMEM)] * len(outs),
        scratch_shapes=list(scratch.values()),
        compiler_params=pltpu.CompilerParams(
            collective_id=1, has_side_effects=True, vmem_limit_bytes=63 * 1024 * 1024
        ),
    )(*operands.values())
    return Refs(outs, results)


def hand_over(values):
    def kernel(*refs):
        for source, result in zip(refs[: len(values)], refs[len(values) :], strict=True):
            result[...] = source[...]

    return pl.pallas_call(
        kernel,
        out_shape=[jax.ShapeDtypeStruct(value.shape, value.dtype) for value in values],
        in_specs=[pl.BlockSpec(memory_space=pltpu.VMEM)] * len(values),
        out_specs=[pl.BlockSpec(memory_space=pltpu.VMEM)] * len(values),
    )(*values)


def gather_all(value, res_dim, nbr_dim):
    value = lax.all_gather(value, "res", axis=res_dim, tiled=True)
    return lax.all_gather(value, "nbr", axis=nbr_dim, tiled=True)


def scatter_sum(value, res_dim, nbr_dim):
    value = lax.psum_scatter(value, "res", scatter_dimension=res_dim, tiled=True)
    return lax.psum_scatter(value, "nbr", scatter_dimension=nbr_dim, tiled=True).astype(F32)


def low(value):
    return value.astype(BF16)


def per_device(
    nodes,
    edges,
    protein_ids,
    time_index,
    neighbors,
    edge_mask,
    time_table,
    msg_in,
    msg_mid,
    msg_out,
    ffn_in,
    ffn_out,
    edge_in,
    edge_hidden,
    node_gains,
    node_biases,
    ffn_bias,
    edge_gains,
    edge_biases,
    d_nodes,
    d_edges,
):
    res_total, nbr_total = lax.axis_size("res"), lax.axis_size("nbr")
    own_rows, width = nodes.shape
    ew = edges.shape[2]
    row_count, slot_count = neighbors.shape
    layers = msg_in.shape[0]
    n_at = lax.axis_index("nbr")
    ff = ffn_bias.shape[1] // nbr_total
    shards = (msg_in.shape[1], msg_mid.shape[1], edge_hidden.shape[2], time_table.shape[0])
    plan = Plan(res_total, nbr_total, slot_count, width, ew, ff, layers, shards)

    operands = dict(
        neighbors=neighbors.T,
        mask=edge_mask.T,
        edges=jnp.transpose(edges, (1, 2, 0)),
        d_edges=jnp.transpose(d_edges, (1, 2, 0)),
        node_biases=jnp.swapaxes(node_biases, 0, 1),
        node_gains=node_gains,
        ffn_bias=ffn_bias,
        edge_gains=edge_gains,
        edge_biases=edge_biases,
    )
    if plan.fast:
        operands.update(
            nodes=nodes,
            d_nodes=d_nodes,
            protein_ids=protein_ids[None, :],
            time_index=time_index,
            msg_in=msg_in,
            msg_mid=msg_mid,
            msg_out=msg_out,
            ffn_in=ffn_in,
            ffn_outt=jnp.swapaxes(ffn_out, 1, 2),
            edge_in_t=jnp.swapaxes(edge_in, 1, 2),
            edge_hidden=edge_hidden,
            time_table=time_table,
        )
        out = run_whole(plan, operands)
        (
            nodes_out, edges_out, g_nodes, g_edges, g_time, g_in, g_mid, g_out, g_fin, g_foutt, g_edge_t,
            g_hid, g_gains, g_biases, g_ffn_bias, g_edge_gains, g_edge_biases,
        ) = hand_over(
            [
                out.nodes_out, out.edges_out, out.g_nodes, out.g_edges, out.o_time, out.o_in, out.o_mid,
                out.o_out, out.o_fin, out.o_foutt, out.o_edge, out.o_hid, out.o_node_gains,
                out.o_node_biases, out.o_ffn_bias, out.o_edge_gains, out.o_edge_biases,
            ]
        )
        return (
            nodes_out,
            jnp.transpose(edges_out, (2, 0, 1)),
            g_nodes,
            jnp.transpose(g_edges, (2, 0, 1)),
            g_time,
            g_in,
            g_mid,
            g_out,
            g_fin,
            jnp.swapaxes(g_foutt, 1, 2),
            jnp.swapaxes(g_edge_t, 1, 2),
            g_hid,
            g_gains,
            jnp.swapaxes(g_biases, 0, 1),
            g_ffn_bias,
            g_edge_gains,
            g_edge_biases,
        )

    count_row = jnp.sum(edge_mask.astype(F32), axis=1)
    matches = protein_ids[:, None] == jnp.arange(time_index.shape[0], dtype=jnp.int32)[None, :]
    step_rows = jnp.sum(jnp.where(matches, time_index[None, :], 0), axis=1)
    mine = lambda a: lax.dynamic_slice_in_dim(a, n_at * own_rows, own_rows, axis=0)
    node_vectors = lambda rows: (rows[:, : SH2 + 1], rows[:, GN1 : GN2 + 1])
    table_low = gather_all(low(time_table), 0, 1)
    w_in = gather_all(low(msg_in), 1, 2)
    w_mid = gather_all(low(msg_mid), 1, 2)
    e_in = gather_all(low(edge_in), 1, 2)
    e_hid = gather_all(low(edge_hidden), 2, 3)
    step_onehot = (
        step_rows[:, None] == jnp.arange(table_low.shape[0], dtype=jnp.int32)[None, :]
    ).astype(BF16)
    state = nodes + jnp.dot(step_onehot, table_low, preferred_element_type=F32)
    count_block = jnp.zeros((8, width), F32).at[0, :row_count].set(count_row)
    packed = lax.all_gather(jnp.concatenate([state, d_nodes, count_block], axis=0), "nbr", axis=0)
    operands.update(
        dict(
            h0=packed[:, :own_rows].reshape(row_count, width).T,
            dh=packed[:, own_rows : 2 * own_rows].reshape(row_count, width).T,
            counts=jnp.sum(packed[:, 2 * own_rows, :row_count], axis=0)[None, :],
            w_in=w_in,
            w_et=jnp.swapaxes(w_in[:, 2 * width :], 1, 2),
            w_mid=w_mid,
            w_midt=jnp.swapaxes(w_mid, 1, 2),
            w_out=gather_all(low(msg_out), 1, 2),
            f_in=lax.all_gather(low(ffn_in), "res", axis=1, tiled=True),
            f_outt=lax.all_gather(jnp.swapaxes(low(ffn_out), 1, 2), "res", axis=1, tiled=True),
            e_int=jnp.swapaxes(e_in, 1, 2),
            e_e=e_in[:, 2 * width :],
            e_hid=e_hid,
            e_hidt=jnp.swapaxes(e_hid, 2, 3),
        )
    )
    out = run_whole(plan, operands)
    g_nodes = mine(out.g_nodes)
    g_table_full = lax.dot_general(
        step_onehot.astype(F32),
        g_nodes,
        (((0,), (0,)), ((), ())),
        precision=lax.Precision.HIGHEST,
        preferred_element_type=F32,
    )
    rows = out.g_vec.T[: layers * VECTORS].reshape(layers, VECTORS, width)
    shared = rows[:, B3 : GN2 + 1] * (1.0 / nbr_total)
    g_bias_ffn = lax.dynamic_update_slice_in_dim(
        jnp.zeros_like(ffn_bias), rows[:, FB, :ff], n_at * ff, axis=1
    )
    vectors, g_ffn_bias, g_edge_biases, g_edge_gains = lax.psum(
        (
            jnp.concatenate([rows[:, :B3], shared], axis=1),
            g_bias_ffn,
            rows[:, C1 : C4 + 1, :ew],
            rows[:, GE, :ew],
        ),
        ("res", "nbr"),
    )
    g_node_biases, g_node_gains = node_vectors(vectors)
    scatter_res = lambda a: lax.psum_scatter(a, "res", scatter_dimension=1, tiled=True).astype(F32)
    return (
        mine(out.nodes_out),
        jnp.transpose(out.edges_out, (2, 0, 1)),
        g_nodes,
        jnp.transpose(out.g_edges, (2, 0, 1)),
        scatter_sum(low(g_table_full), 0, 1),
        scatter_sum(out.g_in, 1, 2),
        scatter_sum(out.g_mid, 1, 2),
        scatter_sum(out.g_out, 1, 2),
        scatter_res(out.g_fin),
        jnp.swapaxes(scatter_res(out.g_foutt), 1, 2),
        jnp.swapaxes(scatter_sum(out.g_eint[:, :, : 2 * width + ew], 2, 1), 1, 2),
        scatter_sum(jnp.swapaxes(out.g_ehid[..., :ew], 2, 3), 2, 3),
        g_node_gains,
        g_node_biases,
        g_ffn_bias,
        g_edge_gains,
        g_edge_biases,
    )


def solution(mesh):
    return jax.shard_map(
        per_device,
        mesh=mesh,
        in_specs=(
            P(("res", "nbr"), None),
            P("res", "nbr", None),
            P(("res", "nbr")),
            P(),
            P("res", "nbr"),
            P("res", "nbr"),
            P("res", "nbr"),
            P(None, "res", "nbr"),
            P(None, "res", "nbr"),
            P(None, "res", "nbr"),
            P(None, "res", "nbr"),
            P(None, "nbr", "res"),
            P(None, "res", "nbr"),
            P(None, None, "res", "nbr"),
            P(),
            P(),
            P(),
            P(),
            P(),
            P(("res", "nbr"), None),
            P("res", "nbr", None),
        ),
        out_specs=(
            P(("res", "nbr"), None),
            P("res", "nbr", None),
            P(("res", "nbr"), None),
            P("res", "nbr", None),
            P("res", "nbr"),
            P(None, "res", "nbr"),
            P(None, "res", "nbr"),
            P(None, "res", "nbr"),
            P(None, "res", "nbr"),
            P(None, "nbr", "res"),
            P(None, "res", "nbr"),
            P(None, None, "res", "nbr"),
            P(),
            P(),
            P(),
            P(),
            P(),
        ),
        check_vma=False,
    )
```

```python
import functools

import jax
import jax.numpy as jnp
from jax import lax
from jax.experimental import pallas as pl
from jax.experimental.pallas import tpu as pltpu
from jax.sharding import PartitionSpec as P

NORM_EPS = 1e-05
F32 = jnp.float32
BF16 = jnp.bfloat16
MESH = pl.DeviceIdType.MESH
LANES = 128
CHUNK = 5
TANH_A = 0.7978845608028654
TANH_B = 0.044715
B1, B2, B3, B5, SH1, SH2, GN1, GN2, FB, C1, C2, C3, C4, GE = range(14)
VECTORS = 14
VEC_ROWS = {B1: 0, B2: 1, B3: 2, B5: 3, SH1: 4, SH2: 5, GN1: 6, GN2: 7, FB: 8, C1: 12, C2: 13, C3: 14, C4: 15, GE: 16}
VEC_PER_LAYER = 20
IN0, TB, MO0, FF0, ED, IN1, MO1, FF1 = range(8)
IN, MO, FF = (IN0, IN1), (MO0, MO1), (FF0, FF1)
BY_CORE, BY_X, BY_Y, BY_Z = range(4)


def nn(left, right):
    return jnp.dot(left, right, preferred_element_type=F32)


def nt(left, right):
    return lax.dot_general(left, right, (((1,), (1,)), ((), ())), preferred_element_type=F32)


def tn(left, right):
    return lax.dot_general(left, right, (((0,), (0,)), ((), ())), preferred_element_type=F32)


def gelu_pair(z):
    sq = z * z
    half = 0.5 + 0.5 * jnp.tanh(z * (TANH_A + (TANH_A * TANH_B) * sq))
    value = z * half
    slope = half + (value * (1.0 - half)) * (2.0 * TANH_A + (6.0 * TANH_A * TANH_B) * sq)
    return value.astype(BF16), slope.astype(BF16)


def norm_parts(value):
    scale = 1.0 / value.shape[0]
    centre = jnp.sum(value, axis=0, keepdims=True) * scale
    offset = value - centre
    spread = jnp.sum(offset * offset, axis=0, keepdims=True) * scale
    rstd = lax.rsqrt(spread + NORM_EPS)
    return offset * rstd, rstd


def norm_back(hat, rstd, gain, grad):
    scale = 1.0 / hat.shape[0]
    weighted = grad * gain
    first = jnp.sum(weighted, axis=0, keepdims=True) * scale
    second = jnp.sum(weighted * hat, axis=0, keepdims=True) * scale
    return rstd * (weighted - first - hat * second)


class Refs:
    def __init__(self, names, values):
        self.__dict__.update(zip(names, values, strict=True))


def up_to(value, step):
    return (value + step - 1) // step * step


class Plan:
    def __init__(self, res_total, nbr_total, slots, width, ew, ff, layers, shards):
        self.res_total, self.nbr_total = res_total, nbr_total
        self.slots, self.width, self.ew, self.ff, self.layers = slots, width, ew, ff, layers
        self.k_in, self.k_mid, self.k_hid, self.k_time = shards
        self.fast = (res_total, nbr_total) == (8, 4) and self.k_in % 8 == 0 and self.k_mid % 16 == 0
        acts = slots * width
        self.acts = [0, 3 * acts]
        self.act_rows = acts
        edge_rows = (slots + CHUNK) * ew
        self.pool_rows = 6 * acts + 4 * edge_rows
        self.edge_at = 6 * acts
        self.edge_rows = edge_rows
        if not self.fast:
            return
        self.in_pad = up_to(self.k_in, 16)
        self.hid_pad = up_to(self.k_hid, 16)
        self.in_rows = self.in_pad
        self.mo_rows = 2 * self.k_mid
        self.ed_rows = self.in_pad + 2 * self.hid_pad
        self.tb_rows = self.k_time
        self.ff_rows = 2 * self.k_mid * (ff // LANES)
        one = 3 * acts
        sizes = {IN0: self.in_rows, MO0: self.mo_rows, ED: self.ed_rows, IN1: self.in_rows,
                 MO1: self.mo_rows, TB: self.tb_rows, FF0: self.ff_rows, FF1: self.ff_rows}
        self.sizes = sizes
        self.stage = {}
        at = 0
        for item in (IN0, TB, MO0):
            self.stage[item] = at
            at += 32 * sizes[item]
        at = one
        for item in (IN1, MO1, ED):
            self.stage[item] = at
            at += 32 * sizes[item]
        top = at
        at = 2 * one
        for item in (FF0, FF1):
            self.stage[item] = at
            at += 8 * sizes[item]
        top = max(top, at)
        self.source, self.recv = {}, {}
        at = 0
        for item in (MO0, IN0):
            self.source[item] = at
            at += 32 * sizes[item]
        at = one
        for item in (IN1, MO1, ED):
            self.source[item] = at
            at += 32 * sizes[item]
        for stage, count in ((BY_CORE, 16), (BY_X, 8), (BY_Y, 4)):
            self.recv[ED, stage] = at
            at += count * sizes[ED]
        at = max(at, 2 * one)
        self.source[FF1] = at
        self.recv[FF1, BY_Y] = at + 8 * sizes[FF1]
        at += 12 * sizes[FF1]
        for stage, count in ((BY_CORE, 16), (BY_X, 8), (BY_Y, 4)):
            for item in (IN1, MO1):
                self.recv[item, stage] = at
                at += count * sizes[item]
        self.recv[IN0, BY_CORE], self.recv[MO0, BY_CORE] = self.recv[IN1, BY_CORE], self.recv[MO1, BY_CORE]
        top = max(top, at)
        self.edge_at = top
        self.source[FF0] = top
        self.recv[FF0, BY_Y] = top + 8 * sizes[FF0]
        at = top + 12 * sizes[FF0]
        for stage, count in ((BY_X, 8), (BY_Y, 4)):
            for item in (IN0, MO0):
                self.recv[item, stage] = at
                at += count * sizes[item]
        at = max(at, top + 4 * edge_rows)
        self.source[TB] = at
        at += 32 * sizes[TB]
        for stage, count in ((BY_CORE, 16), (BY_X, 8), (BY_Y, 4)):
            self.recv[TB, stage] = at
            at += count * sizes[TB]
        for item in sizes:
            self.recv[item, BY_Z] = at
            at += 3 * sizes[item]
        self.pool_rows = at


def whole_kernel(plan, names, *values):
    refs = Refs(names, values)
    fast = plan.fast
    mask_ref, vec_ref = refs.mask_rows, refs.vectors
    onehot, eb, pool, psum, proj, proj_e = refs.onehot, refs.eb, refs.pool, refs.psum, refs.proj, refs.proj_e
    own, own_e, state, ext = refs.own, refs.own_e, refs.state, refs.ext
    joined_a, joined_c, h1b, act = refs.joined_a, refs.joined_c, refs.h1b, refs.act
    slope_f, ubar, ds_ref = refs.slope_f, refs.ubar, refs.ds
    acc_mid, acc_e, acc_z, acc_zs, acc_b2 = refs.acc_mid, refs.acc_e, refs.acc_z, refs.acc_zs, refs.acc_b2
    acc_h2, acc_h3, acc_ee = refs.acc_h2, refs.acc_h3, refs.acc_ee
    acc_t, acc_ts, acc_c = refs.acc_t, refs.acc_ts, refs.acc_c
    wide, vrow, dcur, g_part = refs.wide, refs.vrow, refs.dcur, refs.g_part
    halo_send, halo_recv = refs.halo_send, refs.halo_recv
    ar_part, ar_one, ar_two, ar_three = refs.ar_part, refs.ar_one, refs.ar_two, refs.ar_three
    ar_tot = refs.ar_tot
    w_in, w_et, w_mid, w_midt, w_out = refs.w_in, refs.w_et, refs.w_mid, refs.w_midt, refs.w_out
    f_in, f_outt, e_int, e_e = refs.f_in, refs.f_outt, refs.e_int, refs.e_e
    e_hid, e_hidt = refs.e_hid, refs.e_hidt
    nodes_out, g_nodes = refs.nodes_out, refs.g_nodes
    edges_out, g_edges = refs.edge_state, refs.edge_grad
    cnt_ref = refs.counts
    res_total = plan.res_total
    slots, width, ew, ff = plan.slots, plan.width, plan.ew, plan.ff
    r = lax.axis_index("res")
    n = lax.axis_index("nbr")
    core = lax.rem(n, 2)
    xx = n // 2
    yy = lax.rem(r, 2)
    zz = r // 2
    buddy = n + 1 - 2 * core
    across = lax.rem(n + 2, 4)
    chunks = slots // CHUNK
    half_rows = width // 2
    has_prev = r > 0
    has_next = r < res_total - 1
    sem_at = [0]
    ar_at = [0]

    greeted = [(r, buddy), (r, across)]
    z_peers = []
    if fast:
        greeted.append((r, lax.rem(buddy + 2, 4)))
        y_peer = (r + 1 - 2 * yy, n)
        z_peers = [(2 * lax.rem(zz + k, 4) + yy, n) for k in (1, 2, 3)]
        greeted += [y_peer, *z_peers]
        up_too = jnp.logical_and(yy == 0, has_prev)
        down_too = jnp.logical_and(yy == 1, has_next)
    else:
        up_too, down_too = has_prev, has_next
    barrier = pltpu.get_barrier_semaphore()
    for device in greeted:
        pl.semaphore_signal(barrier, inc=1, device_id=device, device_id_type=MESH)

    def greet(device):
        pl.semaphore_signal(barrier, inc=1, device_id=device, device_id_type=MESH)

    pl.when(up_too)(lambda: greet((r - 1, n)))
    pl.when(down_too)(lambda: greet((r + 1, n)))
    pl.when(has_prev)(lambda: greet((r - 1, across)))
    pl.when(has_next)(lambda: greet((r + 1, across)))
    greetings = len(greeted)
    for there in (up_too, down_too, has_prev, has_next):
        greetings += there.astype(jnp.int32)

    zero_tile = jnp.zeros((width, LANES), BF16)

    @pl.when(jnp.logical_not(has_prev))
    def _():
        for b in range(3):
            ext[b, 0] = zero_tile
            halo_recv[b, 0:2] = jnp.zeros_like(halo_recv[b, 0:2])

    @pl.when(jnp.logical_not(has_next))
    def _():
        for b in range(3):
            ext[b, 2] = zero_tile
            halo_recv[b, 2:4] = jnp.zeros_like(halo_recv[b, 2:4])

    def next_sem():
        at = sem_at[0]
        sem_at[0] = at + 1
        return refs.send_sem.at[at], refs.recv_sem.at[at]

    def remote(src, dst, device):
        ss, rs = next_sem()
        return pltpu.make_async_remote_copy(
            src_ref=src, dst_ref=dst, send_sem=ss, recv_sem=rs, device_id=device, device_id_type=MESH
        )

    def start(copies):
        for copy in copies:
            copy.start()

    def wait(copies):
        for copy in copies:
            copy.wait()

    def rows_of(at, count):
        return pool.at[pl.ds(at, count)]

    def aligned(at):
        return pl.multiple_of(at, 16)

    def vec(layer, which, rows=None):
        at = layer * VECTORS + which
        return vec_ref[0 : (width if rows is None else rows), at : at + 1]

    def put_vec(layer, which, value):
        at = layer * VECTORS + which
        refs.g_vec[0 : value.shape[0], at : at + 1] = jnp.sum(value, axis=1, keepdims=True)

    load_edges = pltpu.make_async_copy(refs.edges, g_edges, refs.local_sem.at[0])
    load_edges.start()

    def two_way(pairs):
        ups = [remote(a, b, (r - 1, col)) for col, a, b, _, _ in pairs]
        downs = [remote(a, b, (r + 1, col)) for col, _, _, a, b in pairs]

        def begin():
            pl.when(has_prev)(lambda: start(ups))
            pl.when(has_next)(lambda: start(downs))

        def finish():
            @pl.when(has_prev)
            def _():
                for up, down in zip(ups, downs, strict=True):
                    up.wait_send()
                    down.wait_recv()

            @pl.when(has_next)
            def _():
                for up, down in zip(ups, downs, strict=True):
                    down.wait_send()
                    up.wait_recv()

        return begin, finish

    def all_reduce(value, meanwhile=lambda: None):
        at = ar_at[0] % 2
        ar_at[0] += 1
        mine = pl.multiple_of(core * half_rows, half_rows)
        theirs = pl.multiple_of(half_rows - mine, half_rows)
        ar_part[at] = value
        one = remote(ar_part.at[at, pl.ds(theirs, half_rows)], ar_one.at[at], (r, buddy))
        one.start()
        one.wait()
        ar_two[at] = (ar_part[at, pl.ds(mine, half_rows)] + ar_one[at]).astype(BF16)
        two = remote(ar_two.at[at], ar_three.at[at], (r, across))
        two.start()
        meanwhile()
        two.wait()
        ar_tot[at, pl.ds(mine, half_rows)] = ar_two[at].astype(F32) + ar_three[at].astype(F32)
        span = ar_tot.at[at, pl.ds(mine, half_rows)]
        three = remote(span, span, (r, buddy))
        three.start()
        three.wait()
        return ar_tot.at[at]

    def extended(b):
        return jnp.concatenate([ext[b, 0], ext[b, 1], ext[b, 2]], axis=1)

    def halo(b, value):
        ext[b, 1] = value
        begin, finish = two_way([(n, ext.at[b, 1], ext.at[b, 2], ext.at[b, 1], ext.at[b, 0])])
        begin()
        return finish

    def halo_back(b, g_ext, g_own, beside_core=lambda: None, beside_far=lambda: None):
        at = ar_at[0] % 2
        ar_at[0] += 1
        my_half = pl.ds(pl.multiple_of(core * half_rows, half_rows), half_rows)
        their_half = pl.ds(pl.multiple_of(half_rows - core * half_rows, half_rows), half_rows)
        for k in range(3):
            part = g_ext[:, k * LANES : (k + 1) * LANES]
            g_part[k] = part + g_own if k == 1 else part
        halo_send[...] = g_part[:, their_half].astype(BF16)
        one = remote(halo_send, refs.halo_core, (r, buddy))
        one.start()
        beside_core()
        one.wait()
        half = refs.halo_half
        half[...] = (g_part[:, my_half] + refs.halo_core[...].astype(F32)).astype(BF16)
        two = remote(half.at[1], refs.halo_x, (r, across))
        begin, finish = two_way(
            [
                (n, half.at[0], halo_recv.at[b, 2], half.at[2], halo_recv.at[b, 0]),
                (across, half.at[0], halo_recv.at[b, 3], half.at[2], halo_recv.at[b, 1]),
            ]
        )
        begin()
        two.start()
        beside_far()
        two.wait()
        finish()
        total = half[1].astype(F32) + refs.halo_x[...].astype(F32)
        for k in (0, 2):
            total += halo_recv[b, k].astype(F32) + halo_recv[b, k + 1].astype(F32)
        ar_tot[at, my_half] = total
        span = ar_tot.at[at, my_half]
        three = remote(span, span, (r, buddy))
        three.start()
        three.wait()
        return ar_tot.at[at]

    FULL = (IN0, MO0, TB, ED, IN1, MO1)
    shard_at = ((core * 2 + xx) * 2 + yy) * 4 + zz
    short_at = yy * 4 + zz

    def my_shard(item):
        at = shard_at if item in FULL else short_at
        return aligned(plan.stage[item] + at * plan.sizes[item])

    def gather_z(item):
        size = plan.sizes[item]
        span = rows_of(my_shard(item), size)
        return [remote(span, span, peer) for peer in z_peers]

    def gather_span(item, count, device):
        size = plan.sizes[item]
        at = shard_at if item in FULL else short_at
        span = rows_of(aligned(plan.stage[item] + (at // count) * (count * size)), count * size)
        return [remote(span, span, device)]

    def gather_y(item):
        return gather_span(item, 4, y_peer)

    def gather_x(item):
        return gather_span(item, 8, (r, across))

    def gather_c(item):
        return gather_span(item, 16, (r, buddy))

    def add_rows(at, other, count):
        block = next(b for b in (512, 256, 128, 64, 32, 16) if count % b == 0)

        def step(i, _):
            to = pl.ds(aligned(at + i * block), block)
            pool[to] = (pool[to].astype(F32) + pool[pl.ds(aligned(other + i * block), block)].astype(F32)).astype(BF16)
            return 0

        lax.fori_loop(0, count // block, step, 0)

    def reduce_pairs(item, stage):
        size, source = plan.sizes[item], plan.source[item]
        if stage == BY_CORE:
            count, mine, theirs, device = 16, core, 1 - core, (r, buddy)
        elif stage == BY_X:
            count, mine, theirs, device = 8, core * 2 + xx, core * 2 + 1 - xx, (r, across)
        else:
            base = (core * 2 + xx) * 2 if item in FULL else 0
            count, mine, theirs, device = 4, base + yy, base + 1 - yy, y_peer
        arrived = plan.recv[item, stage]
        copy = remote(
            rows_of(aligned(source + theirs * (count * size)), count * size),
            rows_of(arrived, count * size),
            device,
        )
        return [copy], lambda: add_rows(aligned(source + mine * (count * size)), arrived, count * size)

    def reduce_z(item):
        size, source = plan.sizes[item], plan.source[item]
        base = ((core * 2 + xx) * 2 + yy) * 4 if item in FULL else yy * 4
        copies = []
        for k in (1, 2, 3):
            to = lax.rem(zz + k, 4)
            copies.append(
                remote(
                    rows_of(aligned(source + (base + to) * size), size),
                    rows_of(plan.recv[item, BY_Z] + (k - 1) * size, size),
                    z_peers[k - 1],
                )
            )

        def total(first, count):
            value = pool[pl.ds(aligned(source + (base + zz) * size + first), count)].astype(F32)
            for k in range(3):
                value += pool[pl.ds(plan.recv[item, BY_Z] + k * size + first, count)].astype(F32)
            return value

        return copies, total

    def blocks():
        for at in range(32):
            c, x, y, z = at // 16, at // 8 % 2, at // 4 % 2, at % 4
            yield at, 2 * z + y, 2 * x + c

    def assemble_in(layer):
        at = plan.stage[IN[layer]]
        for k, rr, nn_ in blocks():
            wide[rr * plan.k_in : (rr + 1) * plan.k_in, nn_ * LANES : (nn_ + 1) * LANES] = pool[
                at + k * plan.in_rows : at + k * plan.in_rows + plan.k_in
            ].astype(F32)
        w_in[layer] = wide[: w_in.shape[1], :width].astype(BF16)
        turned = wide[2 * width : 2 * width + 2 * LANES, :width].T
        w_et[layer] = turned[:, :ew].astype(BF16)

    def assemble_mo(layer):
        at = plan.stage[MO[layer]]
        k_mid = plan.k_mid
        for k, rr, nn_ in blocks():
            to = (layer, slice(rr * k_mid, (rr + 1) * k_mid), slice(nn_ * LANES, (nn_ + 1) * LANES))
            first = at + k * plan.mo_rows
            w_mid[to] = pool[first : first + k_mid]
            w_out[to] = pool[first + k_mid : first + 2 * k_mid]
        w_midt[layer] = w_mid[layer].astype(F32).T.astype(BF16)

    def turn_square(value):
        wide[:ew, :ew] = value
        return wide[: 2 * LANES, : 2 * LANES].T[:ew, :ew]

    def assemble_edge():
        at, cols = plan.stage[ED], ew // 4
        long = up_to(w_in.shape[1], LANES)
        for k, rr, nn_ in blocks():
            first = at + k * plan.ed_rows
            wide[rr * plan.k_in : (rr + 1) * plan.k_in, nn_ * LANES : (nn_ + 1) * LANES] = pool[
                first : first + plan.k_in
            ].astype(F32)
        for nn_ in range(4):
            turned = wide[:long, nn_ * LANES : (nn_ + 1) * LANES].T
            for layer in range(2):
                e_int[layer, nn_ * cols : (nn_ + 1) * cols] = turned[
                    layer * cols : (layer + 1) * cols, : w_in.shape[1]
                ].astype(BF16)
        for layer in range(2):
            for k, rr, nn_ in blocks():
                first = at + k * plan.ed_rows + plan.in_pad + layer * plan.hid_pad
                wide[rr * plan.k_hid : (rr + 1) * plan.k_hid, nn_ * LANES : (nn_ + 1) * LANES] = pool[
                    first : first + plan.k_hid
                ].astype(F32)
            for nn_ in range(4):
                turned = wide[: 2 * LANES, nn_ * LANES : (nn_ + 1) * LANES].T
                for m in range(2):
                    e_hidt[layer, m, nn_ * cols : (nn_ + 1) * cols] = turned[
                        m * cols : (m + 1) * cols, :ew
                    ].astype(BF16)
        for layer in range(2):
            e_e[layer] = turn_square(e_int[layer, :, 2 * width :].astype(F32)).astype(BF16)
            for m in range(2):
                e_hid[layer, m] = turn_square(e_hidt[layer, m].astype(F32)).astype(BF16)

    def assemble_ffn(layer):
        at, k_mid = plan.stage[FF[layer]], plan.k_mid
        for y in range(2):
            for z in range(4):
                rr = 2 * z + y
                for j in range(ff // LANES):
                    for m, ref in enumerate((f_in, f_outt)):
                        first = at + (y * 4 + z) * plan.ff_rows + (m * (ff // LANES) + j) * k_mid
                        ref[layer, rr * k_mid : (rr + 1) * k_mid, j * LANES : (j + 1) * LANES] = pool[
                            first : first + k_mid
                        ]

    def emit_ffn(layer, g_fin, g_foutt):
        if not fast:
            refs.g_fin[layer] = g_fin.astype(BF16)
            refs.g_foutt[layer] = g_foutt.astype(BF16)
            return
        at, k_mid = plan.source[FF[layer]], plan.k_mid
        for m, value in enumerate((g_fin.astype(BF16), g_foutt.astype(BF16))):
            for y in range(2):
                for z in range(4):
                    rr = 2 * z + y
                    for j in range(ff // LANES):
                        first = at + (y * 4 + z) * plan.ff_rows + (m * (ff // LANES) + j) * k_mid
                        pool[first : first + k_mid] = value[
                            rr * k_mid : (rr + 1) * k_mid, j * LANES : (j + 1) * LANES
                        ]

    def emit_middle(layer, g_mid, g_out):
        if not fast:
            refs.g_mid[layer] = g_mid.astype(BF16)
            refs.g_out[layer] = g_out.astype(BF16)
            return
        at, k_mid = plan.source[MO[layer]], plan.k_mid
        for m, value in enumerate((g_mid.astype(BF16), g_out.astype(BF16))):
            for k, rr, nn_ in blocks():
                first = at + k * plan.mo_rows + m * k_mid
                pool[first : first + k_mid] = value[
                    rr * k_mid : (rr + 1) * k_mid, nn_ * LANES : (nn_ + 1) * LANES
                ]

    def emit_input(layer, g_own_rows, g_other_rows, g_edge_rows):
        if not fast:
            refs.g_in[layer, :width] = g_own_rows.astype(BF16)
            refs.g_in[layer, width : 2 * width] = g_other_rows.astype(BF16)
            refs.g_in[layer, 2 * width :] = g_edge_rows.astype(BF16)
            return
        wide[:width, :width] = g_own_rows
        wide[width : 2 * width, :width] = g_other_rows
        wide[2 * width : 2 * width + ew, :width] = g_edge_rows
        at = plan.source[IN[layer]]
        for k, rr, nn_ in blocks():
            first = at + k * plan.in_rows
            pool[first : first + plan.k_in] = wide[
                rr * plan.k_in : (rr + 1) * plan.k_in, nn_ * LANES : (nn_ + 1) * LANES
            ].astype(BF16)

    def emit_edge_all():
        at, cols = plan.source[ED], ew // 4
        long = up_to(w_in.shape[1], LANES)
        fill = LANES - 2 * cols
        for nn_ in range(4):
            span = slice(nn_ * cols, (nn_ + 1) * cols)
            tall = jnp.concatenate(
                [refs.g_eint[0, span].astype(F32), refs.g_eint[1, span].astype(F32), jnp.zeros((fill, long), F32)],
                axis=0,
            ).T
            wide[:long, nn_ * LANES : (nn_ + 1) * LANES] = tall
        for k, rr, nn_ in blocks():
            first = at + k * plan.ed_rows
            pool[first : first + plan.k_in] = wide[
                rr * plan.k_in : (rr + 1) * plan.k_in, nn_ * LANES : (nn_ + 1) * LANES
            ].astype(BF16)
        for layer in range(2):
            for nn_ in range(4):
                span = slice(nn_ * cols, (nn_ + 1) * cols)
                tall = jnp.concatenate(
                    [refs.g_ehid[layer, m, span].astype(F32) for m in range(2)]
                    + [jnp.zeros((fill, 2 * LANES), F32)],
                    axis=0,
                ).T
                wide[: 2 * LANES, nn_ * LANES : (nn_ + 1) * LANES] = tall
            for k, rr, nn_ in blocks():
                first = at + k * plan.ed_rows + plan.in_pad + layer * plan.hid_pad
                pool[first : first + plan.k_hid] = wide[
                    rr * plan.k_hid : (rr + 1) * plan.k_hid, nn_ * LANES : (nn_ + 1) * LANES
                ].astype(BF16)

    def act_at(kind, layer, slot):
        return pl.ds(aligned(plan.acts[layer] + kind * plan.act_rows + slot * width), width)

    U1, S1, S2 = 0, 1, 2
    W1, T1, W2, T2 = 0, 1, 2, 3

    def edge_act(kind, layer, base, j):
        slot = base + j if layer == 0 else slots + j
        return pl.ds(aligned(plan.edge_at + kind * plan.edge_rows + slot * ew), ew)

    def acts(kind, layer, base):
        return jnp.concatenate([pool[act_at(kind, layer, base + j)] for j in range(CHUNK)], axis=1)

    def edge_acts(kind, layer, base):
        return jnp.concatenate([pool[edge_act(kind, layer, base, j)] for j in range(CHUNK)], axis=1)

    def lanes_of(ref, base, *lead):
        return jnp.concatenate([ref[(*lead, base + j)] for j in range(CHUNK)], axis=1)

    def make_vectors():
        refs.g_vec[...] = jnp.zeros_like(refs.g_vec)
        mask_ref[...] = refs.mask[...].astype(F32)
        for layer in range(plan.layers):
            at = layer * VECTORS
            for k in range(6):
                wide[at + k : at + k + 1, :width] = refs.node_biases[k, layer : layer + 1]
            wide[at + GN1 : at + GN2 + 1, :width] = refs.node_gains[layer]
            first = pl.multiple_of(n * ff, ff)
            wide[at + FB : at + FB + 1, :ff] = refs.ffn_bias[layer : layer + 1, pl.ds(first, ff)]
            wide[at + C1 : at + C4 + 1, :ew] = refs.edge_biases[layer]
            wide[at + GE : at + GE + 1, :ew] = refs.edge_gains[layer : layer + 1]
        vec_ref[...] = wide[:LANES, :width].T

    def make_onehot():
        cells = lax.broadcasted_iota(jnp.int32, (3 * LANES, LANES), 0) + (r - 1) * LANES

        def step(s, _):
            onehot[s] = jnp.where(cells == refs.neighbors[pl.ds(s, 1), :], 1.0, 0.0).astype(BF16)
            eb[0, s] = g_edges[s].astype(BF16)
            return 0

        load_edges.wait()
        lax.fori_loop(0, slots, step, 0)

    def prepare_message(layer):
        proj[:, : 3 * LANES] = tn(w_in[layer, width : 2 * width, :], extended(layer)).astype(BF16)
        proj[:, 3 * LANES :] = w_et[layer]
        own[...] = tn(w_in[layer, :width, :], ext[layer, 1]) + vec(layer, B1)
        ubar[layer] = jnp.zeros((width, LANES), F32)

    def prepare_edge(layer):
        proj_e[:, : 3 * LANES] = nn(e_int[layer, :, width : 2 * width], extended(layer + 1)).astype(BF16)
        proj_e[:, 3 * LANES :] = e_int[layer, :, 2 * width :]
        own_e[...] = nn(e_int[layer, :, :width], ext[layer + 1, 1]) + vec(layer, C1, ew)

    def message_forward(layer, base):
        rows = jnp.concatenate([lanes_of(onehot, base), lanes_of(eb, base, layer)], axis=0)
        wide[:width, :] = nn(proj[...], rows)
        for j in range(CHUNK):
            z = wide[:width, j * LANES : (j + 1) * LANES] + own[...]
            pool[act_at(U1, layer, base + j)], pool[act_at(S1, layer, base + j)] = gelu_pair(z)
        wide[:width, :] = nn(w_midt[layer], acts(U1, layer, base))
        for j in range(CHUNK):
            z = wide[:width, j * LANES : (j + 1) * LANES] + vec(layer, B2)
            u2, pool[act_at(S2, layer, base + j)] = gelu_pair(z)
            ubar[layer] += u2.astype(F32) * mask_ref[pl.ds(base + j, 1), :]

    def edge_forward(layer, base, edge_ref, save):
        rows = jnp.concatenate([lanes_of(onehot, base), lanes_of(eb, base, layer)], axis=0)
        z = nn(proj_e[...], rows)
        for j in range(CHUNK):
            zj = z[:, j * LANES : (j + 1) * LANES] + own_e[...]
            pool[edge_act(W1, layer, base, j)], pool[edge_act(T1, layer, base, j)] = gelu_pair(zj)
        z = nn(e_hidt[layer, 0], edge_acts(W1, layer, base))
        for j in range(CHUNK):
            zj = z[:, j * LANES : (j + 1) * LANES] + vec(layer, C2, ew)
            pool[edge_act(W2, layer, base, j)], pool[edge_act(T2, layer, base, j)] = gelu_pair(zj)
        z = nn(e_hidt[layer, 1], edge_acts(W2, layer, base))
        for j in range(CHUNK):
            p = edge_ref[base + j] + z[:, j * LANES : (j + 1) * LANES] + vec(layer, C3, ew)
            hat, rstd = norm_parts(p)
            save(j, hat, rstd, p, hat * vec(layer, GE, ew) + vec(layer, C4, ew))

    def node_update(layer, before_ffn=lambda: None, beside_branch=lambda: None):
        total = all_reduce(ubar[layer])[...]
        high = total.astype(BF16)
        low = (total - high.astype(F32)).astype(BF16)
        counts = cnt_ref[...]
        sums = tn(w_out[layer], high) + tn(w_out[layer], low) + counts * vec(layer, B3)
        merged = state[layer] + sums * (1.0 / counts)
        joined_a[layer] = merged
        hat, _ = norm_parts(merged)
        hidden = hat * vec(layer, GN1) + vec(layer, SH1)
        h1b[layer] = hidden.astype(BF16)
        before_ffn()
        pre = tn(f_in[layer], h1b[layer]) + vec(layer, FB)
        act[layer], slope_f[layer] = gelu_pair(pre)
        branch = all_reduce(nn(f_outt[layer], act[layer]), beside_branch)[...]
        joined = hidden + (branch + vec(layer, B5))
        joined_c[layer] = joined
        hat, _ = norm_parts(joined)
        state[layer + 1] = hat * vec(layer, GN2) + vec(layer, SH2)
        return halo(layer + 1, state[layer + 1].astype(BF16))

    def clear_edge():
        for ref in (acc_h2, acc_h3, acc_ee, acc_t, acc_ts, acc_c):
            ref[...] = jnp.zeros_like(ref)

    def clear_message():
        for ref in (acc_mid, acc_e, acc_z, acc_zs, acc_b2):
            ref[...] = jnp.zeros_like(ref)

    def edge_backward(layer, base, parts):
        lows = []
        for j in range(CHUNK):
            hat, rstd, grad = parts(j)
            acc_c[0] += grad * hat
            acc_c[1] += grad
            dp = norm_back(hat, rstd, vec(layer, GE, ew), grad)
            g_edges[base + j] = dp
            low = dp.astype(BF16)
            acc_c[2] += low.astype(F32)
            lows.append(low)
        out = jnp.concatenate(lows, axis=1)
        acc_h3[...] += nt(out, edge_acts(W2, layer, base))
        grad_two = (nn(e_hid[layer, 1], out) * edge_acts(T2, layer, base).astype(F32)).astype(BF16)
        for j in range(CHUNK):
            acc_c[3] += grad_two[:, j * LANES : (j + 1) * LANES].astype(F32)
        acc_h2[...] += nt(grad_two, edge_acts(W1, layer, base))
        grad_one = (nn(e_hid[layer, 0], grad_two) * edge_acts(T1, layer, base).astype(F32)).astype(BF16)
        for j in range(CHUNK):
            acc_ts[...] += grad_one[:, j * LANES : (j + 1) * LANES].astype(F32)
        acc_t[...] += nt(grad_one, lanes_of(onehot, base))
        acc_ee[...] += nt(grad_one, lanes_of(eb, base, layer))
        back = nn(e_e[layer], grad_one)
        for j in range(CHUNK):
            g_edges[base + j] += back[:, j * LANES : (j + 1) * LANES]

    def edge_terms(layer):
        table = acc_t[...].astype(BF16)
        sums = acc_ts[...].astype(BF16)
        g_ext = tn(e_int[layer, :, width : 2 * width], table)
        g_own = tn(e_int[layer, :, :width], sums)
        return g_ext, g_own

    def edge_finish(layer):
        put_vec(layer, GE, acc_c[0])
        put_vec(layer, C4, acc_c[1])
        put_vec(layer, C3, acc_c[2])
        put_vec(layer, C2, acc_c[3])
        put_vec(layer, C1, acc_ts[...])
        refs.g_ehid[layer, 0, :, :ew] = acc_h2[...].astype(BF16)
        refs.g_ehid[layer, 1, :, :ew] = acc_h3[...].astype(BF16)
        table = acc_t[...].astype(BF16)
        sums = acc_ts[...].astype(BF16)
        refs.g_eint[layer, :, :width] = nt(sums, ext[layer + 1, 1]).astype(BF16)
        refs.g_eint[layer, :, width : 2 * width] = nt(table, extended(layer + 1)).astype(BF16)
        refs.g_eint[layer, :, 2 * width : 2 * width + ew] = acc_ee[...].astype(BF16)

    def message_back_two(layer, base):
        grads = []
        for j in range(CHUNK):
            s = base + j
            slope = pool[act_at(S2, layer, s)].astype(F32)
            dz = (vrow[...] * mask_ref[pl.ds(s, 1), :] * slope).astype(BF16)
            acc_b2[...] += dz.astype(F32)
            pool[act_at(S2, layer, s)] = dz
            grads.append(dz)
        acc_mid[...] += nt(acts(U1, layer, base), jnp.concatenate(grads, axis=1))

    def message_back_one(layer, base, add_edge):
        wide[:width, :] = nn(w_mid[layer], acts(S2, layer, base))
        grads = []
        for j in range(CHUNK):
            slope = pool[act_at(S1, layer, base + j)].astype(F32)
            dz = (wide[:width, j * LANES : (j + 1) * LANES] * slope).astype(BF16)
            acc_zs[...] += dz.astype(F32)
            grads.append(dz)
        grad_one = jnp.concatenate(grads, axis=1)
        acc_z[...] += nt(grad_one, lanes_of(onehot, base))
        acc_e[...] += nt(lanes_of(eb, base, layer), grad_one)
        back = nn(w_in[layer, 2 * width :, :], grad_one)
        for j in range(CHUNK):
            add_edge(base + j, back[:, j * LANES : (j + 1) * LANES])

    def middle_finish(layer):
        put_vec(layer, B2, acc_b2[...])
        emit_middle(layer, acc_mid[...], nt(ubar[layer].astype(BF16), ds_ref[...]))

    def message_terms(layer):
        table = acc_z[...].astype(BF16)
        sums = acc_zs[...].astype(BF16)
        g_ext = nn(w_in[layer, width : 2 * width, :], table)
        g_own = nn(w_in[layer, :width, :], sums)
        return g_ext, g_own

    def message_finish(layer):
        table = acc_z[...].astype(BF16)
        sums = acc_zs[...].astype(BF16)
        emit_input(layer, nt(ext[layer, 1], sums), nt(extended(layer), table), acc_e[...])
        put_vec(layer, B1, acc_zs[...])

    def node_back(layer, meanwhile=lambda: None):
        counts = cnt_ref[...]
        grad = dcur[...]
        hat, rstd = norm_parts(joined_c[layer])
        put_vec(layer, GN2, grad * hat)
        put_vec(layer, SH2, grad)
        dc = norm_back(hat, rstd, vec(layer, GN2), grad)
        dy = dc.astype(BF16)
        put_vec(layer, B5, dy.astype(F32))
        df = (tn(f_outt[layer], dy) * slope_f[layer].astype(F32)).astype(BF16)
        put_vec(layer, FB, df.astype(F32))
        part = nn(f_in[layer], df)
        total = all_reduce(part, meanwhile)
        emit_ffn(layer, nt(h1b[layer], df), nt(dy, act[layer]))
        grad = dc + total[...]
        hat, rstd = norm_parts(joined_a[layer])
        put_vec(layer, GN1, grad * hat)
        put_vec(layer, SH1, grad)
        da = norm_back(hat, rstd, vec(layer, GN1), grad)
        dcur[...] = da
        ds = (da * (1.0 / counts)).astype(BF16)
        ds_ref[...] = ds
        put_vec(layer, B3, ds.astype(F32) * counts)
        vrow[...] = nn(w_out[layer], ds)

    if fast:
        own_rows = refs.nodes.shape[0]
        mine = pl.multiple_of(n * own_rows, own_rows)
        k_mid = plan.k_mid

        def pack_in(layer):
            pool[pl.ds(my_shard(IN[layer]), plan.k_in)] = refs.msg_in[layer].astype(BF16)

        def pack_mo(layer):
            at = my_shard(MO[layer])
            pool[pl.ds(at, k_mid)] = refs.msg_mid[layer].astype(BF16)
            pool[pl.ds(aligned(at + k_mid), k_mid)] = refs.msg_out[layer].astype(BF16)

        def pack_ffn(layer):
            at = my_shard(FF[layer])
            for m, ref in enumerate((refs.ffn_in, refs.ffn_outt)):
                for j in range(ff // LANES):
                    to = aligned(at + (m * (ff // LANES) + j) * k_mid)
                    pool[pl.ds(to, k_mid)] = ref[layer, :, j * LANES : (j + 1) * LANES].astype(BF16)

        def pack_edge():
            cols = ew // 4
            for layer in range(2):
                wide[layer * cols : (layer + 1) * cols, : plan.k_in] = refs.edge_in_t[layer]
            turned = wide[:LANES, : 2 * LANES].T
            at = my_shard(ED)
            pool[pl.ds(at, plan.k_in)] = turned[: plan.k_in].astype(BF16)
            for layer in range(2):
                for m in range(2):
                    wide[: plan.k_hid, m * cols : (m + 1) * cols] = refs.edge_hidden[layer, m]
                to = aligned(at + plan.in_pad + layer * plan.hid_pad)
                pool[pl.ds(to, plan.k_hid)] = wide[: plan.k_hid, :LANES].astype(BF16)

        pack_in(0)
        pool[pl.ds(my_shard(TB), plan.tb_rows)] = refs.time_table[...].astype(BF16)
        refs.all_nodes[pl.ds(mine, own_rows)] = refs.nodes[...]
        refs.all_dnodes[pl.ds(mine, own_rows)] = refs.d_nodes[...]
        steps = jnp.zeros((1, own_rows), jnp.int32)
        for p in range(refs.time_index.shape[0]):
            steps += jnp.where(refs.protein_ids[...] == p, refs.time_index[p], 0)
        refs.all_misc[n, 0:1, :] = jnp.sum(refs.mask[...].astype(F32), axis=0, keepdims=True)
        refs.all_misc[n, 1:2, :own_rows] = steps.astype(F32)
        pl.semaphore_wait(barrier, greetings)

        node_copies, late_copies = [], []
        for k in (1, 2, 3):
            peer = (r, lax.rem(n + k, 4))
            for ref, group in (
                (refs.all_nodes.at[pl.ds(mine, own_rows)], node_copies),
                (refs.all_misc.at[n], node_copies),
                (refs.all_dnodes.at[pl.ds(mine, own_rows)], late_copies),
            ):
                group.append(remote(ref, ref, peer))
        every = range(FF1 + 1)
        gz = {item: gather_z(item) for item in every}
        gy = {item: gather_y(item) for item in every}
        gx = {item: gather_x(item) for item in FULL}
        gc = {item: gather_c(item) for item in FULL}

        def pass_on(before, after, *items):
            for item in items:
                wait(before[item])
                start(after[item])

        def first(stage, *items):
            for item in items:
                start(stage[item])

        first(gz, TB, IN0)
        start(node_copies)
        pack_mo(0)
        first(gz, MO0)
        pack_in(1)
        pack_mo(1)
        first(gz, IN1, MO1)
        pack_edge()
        first(gz, ED)
        pass_on(gz, gy, TB, IN0)
        pack_ffn(0)
        pass_on(gy, gx, TB)
        make_vectors()
        wait(node_copies)
        misc = refs.all_misc[0]
        for k in range(1, 4):
            misc += refs.all_misc[k]
        cnt_ref[...] = misc[0:1]
        steps = jnp.concatenate([refs.all_misc[k, 1:2, :own_rows] for k in range(4)], axis=1)
        times = lax.broadcasted_iota(jnp.int32, (8 * plan.k_time, LANES), 0).astype(F32)
        refs.time_hot[...] = jnp.where(times == steps, 1.0, 0.0).astype(BF16)
        nodes_t = refs.all_nodes[...].T
        pass_on(gx, gc, TB)
        pass_on(gy, gx, IN0)
        wait(gc[TB])
        for k, rr, nn_ in blocks():
            at = plan.stage[TB] + k * plan.tb_rows
            refs.time_rows[rr * plan.k_time : (rr + 1) * plan.k_time, nn_ * LANES : (nn_ + 1) * LANES] = pool[
                at : at + plan.tb_rows
            ]
        state[0] = nodes_t + tn(refs.time_rows[...], refs.time_hot[...])
        finish = halo(0, state[0].astype(BF16))
        pass_on(gz, gy, MO0)
        first(gz, FF0)
        make_onehot()
        pass_on(gy, gx, MO0)
        pass_on(gz, gy, IN1, MO1)
        pack_ffn(1)
        pass_on(gx, gc, IN0)
        wait(gc[IN0])
        assemble_in(0)
        pass_on(gx, gc, MO0)
        pass_on(gy, gx, IN1, MO1)
        pass_on(gz, gy, ED)
        first(gz, FF1)
        wait(gc[MO0])
        assemble_mo(0)
        finish()
        pass_on(gy, gx, ED)
    else:
        make_vectors()
        make_onehot()
        pl.semaphore_wait(barrier, greetings)
        state[0] = refs.h0[...]
        halo(0, state[0].astype(BF16))()

    prepare_message(0)

    def loop_a(i, _):
        message_forward(0, i * CHUNK)
        if fast:

            @pl.when(i == 1)
            def _():
                pass_on(gz, gy, FF0)

        return 0

    lax.fori_loop(0, chunks, loop_a, 0)

    def need_ffn0():
        if fast:
            pass_on(gx, gc, IN1, MO1)
            wait(gy[FF0])
            assemble_ffn(0)

    def beside_branch():
        if fast:
            wait(gc[IN1])
            assemble_in(1)

    finish = node_update(0, need_ffn0, beside_branch)
    if fast:
        start(late_copies)
        pass_on(gx, gc, ED)
        wait(gc[MO1])
        assemble_mo(1)
        wait(gc[ED])
        assemble_edge()
    finish()
    prepare_edge(0)
    if fast:
        pass_on(gz, gy, FF1)
    prepare_message(1)

    def loop_b(i, _):
        base = i * CHUNK

        def save(j, hat, rstd, p, value):
            psum[base + j] = p
            edges_out[base + j] = value
            eb[1, base + j] = value.astype(BF16)

        edge_forward(0, base, g_edges, save)
        message_forward(1, base)
        return 0

    lax.fori_loop(0, chunks, loop_b, 0)
    load_grads = pltpu.make_async_copy(refs.d_edges, g_edges, refs.local_sem.at[1])
    load_grads.start()

    def need_ffn1():
        if fast:
            wait(late_copies)
            wait(gy[FF1])
            assemble_ffn(1)

    finish = node_update(1, need_ffn1)
    if fast:
        refs.all_nodes[...] = state[2].T
        nodes_out[...] = refs.all_nodes[pl.ds(mine, own_rows)]
    else:
        nodes_out[...] = state[2].T
    clear_edge()
    load_grads.wait()
    finish()
    prepare_edge(1)

    def loop_c(i, _):
        base = i * CHUNK
        kept = {}

        def save(j, hat, rstd, p, value):
            edges_out[base + j] = value
            kept[j] = (hat, rstd)

        edge_forward(1, base, edges_out, save)
        edge_backward(1, base, lambda j: (*kept[j], g_edges[base + j]))
        return 0

    lax.fori_loop(0, chunks, loop_c, 0)
    save_edges = pltpu.make_async_copy(edges_out, refs.edges_out, refs.local_sem.at[2])
    save_edges.start()
    g_ext, g_own = edge_terms(1)
    dh = refs.all_dnodes[...].T if fast else refs.dh[...]
    dcur[...] = dh + halo_back(0, g_ext, g_own, beside_far=lambda: edge_finish(1))[...]
    node_back(1)
    clear_message()
    clear_edge()
    reduce_c, reduce_x, reduce_y, reduce_last = {}, {}, {}, {}
    if fast:
        for item in range(FF1 + 1):
            if item in FULL:
                reduce_c[item] = reduce_pairs(item, BY_CORE)
                reduce_x[item] = reduce_pairs(item, BY_X)
            reduce_y[item] = reduce_pairs(item, BY_Y)
            reduce_last[item] = reduce_z(item)

    def reduce_on(before, after, *items):
        for item in items:
            wait(before[item][0])
            before[item][1]()
            start(after[item][0])

    def put_ffn(layer):
        copies, total = reduce_last[FF[layer]]
        wait(copies)
        k_mid, parts = plan.k_mid, ff // LANES
        for m, ref in enumerate((refs.o_fin, refs.o_foutt)):
            for j in range(parts):
                ref[layer, :, j * LANES : (j + 1) * LANES] = total((m * parts + j) * k_mid, k_mid)

    def put_message(layer):
        copies, total = reduce_last[IN[layer]]
        wait(copies)
        refs.o_in[layer] = total(0, plan.k_in)
        copies, total = reduce_last[MO[layer]]
        wait(copies)
        refs.o_mid[layer] = total(0, plan.k_mid)
        refs.o_out[layer] = total(plan.k_mid, plan.k_mid)

    def put_edge():
        copies, total = reduce_last[ED]
        wait(copies)
        cols = ew // 4
        wide[: plan.in_pad, :LANES] = total(0, plan.in_pad)
        turned = wide[: 2 * LANES, :LANES].T
        hidden = total(plan.in_pad, 2 * plan.hid_pad)
        for layer in range(2):
            refs.o_edge[layer] = turned[layer * cols : (layer + 1) * cols, : plan.k_in]
            first = layer * plan.hid_pad
            for m in range(2):
                refs.o_hid[layer, m] = hidden[first : first + plan.k_hid, m * cols : (m + 1) * cols]

    if fast:
        start(reduce_y[FF1][0])

    def loop_d1(i, _):
        base = i * CHUNK

        def add_edge(s, value):
            g_edges[s] += value

        message_back_two(1, base)
        message_back_one(1, base, add_edge)
        return 0

    lax.fori_loop(0, chunks, loop_d1, 0)
    middle_finish(1)
    message_finish(1)
    m_ext, m_own = message_terms(1)
    acc_z[...] = m_ext
    acc_zs[...] = m_own
    if fast:
        start(reduce_c[IN1][0])
        start(reduce_c[MO1][0])

    def loop_d2(i, _):
        base = i * CHUNK
        edge_backward(0, base, lambda j: (*norm_parts(psum[base + j]), g_edges[base + j]))
        if fast:

            @pl.when(i == 1)
            def _():
                reduce_on(reduce_c, reduce_x, IN1)

        return 0

    lax.fori_loop(0, chunks, loop_d2, 0)
    e_ext, e_own = edge_terms(0)

    def beside_edge():
        if fast:
            reduce_on(reduce_c, reduce_x, MO1)
            reduce_on(reduce_y, reduce_last, FF1)
        edge_finish(0)
        if fast:
            emit_edge_all()
            reduce_on(reduce_x, reduce_y, IN1)

    dcur[...] += halo_back(1, acc_z[...] + e_ext, acc_zs[...] + e_own, beside_far=beside_edge)[...]

    def beside_node():
        if fast:
            start(reduce_c[ED][0])
            reduce_on(reduce_x, reduce_y, MO1)
            reduce_on(reduce_y, reduce_last, IN1)

    node_back(0, beside_node)
    clear_message()
    if fast:
        start(reduce_y[FF0][0])
        reduce_on(reduce_c, reduce_x, ED)

    def loop_e1(i, _):
        message_back_two(0, i * CHUNK)
        return 0

    lax.fori_loop(0, chunks, loop_e1, 0)
    middle_finish(0)
    if fast:
        start(reduce_c[MO0][0])
        reduce_on(reduce_y, reduce_last, MO1)

    def loop_e2(i, _):
        base = i * CHUNK

        def add_edge(s, value):
            g_edges[s] += value

        message_back_one(0, base, add_edge)
        if fast:

            @pl.when(i == 0)
            def _():
                reduce_on(reduce_c, reduce_x, MO0)

        return 0

    lax.fori_loop(0, chunks, loop_e2, 0)
    save_grads = pltpu.make_async_copy(g_edges, refs.g_edges, refs.local_sem.at[3])
    save_grads.start()
    m_ext, m_own = message_terms(0)
    if not fast:
        message_finish(0)
        final = dcur[...] + halo_back(2, m_ext, m_own)[...]
        g_nodes[...] = final.T
        save_edges.wait()
        save_grads.wait()
        return

    def beside_last_core():
        message_finish(0)
        start(reduce_c[IN0][0])

    sums = refs.vec_sums
    partners = [(r, buddy), (r, across), y_peer]
    partners += [(2 * (zz + 1 - 2 * lax.rem(zz, 2)) + yy, n), (2 * lax.rem(zz + 2, 4) + yy, n)]
    rounds = [remote(sums.at[2 * k], sums.at[2 * k + 1], partners[k]) for k in range(5)]

    def vec_round(k):
        rounds[k].wait()
        sums[2 * k + 2] = sums[2 * k] + sums[2 * k + 1]
        if k < 4:
            rounds[k + 1].start()

    def beside_last_far():
        table = refs.g_vec[...].T
        sums[0] = jnp.zeros_like(sums[0])
        for layer in range(2):
            for which, row in VEC_ROWS.items():
                value = table[layer * VECTORS + which : layer * VECTORS + which + 1]
                at = layer * VEC_PER_LAYER + row
                if which == FB:
                    sums[0, pl.ds(at + n, 1)] = value
                else:
                    scale = 1.0 / plan.nbr_total if B3 <= which <= GN2 else 1.0
                    sums[0, at : at + 1] = value * scale
        rounds[0].start()
        reduce_on(reduce_c, reduce_x, IN0)
        reduce_on(reduce_y, reduce_last, FF0)
        reduce_on(reduce_x, reduce_y, MO0, ED)
        vec_round(0)
        put_ffn(1)
        put_message(1)

    final = dcur[...] + halo_back(2, m_ext, m_own, beside_last_core, beside_last_far)[...]
    high = final.astype(BF16)
    low = (final - high.astype(F32)).astype(BF16)
    g_times = (nt(refs.time_hot[...], high) + nt(refs.time_hot[...], low)) * (1.0 / plan.nbr_total)
    for k, rr, nn_ in blocks():
        at = plan.source[TB] + k * plan.tb_rows
        pool[at : at + plan.tb_rows] = g_times[
            rr * plan.k_time : (rr + 1) * plan.k_time, nn_ * LANES : (nn_ + 1) * LANES
        ].astype(BF16)
    start(reduce_c[TB][0])
    vec_round(1)
    reduce_on(reduce_x, reduce_y, IN0)
    reduce_on(reduce_c, reduce_x, TB)
    refs.all_dnodes[...] = final.T
    g_nodes[...] = refs.all_dnodes[pl.ds(mine, own_rows)]
    reduce_on(reduce_y, reduce_last, MO0)
    vec_round(2)
    reduce_on(reduce_x, reduce_y, TB)
    reduce_on(reduce_y, reduce_last, IN0, ED)
    vec_round(3)
    put_ffn(0)
    reduce_on(reduce_y, reduce_last, TB)
    vec_round(4)
    for layer in range(2):
        at = layer * VEC_PER_LAYER
        for k in range(6):
            refs.o_node_biases[k, layer : layer + 1] = sums[10, at + k : at + k + 1]
        refs.o_node_gains[layer] = sums[10, at + VEC_ROWS[GN1] : at + VEC_ROWS[GN2] + 1]
        for k in range(4):
            first = at + VEC_ROWS[FB] + k
            refs.o_ffn_bias[layer : layer + 1, k * ff : (k + 1) * ff] = sums[10, first : first + 1, :ff]
        first = at + VEC_ROWS[C1]
        refs.o_edge_biases[layer] = sums[10, first : first + 4, :ew]
        refs.o_edge_gains[layer : layer + 1] = sums[10, first + 4 : first + 5, :ew]
    put_message(0)
    put_edge()
    copies, total = reduce_last[TB]
    wait(copies)
    refs.o_time[...] = total(0, plan.tb_rows)
    save_edges.wait()
    save_grads.wait()


def vmem(shape, dtype):
    return pltpu.VMEM(shape, dtype)


def run_whole(plan, operands):
    lanes, slots, width, ew, ff, layers = LANES, plan.slots, plan.width, plan.ew, plan.ff, plan.layers
    rows_in = 2 * width + ew
    node_rows = lanes // plan.nbr_total if plan.fast else lanes
    outs = dict(
        nodes_out=((node_rows, width), F32),
        edges_out=((slots, ew, lanes), F32),
        g_nodes=((node_rows, width), F32),
        g_edges=((slots, ew, lanes), F32),
    )
    scratch = dict(
        onehot=vmem((slots, 3 * lanes, lanes), BF16),
        eb=vmem((layers, slots, ew, lanes), BF16),
        pool=vmem((plan.pool_rows, lanes), BF16),
        psum=vmem((slots, ew, lanes), F32),
        proj=vmem((width, 3 * lanes + ew), BF16),
        proj_e=vmem((ew, 3 * lanes + ew), BF16),
        own=vmem((width, lanes), F32),
        own_e=vmem((ew, lanes), F32),
        state=vmem((3, width, lanes), F32),
        ext=vmem((3, 3, width, lanes), BF16),
        joined_a=vmem((layers, width, lanes), F32),
        joined_c=vmem((layers, width, lanes), F32),
        h1b=vmem((layers, width, lanes), BF16),
        act=vmem((layers, ff, lanes), BF16),
        slope_f=vmem((layers, ff, lanes), BF16),
        ubar=vmem((layers, width, lanes), F32),
        ds=vmem((width, lanes), BF16),
        acc_mid=vmem((width, width), F32),
        acc_e=vmem((ew, width), F32),
        acc_z=vmem((width, 3 * lanes), F32),
        acc_zs=vmem((width, lanes), F32),
        acc_b2=vmem((width, lanes), F32),
        acc_h2=vmem((ew, ew), F32),
        acc_h3=vmem((ew, ew), F32),
        acc_ee=vmem((ew, ew), F32),
        acc_t=vmem((ew, 3 * lanes), F32),
        acc_ts=vmem((ew, lanes), F32),
        acc_c=vmem((4, ew, lanes), F32),
        wide=vmem((up_to(rows_in, lanes), CHUNK * lanes), F32),
        vrow=vmem((width, lanes), F32),
        dcur=vmem((width, lanes), F32),
        g_part=vmem((3, width, lanes), F32),
        halo_send=vmem((3, width // 2, lanes), BF16),
        halo_core=vmem((3, width // 2, lanes), BF16),
        halo_half=vmem((3, width // 2, lanes), BF16),
        halo_x=vmem((width // 2, lanes), BF16),
        halo_recv=vmem((3, 4, width // 2, lanes), BF16),
        ar_part=vmem((2, width, lanes), F32),
        ar_one=vmem((2, width // 2, lanes), F32),
        ar_two=vmem((2, width // 2, lanes), BF16),
        ar_three=vmem((2, width // 2, lanes), BF16),
        mask_rows=vmem((slots, lanes), F32),
        vectors=vmem((width, lanes), F32),
        ar_tot=vmem((2, width, lanes), F32),
        send_sem=pltpu.SemaphoreType.DMA((160,)),
        recv_sem=pltpu.SemaphoreType.DMA((160,)),
        local_sem=pltpu.SemaphoreType.DMA((4,)),
        edge_state=vmem((slots, ew, lanes), F32),
        edge_grad=vmem((slots, ew, lanes), F32),
    )
    kept = dict(
        g_eint=((layers, ew, up_to(rows_in, lanes)), BF16),
        g_ehid=((layers, 2, ew, 2 * lanes), BF16),
        g_vec=((width, lanes), F32),
    )
    if plan.fast:
        scratch.update({name: vmem(*spec) for name, spec in kept.items()})
        own_rows = lanes // plan.nbr_total
        scratch.update(
            dict(
                counts=vmem((1, lanes), F32),
                all_nodes=vmem((lanes, width), F32),
                all_dnodes=vmem((lanes, width), F32),
                all_misc=vmem((plan.nbr_total, 8, lanes), F32),
                time_hot=vmem((8 * plan.k_time, lanes), BF16),
                time_rows=vmem((8 * plan.k_time, width), BF16),
                vec_sums=vmem((11, layers * VEC_PER_LAYER, width), F32),
                w_in=vmem((layers, rows_in, width), BF16),
                w_et=vmem((layers, width, ew), BF16),
                w_mid=vmem((layers, width, width), BF16),
                w_midt=vmem((layers, width, width), BF16),
                w_out=vmem((layers, width, width), BF16),
                f_in=vmem((layers, width, ff), BF16),
                f_outt=vmem((layers, width, ff), BF16),
                e_int=vmem((layers, ew, rows_in), BF16),
                e_e=vmem((layers, ew, ew), BF16),
                e_hid=vmem((layers, 2, ew, ew), BF16),
                e_hidt=vmem((layers, 2, ew, ew), BF16),
            )
        )
        outs.update(
            dict(
                o_in=((layers, plan.k_in, lanes), F32),
                o_mid=((layers, plan.k_mid, lanes), F32),
                o_out=((layers, plan.k_mid, lanes), F32),
                o_fin=((layers, plan.k_mid, ff), F32),
                o_foutt=((layers, plan.k_mid, ff), F32),
                o_edge=((layers, ew // 4, plan.k_in), F32),
                o_hid=((layers, 2, plan.k_hid, ew // 4), F32),
                o_time=((plan.tb_rows, lanes), F32),
                o_node_biases=((6, layers, width), F32),
                o_node_gains=((layers, 2, width), F32),
                o_ffn_bias=((layers, 4 * ff), F32),
                o_edge_gains=((layers, ew), F32),
                o_edge_biases=((layers, 4, ew), F32),
            )
        )
    else:
        outs.update(
            dict(
                g_in=((layers, rows_in, width), BF16),
                g_mid=((layers, width, width), BF16),
                g_out=((layers, width, width), BF16),
                g_fin=((layers, width, ff), BF16),
                g_foutt=((layers, width, ff), BF16),
                **kept,
            )
        )
    names = (*operands, *outs, *scratch)
    in_hbm, in_smem = dict(edges=1, d_edges=1, edges_out=1, g_edges=1), dict(time_index=1)
    place = lambda name: pl.BlockSpec(
        memory_space=pl.ANY if name in in_hbm else pltpu.SMEM if name in in_smem else pltpu.VMEM
    )
    results = pl.pallas_call(
        functools.partial(whole_kernel, plan, names),
        out_shape=tuple(jax.ShapeDtypeStruct(*spec) for spec in outs.values()),
        in_specs=[place(name) for name in operands],
        out_specs=[place(name) for name in outs],
        scratch_shapes=list(scratch.values()),
        compiler_params=pltpu.CompilerParams(
            collective_id=1, has_side_effects=True, vmem_limit_bytes=63 * 1024 * 1024
        ),
    )(*operands.values())
    return Refs(outs, results)


def hand_over(values):
    count = len(values)

    def kernel(*refs):
        sources, results, held = refs[:count], refs[count : 2 * count], refs[2 * count : 3 * count]
        come, go = refs[3 * count :]
        arriving = [pltpu.make_async_copy(sources[k], held[k], come.at[k]) for k in range(count)]
        leaving = [pltpu.make_async_copy(held[k], results[k], go.at[k]) for k in range(count)]
        for copy in arriving:
            copy.start()
        for first, second in zip(arriving, leaving, strict=True):
            first.wait()
            second.start()
        for copy in leaving:
            copy.wait()

    specs = [pl.BlockSpec(memory_space=pl.ANY)] * count
    return pl.pallas_call(
        kernel,
        out_shape=[jax.ShapeDtypeStruct(value.shape, value.dtype) for value in values],
        in_specs=specs,
        out_specs=specs,
        scratch_shapes=[
            *(pltpu.VMEM(value.shape, value.dtype) for value in values),
            pltpu.SemaphoreType.DMA((count,)),
            pltpu.SemaphoreType.DMA((count,)),
        ],
    )(*values)


def gather_all(value, res_dim, nbr_dim):
    value = lax.all_gather(value, "res", axis=res_dim, tiled=True)
    return lax.all_gather(value, "nbr", axis=nbr_dim, tiled=True)


def scatter_sum(value, res_dim, nbr_dim):
    value = lax.psum_scatter(value, "res", scatter_dimension=res_dim, tiled=True)
    return lax.psum_scatter(value, "nbr", scatter_dimension=nbr_dim, tiled=True).astype(F32)


def low(value):
    return value.astype(BF16)


def per_device(
    nodes,
    edges,
    protein_ids,
    time_index,
    neighbors,
    edge_mask,
    time_table,
    msg_in,
    msg_mid,
    msg_out,
    ffn_in,
    ffn_out,
    edge_in,
    edge_hidden,
    node_gains,
    node_biases,
    ffn_bias,
    edge_gains,
    edge_biases,
    d_nodes,
    d_edges,
):
    res_total, nbr_total = lax.axis_size("res"), lax.axis_size("nbr")
    own_rows, width = nodes.shape
    ew = edges.shape[2]
    row_count, slot_count = neighbors.shape
    layers = msg_in.shape[0]
    n_at = lax.axis_index("nbr")
    ff = ffn_bias.shape[1] // nbr_total
    shards = (msg_in.shape[1], msg_mid.shape[1], edge_hidden.shape[2], time_table.shape[0])
    plan = Plan(res_total, nbr_total, slot_count, width, ew, ff, layers, shards)

    operands = dict(
        neighbors=neighbors.T,
        mask=edge_mask.T,
        edges=jnp.transpose(edges, (1, 2, 0)),
        d_edges=jnp.transpose(d_edges, (1, 2, 0)),
        node_biases=jnp.swapaxes(node_biases, 0, 1),
        node_gains=node_gains,
        ffn_bias=ffn_bias,
        edge_gains=edge_gains,
        edge_biases=edge_biases,
    )
    if plan.fast:
        operands.update(
            nodes=nodes,
            d_nodes=d_nodes,
            protein_ids=protein_ids[None, :],
            time_index=time_index,
            msg_in=msg_in,
            msg_mid=msg_mid,
            msg_out=msg_out,
            ffn_in=ffn_in,
            ffn_outt=jnp.swapaxes(ffn_out, 1, 2),
            edge_in_t=jnp.swapaxes(edge_in, 1, 2),
            edge_hidden=edge_hidden,
            time_table=time_table,
        )
        out = run_whole(plan, operands)
        (
            nodes_out, edges_out, g_nodes, g_edges, g_time, g_in, g_mid, g_out, g_fin, g_foutt, g_edge_t,
            g_hid, g_gains, g_biases, g_ffn_bias, g_edge_gains, g_edge_biases,
        ) = hand_over(
            [
                out.nodes_out, out.edges_out, out.g_nodes, out.g_edges, out.o_time, out.o_in, out.o_mid,
                out.o_out, out.o_fin, out.o_foutt, out.o_edge, out.o_hid, out.o_node_gains,
                out.o_node_biases, out.o_ffn_bias, out.o_edge_gains, out.o_edge_biases,
            ]
        )
        return (
            nodes_out,
            jnp.transpose(edges_out, (2, 0, 1)),
            g_nodes,
            jnp.transpose(g_edges, (2, 0, 1)),
            g_time,
            g_in,
            g_mid,
            g_out,
            g_fin,
            jnp.swapaxes(g_foutt, 1, 2),
            jnp.swapaxes(g_edge_t, 1, 2),
            g_hid,
            g_gains,
            jnp.swapaxes(g_biases, 0, 1),
            g_ffn_bias,
            g_edge_gains,
            g_edge_biases,
        )

    count_row = jnp.sum(edge_mask.astype(F32), axis=1)
    matches = protein_ids[:, None] == jnp.arange(time_index.shape[0], dtype=jnp.int32)[None, :]
    step_rows = jnp.sum(jnp.where(matches, time_index[None, :], 0), axis=1)
    mine = lambda a: lax.dynamic_slice_in_dim(a, n_at * own_rows, own_rows, axis=0)
    node_vectors = lambda rows: (rows[:, : SH2 + 1], rows[:, GN1 : GN2 + 1])
    table_low = gather_all(low(time_table), 0, 1)
    w_in = gather_all(low(msg_in), 1, 2)
    w_mid = gather_all(low(msg_mid), 1, 2)
    e_in = gather_all(low(edge_in), 1, 2)
    e_hid = gather_all(low(edge_hidden), 2, 3)
    step_onehot = (
        step_rows[:, None] == jnp.arange(table_low.shape[0], dtype=jnp.int32)[None, :]
    ).astype(BF16)
    state = nodes + jnp.dot(step_onehot, table_low, preferred_element_type=F32)
    count_block = jnp.zeros((8, width), F32).at[0, :row_count].set(count_row)
    packed = lax.all_gather(jnp.concatenate([state, d_nodes, count_block], axis=0), "nbr", axis=0)
    operands.update(
        dict(
            h0=packed[:, :own_rows].reshape(row_count, width).T,
            dh=packed[:, own_rows : 2 * own_rows].reshape(row_count, width).T,
            counts=jnp.sum(packed[:, 2 * own_rows, :row_count], axis=0)[None, :],
            w_in=w_in,
            w_et=jnp.swapaxes(w_in[:, 2 * width :], 1, 2),
            w_mid=w_mid,
            w_midt=jnp.swapaxes(w_mid, 1, 2),
            w_out=gather_all(low(msg_out), 1, 2),
            f_in=lax.all_gather(low(ffn_in), "res", axis=1, tiled=True),
            f_outt=lax.all_gather(jnp.swapaxes(low(ffn_out), 1, 2), "res", axis=1, tiled=True),
            e_int=jnp.swapaxes(e_in, 1, 2),
            e_e=e_in[:, 2 * width :],
            e_hid=e_hid,
            e_hidt=jnp.swapaxes(e_hid, 2, 3),
        )
    )
    out = run_whole(plan, operands)
    g_nodes = mine(out.g_nodes)
    g_table_full = lax.dot_general(
        step_onehot.astype(F32),
        g_nodes,
        (((0,), (0,)), ((), ())),
        precision=lax.Precision.HIGHEST,
        preferred_element_type=F32,
    )
    rows = out.g_vec.T[: layers * VECTORS].reshape(layers, VECTORS, width)
    shared = rows[:, B3 : GN2 + 1] * (1.0 / nbr_total)
    g_bias_ffn = lax.dynamic_update_slice_in_dim(
        jnp.zeros_like(ffn_bias), rows[:, FB, :ff], n_at * ff, axis=1
    )
    vectors, g_ffn_bias, g_edge_biases, g_edge_gains = lax.psum(
        (
            jnp.concatenate([rows[:, :B3], shared], axis=1),
            g_bias_ffn,
            rows[:, C1 : C4 + 1, :ew],
            rows[:, GE, :ew],
        ),
        ("res", "nbr"),
    )
    g_node_biases, g_node_gains = node_vectors(vectors)
    scatter_res = lambda a: lax.psum_scatter(a, "res", scatter_dimension=1, tiled=True).astype(F32)
    return (
        mine(out.nodes_out),
        jnp.transpose(out.edges_out, (2, 0, 1)),
        g_nodes,
        jnp.transpose(out.g_edges, (2, 0, 1)),
        scatter_sum(low(g_table_full), 0, 1),
        scatter_sum(out.g_in, 1, 2),
        scatter_sum(out.g_mid, 1, 2),
        scatter_sum(out.g_out, 1, 2),
        scatter_res(out.g_fin),
        jnp.swapaxes(scatter_res(out.g_foutt), 1, 2),
        jnp.swapaxes(scatter_sum(out.g_eint[:, :, : 2 * width + ew], 2, 1), 1, 2),
        scatter_sum(jnp.swapaxes(out.g_ehid[..., :ew], 2, 3), 2, 3),
        g_node_gains,
        g_node_biases,
        g_ffn_bias,
        g_edge_gains,
        g_edge_biases,
    )


def solution(mesh):
    return jax.shard_map(
        per_device,
        mesh=mesh,
        in_specs=(
            P(("res", "nbr"), None),
            P("res", "nbr", None),
            P(("res", "nbr")),
            P(),
            P("res", "nbr"),
            P("res", "nbr"),
            P("res", "nbr"),
            P(None, "res", "nbr"),
            P(None, "res", "nbr"),
            P(None, "res", "nbr"),
            P(None, "res", "nbr"),
            P(None, "nbr", "res"),
            P(None, "res", "nbr"),
            P(None, None, "res", "nbr"),
            P(),
            P(),
            P(),
            P(),
            P(),
            P(("res", "nbr"), None),
            P("res", "nbr", None),
        ),
        out_specs=(
            P(("res", "nbr"), None),
            P("res", "nbr", None),
            P(("res", "nbr"), None),
            P("res", "nbr", None),
            P("res", "nbr"),
            P(None, "res", "nbr"),
            P(None, "res", "nbr"),
            P(None, "res", "nbr"),
            P(None, "res", "nbr"),
            P(None, "nbr", "res"),
            P(None, "res", "nbr"),
            P(None, None, "res", "nbr"),
            P(),
            P(),
            P(),
            P(),
            P(),
        ),
        check_vma=False,
    )
```

```python
import functools

import jax
import jax.numpy as jnp
from jax import lax
from jax.experimental import pallas as pl
from jax.experimental.pallas import tpu as pltpu
from jax.sharding import PartitionSpec as P

NORM_EPS = 1e-05
F32 = jnp.float32
BF16 = jnp.bfloat16
MESH = pl.DeviceIdType.MESH
LANES = 128
CHUNK = 5
TANH_A = 0.7978845608028654
TANH_B = 0.044715
B1, B2, B3, B5, SH1, SH2, GN1, GN2, FB, C1, C2, C3, C4, GE = range(14)
VECTORS = 14
VEC_ROWS = {B1: 0, B2: 1, B3: 2, B5: 3, SH1: 4, SH2: 5, GN1: 6, GN2: 7, FB: 8, C1: 12, C2: 13, C3: 14, C4: 15, GE: 16}
VEC_PER_LAYER = 20
IN0, TB, MO0, FF0, ED, IN1, MO1, FF1 = range(8)
IN, MO, FF = (IN0, IN1), (MO0, MO1), (FF0, FF1)
BY_CORE, BY_X, BY_Y, BY_Z = range(4)


def nn(left, right):
    return jnp.dot(left, right, preferred_element_type=F32)


def nt(left, right):
    return lax.dot_general(left, right, (((1,), (1,)), ((), ())), preferred_element_type=F32)


def tn(left, right):
    return lax.dot_general(left, right, (((0,), (0,)), ((), ())), preferred_element_type=F32)


def gelu_pair(z):
    sq = z * z
    half = 0.5 + 0.5 * jnp.tanh(z * (TANH_A + (TANH_A * TANH_B) * sq))
    value = z * half
    slope = half + (value * (1.0 - half)) * (2.0 * TANH_A + (6.0 * TANH_A * TANH_B) * sq)
    return value.astype(BF16), slope.astype(BF16)


def norm_parts(value):
    scale = 1.0 / value.shape[0]
    centre = jnp.sum(value, axis=0, keepdims=True) * scale
    offset = value - centre
    spread = jnp.sum(offset * offset, axis=0, keepdims=True) * scale
    rstd = lax.rsqrt(spread + NORM_EPS)
    return offset * rstd, rstd


def norm_back(hat, rstd, gain, grad):
    scale = 1.0 / hat.shape[0]
    weighted = grad * gain
    first = jnp.sum(weighted, axis=0, keepdims=True) * scale
    second = jnp.sum(weighted * hat, axis=0, keepdims=True) * scale
    return rstd * (weighted - first - hat * second)


class Refs:
    def __init__(self, names, values):
        self.__dict__.update(zip(names, values, strict=True))


def up_to(value, step):
    return (value + step - 1) // step * step


class Plan:
    def __init__(self, res_total, nbr_total, slots, width, ew, ff, layers, shards):
        self.res_total, self.nbr_total = res_total, nbr_total
        self.slots, self.width, self.ew, self.ff, self.layers = slots, width, ew, ff, layers
        self.k_in, self.k_mid, self.k_hid, self.k_time = shards
        self.fast = (res_total, nbr_total) == (8, 4) and self.k_in % 8 == 0 and self.k_mid % 16 == 0
        acts = slots * width
        self.acts = [0, 3 * acts]
        self.act_rows = acts
        edge_rows = (slots + CHUNK) * ew
        self.pool_rows = 6 * acts + 4 * edge_rows
        self.edge_at = 6 * acts
        self.edge_rows = edge_rows
        if not self.fast:
            return
        self.in_pad = up_to(self.k_in, 16)
        self.hid_pad = up_to(self.k_hid, 16)
        self.in_rows = self.in_pad
        self.mo_rows = 2 * self.k_mid
        self.ed_rows = self.in_pad + 2 * self.hid_pad
        self.tb_rows = self.k_time
        self.ff_rows = 2 * self.k_mid * (ff // LANES)
        one = 3 * acts
        sizes = {IN0: self.in_rows, MO0: self.mo_rows, ED: self.ed_rows, IN1: self.in_rows,
                 MO1: self.mo_rows, TB: self.tb_rows, FF0: self.ff_rows, FF1: self.ff_rows}
        self.sizes = sizes
        self.stage = {}
        at = 0
        for item in (IN0, TB, MO0):
            self.stage[item] = at
            at += 32 * sizes[item]
        at = one
        for item in (IN1, MO1, ED):
            self.stage[item] = at
            at += 32 * sizes[item]
        top = at
        at = 2 * one
        for item in (FF0, FF1):
            self.stage[item] = at
            at += 8 * sizes[item]
        top = max(top, at)
        self.source, self.recv = {}, {}
        at = 0
        for item in (MO0, IN0):
            self.source[item] = at
            at += 32 * sizes[item]
        at = one
        for item in (IN1, MO1, ED):
            self.source[item] = at
            at += 32 * sizes[item]
        for stage, count in ((BY_CORE, 16), (BY_X, 8), (BY_Y, 4)):
            self.recv[ED, stage] = at
            at += count * sizes[ED]
        at = max(at, 2 * one)
        self.source[FF1] = at
        self.recv[FF1, BY_Y] = at + 8 * sizes[FF1]
        at += 12 * sizes[FF1]
        for stage, count in ((BY_CORE, 16), (BY_X, 8), (BY_Y, 4)):
            for item in (IN1, MO1):
                self.recv[item, stage] = at
                at += count * sizes[item]
        self.recv[IN0, BY_CORE], self.recv[MO0, BY_CORE] = self.recv[IN1, BY_CORE], self.recv[MO1, BY_CORE]
        top = max(top, at)
        self.edge_at = top
        self.source[FF0] = top
        self.recv[FF0, BY_Y] = top + 8 * sizes[FF0]
        at = top + 12 * sizes[FF0]
        for stage, count in ((BY_X, 8), (BY_Y, 4)):
            for item in (IN0, MO0):
                self.recv[item, stage] = at
                at += count * sizes[item]
        at = max(at, top + 4 * edge_rows)
        self.source[TB] = at
        at += 32 * sizes[TB]
        for stage, count in ((BY_CORE, 16), (BY_X, 8), (BY_Y, 4)):
            self.recv[TB, stage] = at
            at += count * sizes[TB]
        for item in sizes:
            self.recv[item, BY_Z] = at
            at += 3 * sizes[item]
        self.pool_rows = at


def whole_kernel(plan, names, *values):
    refs = Refs(names, values)
    fast = plan.fast
    mask_ref, vec_ref = refs.mask_rows, refs.vectors
    onehot, eb, pool, psum, proj, proj_e = refs.onehot, refs.eb, refs.pool, refs.psum, refs.proj, refs.proj_e
    own, own_e, state, ext = refs.own, refs.own_e, refs.state, refs.ext
    joined_a, joined_c, h1b, act = refs.joined_a, refs.joined_c, refs.h1b, refs.act
    slope_f, ubar, ds_ref = refs.slope_f, refs.ubar, refs.ds
    acc_mid, acc_e, acc_z, acc_zs, acc_b2 = refs.acc_mid, refs.acc_e, refs.acc_z, refs.acc_zs, refs.acc_b2
    acc_h2, acc_h3, acc_ee = refs.acc_h2, refs.acc_h3, refs.acc_ee
    acc_t, acc_ts, acc_c = refs.acc_t, refs.acc_ts, refs.acc_c
    wide, vrow, dcur, g_part = refs.wide, refs.vrow, refs.dcur, refs.g_part
    halo_send, halo_recv = refs.halo_send, refs.halo_recv
    ar_part, ar_one, ar_two, ar_three = refs.ar_part, refs.ar_one, refs.ar_two, refs.ar_three
    ar_tot = refs.ar_tot
    w_in, w_et, w_mid, w_midt, w_out = refs.w_in, refs.w_et, refs.w_mid, refs.w_midt, refs.w_out
    f_in, f_outt, e_int, e_e = refs.f_in, refs.f_outt, refs.e_int, refs.e_e
    e_hid, e_hidt = refs.e_hid, refs.e_hidt
    nodes_out, g_nodes = refs.nodes_out, refs.g_nodes
    edges_out, g_edges = refs.edge_state, refs.edge_grad
    cnt_ref = refs.counts
    res_total = plan.res_total
    slots, width, ew, ff = plan.slots, plan.width, plan.ew, plan.ff
    r = lax.axis_index("res")
    n = lax.axis_index("nbr")
    core = lax.rem(n, 2)
    xx = n // 2
    yy = lax.rem(r, 2)
    zz = r // 2
    buddy = n + 1 - 2 * core
    across = lax.rem(n + 2, 4)
    chunks = slots // CHUNK
    half_rows = width // 2
    has_prev = r > 0
    has_next = r < res_total - 1
    sem_at = [0]
    ar_at = [0]

    greeted = [(r, buddy), (r, across)]
    z_peers = []
    if fast:
        greeted.append((r, lax.rem(buddy + 2, 4)))
        y_peer = (r + 1 - 2 * yy, n)
        z_peers = [(2 * lax.rem(zz + k, 4) + yy, n) for k in (1, 2, 3)]
        greeted += [y_peer, *z_peers]
        up_too = jnp.logical_and(yy == 0, has_prev)
        down_too = jnp.logical_and(yy == 1, has_next)
    else:
        up_too, down_too = has_prev, has_next
    barrier = pltpu.get_barrier_semaphore()
    for device in greeted:
        pl.semaphore_signal(barrier, inc=1, device_id=device, device_id_type=MESH)

    def greet(device):
        pl.semaphore_signal(barrier, inc=1, device_id=device, device_id_type=MESH)

    pl.when(up_too)(lambda: greet((r - 1, n)))
    pl.when(down_too)(lambda: greet((r + 1, n)))
    pl.when(has_prev)(lambda: greet((r - 1, across)))
    pl.when(has_next)(lambda: greet((r + 1, across)))
    greetings = len(greeted)
    for there in (up_too, down_too, has_prev, has_next):
        greetings += there.astype(jnp.int32)

    zero_tile = jnp.zeros((width, LANES), BF16)

    @pl.when(jnp.logical_not(has_prev))
    def _():
        for b in range(3):
            ext[b, 0] = zero_tile
            halo_recv[b, 0:2] = jnp.zeros_like(halo_recv[b, 0:2])

    @pl.when(jnp.logical_not(has_next))
    def _():
        for b in range(3):
            ext[b, 2] = zero_tile
            halo_recv[b, 2:4] = jnp.zeros_like(halo_recv[b, 2:4])

    def next_sem():
        at = sem_at[0]
        sem_at[0] = at + 1
        return refs.send_sem.at[at], refs.recv_sem.at[at]

    def remote(src, dst, device):
        ss, rs = next_sem()
        return pltpu.make_async_remote_copy(
            src_ref=src, dst_ref=dst, send_sem=ss, recv_sem=rs, device_id=device, device_id_type=MESH
        )

    def start(copies):
        for copy in copies:
            copy.start()

    def wait(copies):
        for copy in copies:
            copy.wait()

    def rows_of(at, count):
        return pool.at[pl.ds(at, count)]

    def aligned(at):
        return pl.multiple_of(at, 16)

    def vec(layer, which, rows=None):
        at = layer * VECTORS + which
        return vec_ref[0 : (width if rows is None else rows), at : at + 1]

    def put_vec(layer, which, value):
        at = layer * VECTORS + which
        refs.g_vec[0 : value.shape[0], at : at + 1] = jnp.sum(value, axis=1, keepdims=True)

    load_edges = pltpu.make_async_copy(refs.edges, g_edges, refs.local_sem.at[0])
    load_edges.start()

    def two_way(pairs):
        ups = [remote(a, b, (r - 1, col)) for col, a, b, _, _ in pairs]
        downs = [remote(a, b, (r + 1, col)) for col, _, _, a, b in pairs]

        def begin():
            pl.when(has_prev)(lambda: start(ups))
            pl.when(has_next)(lambda: start(downs))

        def finish():
            @pl.when(has_prev)
            def _():
                for up, down in zip(ups, downs, strict=True):
                    up.wait_send()
                    down.wait_recv()

            @pl.when(has_next)
            def _():
                for up, down in zip(ups, downs, strict=True):
                    down.wait_send()
                    up.wait_recv()

        return begin, finish

    def all_reduce(value, meanwhile=lambda: None):
        at = ar_at[0] % 2
        ar_at[0] += 1
        mine = pl.multiple_of(core * half_rows, half_rows)
        theirs = pl.multiple_of(half_rows - mine, half_rows)
        ar_part[at] = value
        one = remote(ar_part.at[at, pl.ds(theirs, half_rows)], ar_one.at[at], (r, buddy))
        one.start()
        one.wait()
        ar_two[at] = (ar_part[at, pl.ds(mine, half_rows)] + ar_one[at]).astype(BF16)
        two = remote(ar_two.at[at], ar_three.at[at], (r, across))
        two.start()
        meanwhile()
        two.wait()
        ar_tot[at, pl.ds(mine, half_rows)] = ar_two[at].astype(F32) + ar_three[at].astype(F32)
        span = ar_tot.at[at, pl.ds(mine, half_rows)]
        three = remote(span, span, (r, buddy))
        three.start()
        three.wait()
        return ar_tot.at[at]

    def extended(b):
        return jnp.concatenate([ext[b, 0], ext[b, 1], ext[b, 2]], axis=1)

    def halo(b, value):
        ext[b, 1] = value
        begin, finish = two_way([(n, ext.at[b, 1], ext.at[b, 2], ext.at[b, 1], ext.at[b, 0])])
        begin()
        return finish

    def halo_back(b, g_ext, g_own, beside_core=lambda: None, beside_far=lambda: None):
        at = ar_at[0] % 2
        ar_at[0] += 1
        my_half = pl.ds(pl.multiple_of(core * half_rows, half_rows), half_rows)
        their_half = pl.ds(pl.multiple_of(half_rows - core * half_rows, half_rows), half_rows)
        for k in range(3):
            part = g_ext[:, k * LANES : (k + 1) * LANES]
            g_part[k] = part + g_own if k == 1 else part
        halo_send[...] = g_part[:, their_half].astype(BF16)
        one = remote(halo_send, refs.halo_core, (r, buddy))
        one.start()
        beside_core()
        one.wait()
        half = refs.halo_half
        half[...] = (g_part[:, my_half] + refs.halo_core[...].astype(F32)).astype(BF16)
        two = remote(half.at[1], refs.halo_x, (r, across))
        begin, finish = two_way(
            [
                (n, half.at[0], halo_recv.at[b, 2], half.at[2], halo_recv.at[b, 0]),
                (across, half.at[0], halo_recv.at[b, 3], half.at[2], halo_recv.at[b, 1]),
            ]
        )
        begin()
        two.start()
        beside_far()
        two.wait()
        finish()
        total = half[1].astype(F32) + refs.halo_x[...].astype(F32)
        for k in (0, 2):
            total += halo_recv[b, k].astype(F32) + halo_recv[b, k + 1].astype(F32)
        ar_tot[at, my_half] = total
        span = ar_tot.at[at, my_half]
        three = remote(span, span, (r, buddy))
        three.start()
        three.wait()
        return ar_tot.at[at]

    FULL = (IN0, MO0, TB, ED, IN1, MO1)
    shard_at = ((core * 2 + xx) * 2 + yy) * 4 + zz
    short_at = yy * 4 + zz

    def my_shard(item):
        at = shard_at if item in FULL else short_at
        return aligned(plan.stage[item] + at * plan.sizes[item])

    def gather_z(item):
        size = plan.sizes[item]
        span = rows_of(my_shard(item), size)
        return [remote(span, span, peer) for peer in z_peers]

    def gather_span(item, count, device):
        size = plan.sizes[item]
        at = shard_at if item in FULL else short_at
        span = rows_of(aligned(plan.stage[item] + (at // count) * (count * size)), count * size)
        return [remote(span, span, device)]

    def gather_y(item):
        return gather_span(item, 4, y_peer)

    def gather_x(item):
        return gather_span(item, 8, (r, across))

    def gather_c(item):
        return gather_span(item, 16, (r, buddy))

    def add_rows(at, other, count):
        block = next(b for b in (512, 256, 128, 64, 32, 16) if count % b == 0)

        def step(i, _):
            to = pl.ds(aligned(at + i * block), block)
            pool[to] = (pool[to].astype(F32) + pool[pl.ds(aligned(other + i * block), block)].astype(F32)).astype(BF16)
            return 0

        lax.fori_loop(0, count // block, step, 0)

    def reduce_pairs(item, stage):
        size, source = plan.sizes[item], plan.source[item]
        if stage == BY_CORE:
            count, mine, theirs, device = 16, core, 1 - core, (r, buddy)
        elif stage == BY_X:
            count, mine, theirs, device = 8, core * 2 + xx, core * 2 + 1 - xx, (r, across)
        else:
            base = (core * 2 + xx) * 2 if item in FULL else 0
            count, mine, theirs, device = 4, base + yy, base + 1 - yy, y_peer
        arrived = plan.recv[item, stage]
        copy = remote(
            rows_of(aligned(source + theirs * (count * size)), count * size),
            rows_of(arrived, count * size),
            device,
        )
        return [copy], lambda: add_rows(aligned(source + mine * (count * size)), arrived, count * size)

    def reduce_z(item):
        size, source = plan.sizes[item], plan.source[item]
        base = ((core * 2 + xx) * 2 + yy) * 4 if item in FULL else yy * 4
        copies = []
        for k in (1, 2, 3):
            to = lax.rem(zz + k, 4)
            copies.append(
                remote(
                    rows_of(aligned(source + (base + to) * size), size),
                    rows_of(plan.recv[item, BY_Z] + (k - 1) * size, size),
                    z_peers[k - 1],
                )
            )

        def total(first, count):
            value = pool[pl.ds(aligned(source + (base + zz) * size + first), count)].astype(F32)
            for k in range(3):
                value += pool[pl.ds(plan.recv[item, BY_Z] + k * size + first, count)].astype(F32)
            return value

        return copies, total

    def blocks():
        for at in range(32):
            c, x, y, z = at // 16, at // 8 % 2, at // 4 % 2, at % 4
            yield at, 2 * z + y, 2 * x + c

    def assemble_in(layer):
        at = plan.stage[IN[layer]]
        for k, rr, nn_ in blocks():
            wide[rr * plan.k_in : (rr + 1) * plan.k_in, nn_ * LANES : (nn_ + 1) * LANES] = pool[
                at + k * plan.in_rows : at + k * plan.in_rows + plan.k_in
            ].astype(F32)
        w_in[layer] = wide[: w_in.shape[1], :width].astype(BF16)
        turned = wide[2 * width : 2 * width + 2 * LANES, :width].T
        w_et[layer] = turned[:, :ew].astype(BF16)

    def assemble_mo(layer):
        at = plan.stage[MO[layer]]
        k_mid = plan.k_mid
        for k, rr, nn_ in blocks():
            to = (layer, slice(rr * k_mid, (rr + 1) * k_mid), slice(nn_ * LANES, (nn_ + 1) * LANES))
            first = at + k * plan.mo_rows
            w_mid[to] = pool[first : first + k_mid]
            w_out[to] = pool[first + k_mid : first + 2 * k_mid]
        w_midt[layer] = w_mid[layer].astype(F32).T.astype(BF16)

    def turn_square(value):
        wide[:ew, :ew] = value
        return wide[: 2 * LANES, : 2 * LANES].T[:ew, :ew]

    def assemble_edge():
        at, cols = plan.stage[ED], ew // 4
        long = up_to(w_in.shape[1], LANES)
        for k, rr, nn_ in blocks():
            first = at + k * plan.ed_rows
            wide[rr * plan.k_in : (rr + 1) * plan.k_in, nn_ * LANES : (nn_ + 1) * LANES] = pool[
                first : first + plan.k_in
            ].astype(F32)
        for nn_ in range(4):
            turned = wide[:long, nn_ * LANES : (nn_ + 1) * LANES].T
            for layer in range(2):
                e_int[layer, nn_ * cols : (nn_ + 1) * cols] = turned[
                    layer * cols : (layer + 1) * cols, : w_in.shape[1]
                ].astype(BF16)
        for layer in range(2):
            for k, rr, nn_ in blocks():
                first = at + k * plan.ed_rows + plan.in_pad + layer * plan.hid_pad
                wide[rr * plan.k_hid : (rr + 1) * plan.k_hid, nn_ * LANES : (nn_ + 1) * LANES] = pool[
                    first : first + plan.k_hid
                ].astype(F32)
            for nn_ in range(4):
                turned = wide[: 2 * LANES, nn_ * LANES : (nn_ + 1) * LANES].T
                for m in range(2):
                    e_hidt[layer, m, nn_ * cols : (nn_ + 1) * cols] = turned[
                        m * cols : (m + 1) * cols, :ew
                    ].astype(BF16)
        for layer in range(2):
            e_e[layer] = turn_square(e_int[layer, :, 2 * width :].astype(F32)).astype(BF16)
            for m in range(2):
                e_hid[layer, m] = turn_square(e_hidt[layer, m].astype(F32)).astype(BF16)

    def assemble_ffn(layer):
        at, k_mid = plan.stage[FF[layer]], plan.k_mid
        for y in range(2):
            for z in range(4):
                rr = 2 * z + y
                for j in range(ff // LANES):
                    for m, ref in enumerate((f_in, f_outt)):
                        first = at + (y * 4 + z) * plan.ff_rows + (m * (ff // LANES) + j) * k_mid
                        ref[layer, rr * k_mid : (rr + 1) * k_mid, j * LANES : (j + 1) * LANES] = pool[
                            first : first + k_mid
                        ]

    def emit_ffn(layer, g_fin, g_foutt):
        if not fast:
            refs.g_fin[layer] = g_fin.astype(BF16)
            refs.g_foutt[layer] = g_foutt.astype(BF16)
            return
        at, k_mid = plan.source[FF[layer]], plan.k_mid
        for m, value in enumerate((g_fin.astype(BF16), g_foutt.astype(BF16))):
            for y in range(2):
                for z in range(4):
                    rr = 2 * z + y
                    for j in range(ff // LANES):
                        first = at + (y * 4 + z) * plan.ff_rows + (m * (ff // LANES) + j) * k_mid
                        pool[first : first + k_mid] = value[
                            rr * k_mid : (rr + 1) * k_mid, j * LANES : (j + 1) * LANES
                        ]

    def emit_middle(layer, g_mid, g_out):
        if not fast:
            refs.g_mid[layer] = g_mid.astype(BF16)
            refs.g_out[layer] = g_out.astype(BF16)
            return
        at, k_mid = plan.source[MO[layer]], plan.k_mid
        for m, value in enumerate((g_mid.astype(BF16), g_out.astype(BF16))):
            for k, rr, nn_ in blocks():
                first = at + k * plan.mo_rows + m * k_mid
                pool[first : first + k_mid] = value[
                    rr * k_mid : (rr + 1) * k_mid, nn_ * LANES : (nn_ + 1) * LANES
                ]

    def emit_input(layer, g_own_rows, g_other_rows, g_edge_rows):
        if not fast:
            refs.g_in[layer, :width] = g_own_rows.astype(BF16)
            refs.g_in[layer, width : 2 * width] = g_other_rows.astype(BF16)
            refs.g_in[layer, 2 * width :] = g_edge_rows.astype(BF16)
            return
        wide[:width, :width] = g_own_rows
        wide[width : 2 * width, :width] = g_other_rows
        wide[2 * width : 2 * width + ew, :width] = g_edge_rows
        at = plan.source[IN[layer]]
        for k, rr, nn_ in blocks():
            first = at + k * plan.in_rows
            pool[first : first + plan.k_in] = wide[
                rr * plan.k_in : (rr + 1) * plan.k_in, nn_ * LANES : (nn_ + 1) * LANES
            ].astype(BF16)

    def emit_edge_all():
        at, cols = plan.source[ED], ew // 4
        long = up_to(w_in.shape[1], LANES)
        fill = LANES - 2 * cols
        for nn_ in range(4):
            span = slice(nn_ * cols, (nn_ + 1) * cols)
            tall = jnp.concatenate(
                [refs.g_eint[0, span].astype(F32), refs.g_eint[1, span].astype(F32), jnp.zeros((fill, long), F32)],
                axis=0,
            ).T
            wide[:long, nn_ * LANES : (nn_ + 1) * LANES] = tall
        for k, rr, nn_ in blocks():
            first = at + k * plan.ed_rows
            pool[first : first + plan.k_in] = wide[
                rr * plan.k_in : (rr + 1) * plan.k_in, nn_ * LANES : (nn_ + 1) * LANES
            ].astype(BF16)
        for layer in range(2):
            for nn_ in range(4):
                span = slice(nn_ * cols, (nn_ + 1) * cols)
                tall = jnp.concatenate(
                    [refs.g_ehid[layer, m, span].astype(F32) for m in range(2)]
                    + [jnp.zeros((fill, 2 * LANES), F32)],
                    axis=0,
                ).T
                wide[: 2 * LANES, nn_ * LANES : (nn_ + 1) * LANES] = tall
            for k, rr, nn_ in blocks():
                first = at + k * plan.ed_rows + plan.in_pad + layer * plan.hid_pad
                pool[first : first + plan.k_hid] = wide[
                    rr * plan.k_hid : (rr + 1) * plan.k_hid, nn_ * LANES : (nn_ + 1) * LANES
                ].astype(BF16)

    def act_at(kind, layer, slot):
        return pl.ds(aligned(plan.acts[layer] + kind * plan.act_rows + slot * width), width)

    U1, S1, S2 = 0, 1, 2
    W1, T1, W2, T2 = 0, 1, 2, 3

    def edge_act(kind, layer, base, j):
        slot = base + j if layer == 0 else slots + j
        return pl.ds(aligned(plan.edge_at + kind * plan.edge_rows + slot * ew), ew)

    def acts(kind, layer, base):
        return jnp.concatenate([pool[act_at(kind, layer, base + j)] for j in range(CHUNK)], axis=1)

    def edge_acts(kind, layer, base):
        return jnp.concatenate([pool[edge_act(kind, layer, base, j)] for j in range(CHUNK)], axis=1)

    def lanes_of(ref, base, *lead):
        return jnp.concatenate([ref[(*lead, base + j)] for j in range(CHUNK)], axis=1)

    def make_vectors():
        refs.g_vec[...] = jnp.zeros_like(refs.g_vec)
        mask_ref[...] = refs.mask[...].astype(F32)
        for layer in range(plan.layers):
            at = layer * VECTORS
            for k in range(6):
                wide[at + k : at + k + 1, :width] = refs.node_biases[k, layer : layer + 1]
            wide[at + GN1 : at + GN2 + 1, :width] = refs.node_gains[layer]
            first = pl.multiple_of(n * ff, ff)
            wide[at + FB : at + FB + 1, :ff] = refs.ffn_bias[layer : layer + 1, pl.ds(first, ff)]
            wide[at + C1 : at + C4 + 1, :ew] = refs.edge_biases[layer]
            wide[at + GE : at + GE + 1, :ew] = refs.edge_gains[layer : layer + 1]
        vec_ref[...] = wide[:LANES, :width].T

    def make_onehot():
        cells = lax.broadcasted_iota(jnp.int32, (3 * LANES, LANES), 0) + (r - 1) * LANES

        def step(s, _):
            onehot[s] = jnp.where(cells == refs.neighbors[pl.ds(s, 1), :], 1.0, 0.0).astype(BF16)
            eb[0, s] = g_edges[s].astype(BF16)
            return 0

        load_edges.wait()
        lax.fori_loop(0, slots, step, 0)

    def prepare_message(layer):
        proj[:, : 3 * LANES] = tn(w_in[layer, width : 2 * width, :], extended(layer)).astype(BF16)
        proj[:, 3 * LANES :] = w_et[layer]
        own[...] = tn(w_in[layer, :width, :], ext[layer, 1]) + vec(layer, B1)
        ubar[layer] = jnp.zeros((width, LANES), F32)

    def prepare_edge(layer):
        proj_e[:, : 3 * LANES] = nn(e_int[layer, :, width : 2 * width], extended(layer + 1)).astype(BF16)
        proj_e[:, 3 * LANES :] = e_int[layer, :, 2 * width :]
        own_e[...] = nn(e_int[layer, :, :width], ext[layer + 1, 1]) + vec(layer, C1, ew)

    def message_forward(layer, base):
        rows = jnp.concatenate([lanes_of(onehot, base), lanes_of(eb, base, layer)], axis=0)
        wide[:width, :] = nn(proj[...], rows)
        for j in range(CHUNK):
            z = wide[:width, j * LANES : (j + 1) * LANES] + own[...]
            pool[act_at(U1, layer, base + j)], pool[act_at(S1, layer, base + j)] = gelu_pair(z)
        wide[:width, :] = nn(w_midt[layer], acts(U1, layer, base))
        for j in range(CHUNK):
            z = wide[:width, j * LANES : (j + 1) * LANES] + vec(layer, B2)
            u2, pool[act_at(S2, layer, base + j)] = gelu_pair(z)
            ubar[layer] += u2.astype(F32) * mask_ref[pl.ds(base + j, 1), :]

    def edge_forward(layer, base, edge_ref, save):
        rows = jnp.concatenate([lanes_of(onehot, base), lanes_of(eb, base, layer)], axis=0)
        z = nn(proj_e[...], rows)
        for j in range(CHUNK):
            zj = z[:, j * LANES : (j + 1) * LANES] + own_e[...]
            pool[edge_act(W1, layer, base, j)], pool[edge_act(T1, layer, base, j)] = gelu_pair(zj)
        z = nn(e_hidt[layer, 0], edge_acts(W1, layer, base))
        for j in range(CHUNK):
            zj = z[:, j * LANES : (j + 1) * LANES] + vec(layer, C2, ew)
            pool[edge_act(W2, layer, base, j)], pool[edge_act(T2, layer, base, j)] = gelu_pair(zj)
        z = nn(e_hidt[layer, 1], edge_acts(W2, layer, base))
        for j in range(CHUNK):
            p = edge_ref[base + j] + z[:, j * LANES : (j + 1) * LANES] + vec(layer, C3, ew)
            hat, rstd = norm_parts(p)
            save(j, hat, rstd, p, hat * vec(layer, GE, ew) + vec(layer, C4, ew))

    def node_update(layer, before_ffn=lambda: None, beside_branch=lambda: None):
        total = all_reduce(ubar[layer])[...]
        high = total.astype(BF16)
        low = (total - high.astype(F32)).astype(BF16)
        counts = cnt_ref[...]
        sums = tn(w_out[layer], high) + tn(w_out[layer], low) + counts * vec(layer, B3)
        merged = state[layer] + sums * (1.0 / counts)
        joined_a[layer] = merged
        hat, _ = norm_parts(merged)
        hidden = hat * vec(layer, GN1) + vec(layer, SH1)
        h1b[layer] = hidden.astype(BF16)
        before_ffn()
        pre = tn(f_in[layer], h1b[layer]) + vec(layer, FB)
        act[layer], slope_f[layer] = gelu_pair(pre)
        branch = all_reduce(nn(f_outt[layer], act[layer]), beside_branch)[...]
        joined = hidden + (branch + vec(layer, B5))
        joined_c[layer] = joined
        hat, _ = norm_parts(joined)
        state[layer + 1] = hat * vec(layer, GN2) + vec(layer, SH2)
        return halo(layer + 1, state[layer + 1].astype(BF16))

    def clear_edge():
        for ref in (acc_h2, acc_h3, acc_ee, acc_t, acc_ts, acc_c):
            ref[...] = jnp.zeros_like(ref)

    def clear_message():
        for ref in (acc_mid, acc_e, acc_z, acc_zs, acc_b2):
            ref[...] = jnp.zeros_like(ref)

    def edge_backward(layer, base, parts):
        lows = []
        for j in range(CHUNK):
            hat, rstd, grad = parts(j)
            acc_c[0] += grad * hat
            acc_c[1] += grad
            dp = norm_back(hat, rstd, vec(layer, GE, ew), grad)
            g_edges[base + j] = dp
            low = dp.astype(BF16)
            acc_c[2] += low.astype(F32)
            lows.append(low)
        out = jnp.concatenate(lows, axis=1)
        acc_h3[...] += nt(out, edge_acts(W2, layer, base))
        grad_two = (nn(e_hid[layer, 1], out) * edge_acts(T2, layer, base).astype(F32)).astype(BF16)
        for j in range(CHUNK):
            acc_c[3] += grad_two[:, j * LANES : (j + 1) * LANES].astype(F32)
        acc_h2[...] += nt(grad_two, edge_acts(W1, layer, base))
        grad_one = (nn(e_hid[layer, 0], grad_two) * edge_acts(T1, layer, base).astype(F32)).astype(BF16)
        for j in range(CHUNK):
            acc_ts[...] += grad_one[:, j * LANES : (j + 1) * LANES].astype(F32)
        acc_t[...] += nt(grad_one, lanes_of(onehot, base))
        acc_ee[...] += nt(grad_one, lanes_of(eb, base, layer))
        back = nn(e_e[layer], grad_one)
        for j in range(CHUNK):
            g_edges[base + j] += back[:, j * LANES : (j + 1) * LANES]

    def edge_terms(layer):
        table = acc_t[...].astype(BF16)
        sums = acc_ts[...].astype(BF16)
        g_ext = tn(e_int[layer, :, width : 2 * width], table)
        g_own = tn(e_int[layer, :, :width], sums)
        return g_ext, g_own

    def edge_finish(layer):
        put_vec(layer, GE, acc_c[0])
        put_vec(layer, C4, acc_c[1])
        put_vec(layer, C3, acc_c[2])
        put_vec(layer, C2, acc_c[3])
        put_vec(layer, C1, acc_ts[...])
        refs.g_ehid[layer, 0, :, :ew] = acc_h2[...].astype(BF16)
        refs.g_ehid[layer, 1, :, :ew] = acc_h3[...].astype(BF16)
        table = acc_t[...].astype(BF16)
        sums = acc_ts[...].astype(BF16)
        refs.g_eint[layer, :, :width] = nt(sums, ext[layer + 1, 1]).astype(BF16)
        refs.g_eint[layer, :, width : 2 * width] = nt(table, extended(layer + 1)).astype(BF16)
        refs.g_eint[layer, :, 2 * width : 2 * width + ew] = acc_ee[...].astype(BF16)

    def message_back_two(layer, base):
        grads = []
        for j in range(CHUNK):
            s = base + j
            slope = pool[act_at(S2, layer, s)].astype(F32)
            dz = (vrow[...] * mask_ref[pl.ds(s, 1), :] * slope).astype(BF16)
            acc_b2[...] += dz.astype(F32)
            pool[act_at(S2, layer, s)] = dz
            grads.append(dz)
        acc_mid[...] += nt(acts(U1, layer, base), jnp.concatenate(grads, axis=1))

    def message_back_one(layer, base, add_edge):
        wide[:width, :] = nn(w_mid[layer], acts(S2, layer, base))
        grads = []
        for j in range(CHUNK):
            slope = pool[act_at(S1, layer, base + j)].astype(F32)
            dz = (wide[:width, j * LANES : (j + 1) * LANES] * slope).astype(BF16)
            acc_zs[...] += dz.astype(F32)
            grads.append(dz)
        grad_one = jnp.concatenate(grads, axis=1)
        acc_z[...] += nt(grad_one, lanes_of(onehot, base))
        acc_e[...] += nt(lanes_of(eb, base, layer), grad_one)
        back = nn(w_in[layer, 2 * width :, :], grad_one)
        for j in range(CHUNK):
            add_edge(base + j, back[:, j * LANES : (j + 1) * LANES])

    def middle_finish(layer):
        put_vec(layer, B2, acc_b2[...])
        emit_middle(layer, acc_mid[...], nt(ubar[layer].astype(BF16), ds_ref[...]))

    def message_terms(layer):
        table = acc_z[...].astype(BF16)
        sums = acc_zs[...].astype(BF16)
        g_ext = nn(w_in[layer, width : 2 * width, :], table)
        g_own = nn(w_in[layer, :width, :], sums)
        return g_ext, g_own

    def message_finish(layer):
        table = acc_z[...].astype(BF16)
        sums = acc_zs[...].astype(BF16)
        emit_input(layer, nt(ext[layer, 1], sums), nt(extended(layer), table), acc_e[...])
        put_vec(layer, B1, acc_zs[...])

    def node_back(layer, meanwhile=lambda: None):
        counts = cnt_ref[...]
        grad = dcur[...]
        hat, rstd = norm_parts(joined_c[layer])
        put_vec(layer, GN2, grad * hat)
        put_vec(layer, SH2, grad)
        dc = norm_back(hat, rstd, vec(layer, GN2), grad)
        dy = dc.astype(BF16)
        put_vec(layer, B5, dy.astype(F32))
        df = (tn(f_outt[layer], dy) * slope_f[layer].astype(F32)).astype(BF16)
        put_vec(layer, FB, df.astype(F32))
        part = nn(f_in[layer], df)
        total = all_reduce(part, meanwhile)
        emit_ffn(layer, nt(h1b[layer], df), nt(dy, act[layer]))
        grad = dc + total[...]
        hat, rstd = norm_parts(joined_a[layer])
        put_vec(layer, GN1, grad * hat)
        put_vec(layer, SH1, grad)
        da = norm_back(hat, rstd, vec(layer, GN1), grad)
        dcur[...] = da
        ds = (da * (1.0 / counts)).astype(BF16)
        ds_ref[...] = ds
        put_vec(layer, B3, ds.astype(F32) * counts)
        vrow[...] = nn(w_out[layer], ds)

    if fast:
        own_rows = refs.nodes.shape[0]
        mine = pl.multiple_of(n * own_rows, own_rows)
        k_mid = plan.k_mid

        def pack_in(layer):
            pool[pl.ds(my_shard(IN[layer]), plan.k_in)] = refs.msg_in[layer].astype(BF16)

        def pack_mo(layer):
            at = my_shard(MO[layer])
            pool[pl.ds(at, k_mid)] = refs.msg_mid[layer].astype(BF16)
            pool[pl.ds(aligned(at + k_mid), k_mid)] = refs.msg_out[layer].astype(BF16)

        def pack_ffn(layer):
            at = my_shard(FF[layer])
            for m, ref in enumerate((refs.ffn_in, refs.ffn_outt)):
                for j in range(ff // LANES):
                    to = aligned(at + (m * (ff // LANES) + j) * k_mid)
                    pool[pl.ds(to, k_mid)] = ref[layer, :, j * LANES : (j + 1) * LANES].astype(BF16)

        def pack_edge():
            cols = ew // 4
            for layer in range(2):
                wide[layer * cols : (layer + 1) * cols, : plan.k_in] = refs.edge_in_t[layer]
            turned = wide[:LANES, : 2 * LANES].T
            at = my_shard(ED)
            pool[pl.ds(at, plan.k_in)] = turned[: plan.k_in].astype(BF16)
            for layer in range(2):
                for m in range(2):
                    wide[: plan.k_hid, m * cols : (m + 1) * cols] = refs.edge_hidden[layer, m]
                to = aligned(at + plan.in_pad + layer * plan.hid_pad)
                pool[pl.ds(to, plan.k_hid)] = wide[: plan.k_hid, :LANES].astype(BF16)

        pack_in(0)
        pool[pl.ds(my_shard(TB), plan.tb_rows)] = refs.time_table[...].astype(BF16)
        refs.all_nodes[pl.ds(mine, own_rows)] = refs.nodes[...]
        refs.all_dnodes[pl.ds(mine, own_rows)] = refs.d_nodes[...]
        steps = jnp.zeros((1, own_rows), jnp.int32)
        for p in range(refs.time_index.shape[0]):
            steps += jnp.where(refs.protein_ids[...] == p, refs.time_index[p], 0)
        refs.all_misc[n, 0:1, :] = jnp.sum(refs.mask[...].astype(F32), axis=0, keepdims=True)
        refs.all_misc[n, 1:2, :own_rows] = steps.astype(F32)
        pl.semaphore_wait(barrier, greetings)

        node_copies, late_copies = [], []
        for k in (1, 2, 3):
            peer = (r, lax.rem(n + k, 4))
            for ref, group in (
                (refs.all_nodes.at[pl.ds(mine, own_rows)], node_copies),
                (refs.all_misc.at[n], node_copies),
                (refs.all_dnodes.at[pl.ds(mine, own_rows)], late_copies),
            ):
                group.append(remote(ref, ref, peer))
        every = range(FF1 + 1)
        gz = {item: gather_z(item) for item in every}
        gy = {item: gather_y(item) for item in every}
        gx = {item: gather_x(item) for item in FULL}
        gc = {item: gather_c(item) for item in FULL}

        def pass_on(before, after, *items):
            for item in items:
                wait(before[item])
                start(after[item])

        def first(stage, *items):
            for item in items:
                start(stage[item])

        first(gz, TB, IN0)
        start(node_copies)
        pack_mo(0)
        first(gz, MO0)
        pack_in(1)
        pack_mo(1)
        first(gz, IN1, MO1)
        pack_edge()
        first(gz, ED)
        pass_on(gz, gy, TB, IN0)
        pack_ffn(0)
        pass_on(gy, gx, TB)
        make_vectors()
        wait(node_copies)
        misc = refs.all_misc[0]
        for k in range(1, 4):
            misc += refs.all_misc[k]
        cnt_ref[...] = misc[0:1]
        steps = jnp.concatenate([refs.all_misc[k, 1:2, :own_rows] for k in range(4)], axis=1)
        times = lax.broadcasted_iota(jnp.int32, (8 * plan.k_time, LANES), 0).astype(F32)
        refs.time_hot[...] = jnp.where(times == steps, 1.0, 0.0).astype(BF16)
        nodes_t = refs.all_nodes[...].T
        pass_on(gx, gc, TB)
        pass_on(gy, gx, IN0)
        wait(gc[TB])
        for k, rr, nn_ in blocks():
            at = plan.stage[TB] + k * plan.tb_rows
            refs.time_rows[rr * plan.k_time : (rr + 1) * plan.k_time, nn_ * LANES : (nn_ + 1) * LANES] = pool[
                at : at + plan.tb_rows
            ]
        state[0] = nodes_t + tn(refs.time_rows[...], refs.time_hot[...])
        finish = halo(0, state[0].astype(BF16))
        pass_on(gz, gy, MO0)
        first(gz, FF0)
        make_onehot()
        pass_on(gy, gx, MO0)
        pass_on(gz, gy, IN1, MO1)
        pack_ffn(1)
        pass_on(gx, gc, IN0)
        wait(gc[IN0])
        assemble_in(0)
        pass_on(gx, gc, MO0)
        pass_on(gy, gx, IN1, MO1)
        pass_on(gz, gy, ED)
        first(gz, FF1)
        wait(gc[MO0])
        assemble_mo(0)
        finish()
        pass_on(gy, gx, ED)
    else:
        make_vectors()
        make_onehot()
        pl.semaphore_wait(barrier, greetings)
        state[0] = refs.h0[...]
        halo(0, state[0].astype(BF16))()

    prepare_message(0)

    def loop_a(i, _):
        message_forward(0, i * CHUNK)
        if fast:

            @pl.when(i == 1)
            def _():
                pass_on(gz, gy, FF0)

        return 0

    lax.fori_loop(0, chunks, loop_a, 0)

    def need_ffn0():
        if fast:
            pass_on(gx, gc, IN1, MO1)
            wait(gy[FF0])
            assemble_ffn(0)

    def beside_branch():
        if fast:
            wait(gc[IN1])
            assemble_in(1)

    finish = node_update(0, need_ffn0, beside_branch)
    if fast:
        start(late_copies)
        pass_on(gx, gc, ED)
        wait(gc[MO1])
        assemble_mo(1)
        wait(gc[ED])
        assemble_edge()
    finish()
    prepare_edge(0)
    if fast:
        pass_on(gz, gy, FF1)
    prepare_message(1)

    def loop_b(i, _):
        base = i * CHUNK

        def save(j, hat, rstd, p, value):
            psum[base + j] = p
            edges_out[base + j] = value
            eb[1, base + j] = value.astype(BF16)

        edge_forward(0, base, g_edges, save)
        message_forward(1, base)
        return 0

    lax.fori_loop(0, chunks, loop_b, 0)
    load_grads = pltpu.make_async_copy(refs.d_edges, g_edges, refs.local_sem.at[1])
    load_grads.start()

    def need_ffn1():
        if fast:
            wait(late_copies)
            wait(gy[FF1])
            assemble_ffn(1)

    finish = node_update(1, need_ffn1)
    if fast:
        refs.all_nodes[...] = state[2].T
        nodes_out[...] = refs.all_nodes[pl.ds(mine, own_rows)]
    else:
        nodes_out[...] = state[2].T
    clear_edge()
    load_grads.wait()
    finish()
    prepare_edge(1)

    def loop_c(i, _):
        base = i * CHUNK
        kept = {}

        def save(j, hat, rstd, p, value):
            edges_out[base + j] = value
            kept[j] = (hat, rstd)

        edge_forward(1, base, edges_out, save)
        edge_backward(1, base, lambda j: (*kept[j], g_edges[base + j]))
        return 0

    lax.fori_loop(0, chunks, loop_c, 0)
    save_edges = pltpu.make_async_copy(edges_out, refs.edges_out, refs.local_sem.at[2])
    save_edges.start()
    g_ext, g_own = edge_terms(1)
    dh = refs.all_dnodes[...].T if fast else refs.dh[...]
    dcur[...] = dh + halo_back(0, g_ext, g_own, beside_far=lambda: edge_finish(1))[...]
    node_back(1)
    clear_message()
    clear_edge()
    reduce_c, reduce_x, reduce_y, reduce_last = {}, {}, {}, {}
    if fast:
        for item in range(FF1 + 1):
            if item in FULL:
                reduce_c[item] = reduce_pairs(item, BY_CORE)
                reduce_x[item] = reduce_pairs(item, BY_X)
            reduce_y[item] = reduce_pairs(item, BY_Y)
            reduce_last[item] = reduce_z(item)

    def reduce_on(before, after, *items):
        for item in items:
            wait(before[item][0])
            before[item][1]()
            start(after[item][0])

    def put_ffn(layer):
        copies, total = reduce_last[FF[layer]]
        wait(copies)
        k_mid, parts = plan.k_mid, ff // LANES
        for m, ref in enumerate((refs.o_fin, refs.o_foutt)):
            for j in range(parts):
                ref[layer, :, j * LANES : (j + 1) * LANES] = total((m * parts + j) * k_mid, k_mid)

    def put_message(layer):
        copies, total = reduce_last[IN[layer]]
        wait(copies)
        refs.o_in[layer] = total(0, plan.k_in)
        copies, total = reduce_last[MO[layer]]
        wait(copies)
        refs.o_mid[layer] = total(0, plan.k_mid)
        refs.o_out[layer] = total(plan.k_mid, plan.k_mid)

    def put_edge():
        copies, total = reduce_last[ED]
        wait(copies)
        cols = ew // 4
        wide[: plan.in_pad, :LANES] = total(0, plan.in_pad)
        turned = wide[: 2 * LANES, :LANES].T
        hidden = total(plan.in_pad, 2 * plan.hid_pad)
        for layer in range(2):
            refs.o_edge[layer] = turned[layer * cols : (layer + 1) * cols, : plan.k_in]
            first = layer * plan.hid_pad
            for m in range(2):
                refs.o_hid[layer, m] = hidden[first : first + plan.k_hid, m * cols : (m + 1) * cols]

    if fast:
        start(reduce_y[FF1][0])

    def loop_d1(i, _):
        base = i * CHUNK

        def add_edge(s, value):
            g_edges[s] += value

        message_back_two(1, base)
        message_back_one(1, base, add_edge)
        return 0

    lax.fori_loop(0, chunks, loop_d1, 0)
    middle_finish(1)
    message_finish(1)
    m_ext, m_own = message_terms(1)
    acc_z[...] = m_ext
    acc_zs[...] = m_own
    if fast:
        start(reduce_c[IN1][0])
        start(reduce_c[MO1][0])

    def loop_d2(i, _):
        base = i * CHUNK
        edge_backward(0, base, lambda j: (*norm_parts(psum[base + j]), g_edges[base + j]))
        if fast:

            @pl.when(i == 1)
            def _():
                reduce_on(reduce_c, reduce_x, IN1)

        return 0

    lax.fori_loop(0, chunks, loop_d2, 0)
    e_ext, e_own = edge_terms(0)

    def beside_edge():
        if fast:
            reduce_on(reduce_c, reduce_x, MO1)
            reduce_on(reduce_y, reduce_last, FF1)
        edge_finish(0)
        if fast:
            emit_edge_all()
            reduce_on(reduce_x, reduce_y, IN1)

    dcur[...] += halo_back(1, acc_z[...] + e_ext, acc_zs[...] + e_own, beside_far=beside_edge)[...]

    def beside_node():
        if fast:
            start(reduce_c[ED][0])
            reduce_on(reduce_x, reduce_y, MO1)
            reduce_on(reduce_y, reduce_last, IN1)

    node_back(0, beside_node)
    clear_message()
    if fast:
        start(reduce_y[FF0][0])
        reduce_on(reduce_c, reduce_x, ED)

    def loop_e1(i, _):
        message_back_two(0, i * CHUNK)
        return 0

    lax.fori_loop(0, chunks, loop_e1, 0)
    middle_finish(0)
    if fast:
        start(reduce_c[MO0][0])
        reduce_on(reduce_y, reduce_last, MO1)

    def loop_e2(i, _):
        base = i * CHUNK

        def add_edge(s, value):
            g_edges[s] += value

        message_back_one(0, base, add_edge)
        if fast:

            @pl.when(i == 0)
            def _():
                reduce_on(reduce_c, reduce_x, MO0)

        return 0

    lax.fori_loop(0, chunks, loop_e2, 0)
    save_grads = pltpu.make_async_copy(g_edges, refs.g_edges, refs.local_sem.at[3])
    save_grads.start()
    m_ext, m_own = message_terms(0)
    if not fast:
        message_finish(0)
        final = dcur[...] + halo_back(2, m_ext, m_own)[...]
        g_nodes[...] = final.T
        save_edges.wait()
        save_grads.wait()
        return

    sums = refs.vec_sums
    partners = [(r, buddy), (r, across), y_peer]
    partners += [(2 * (zz + 1 - 2 * lax.rem(zz, 2)) + yy, n), (2 * lax.rem(zz + 2, 4) + yy, n)]
    rounds = [remote(sums.at[2 * k], sums.at[2 * k + 1], partners[k]) for k in range(5)]

    def vec_round(k):
        rounds[k].wait()
        sums[2 * k + 2] = sums[2 * k] + sums[2 * k + 1]
        if k < 4:
            rounds[k + 1].start()

    def beside_last_far():
        reduce_on(reduce_y, reduce_last, FF0)
        message_finish(0)
        start(reduce_c[IN0][0])
        reduce_on(reduce_x, reduce_y, MO0, ED)
        table = refs.g_vec[...].T
        sums[0] = jnp.zeros_like(sums[0])
        for layer in range(2):
            for which, row in VEC_ROWS.items():
                value = table[layer * VECTORS + which : layer * VECTORS + which + 1]
                at = layer * VEC_PER_LAYER + row
                if which == FB:
                    sums[0, pl.ds(at + n, 1)] = value
                else:
                    scale = 1.0 / plan.nbr_total if B3 <= which <= GN2 else 1.0
                    sums[0, at : at + 1] = value * scale
        rounds[0].start()
        reduce_on(reduce_c, reduce_x, IN0)
        vec_round(0)
        put_ffn(1)
        put_message(1)

    final = dcur[...] + halo_back(2, m_ext, m_own, beside_far=beside_last_far)[...]
    high = final.astype(BF16)
    low = (final - high.astype(F32)).astype(BF16)
    g_times = (nt(refs.time_hot[...], high) + nt(refs.time_hot[...], low)) * (1.0 / plan.nbr_total)
    for k, rr, nn_ in blocks():
        at = plan.source[TB] + k * plan.tb_rows
        pool[at : at + plan.tb_rows] = g_times[
            rr * plan.k_time : (rr + 1) * plan.k_time, nn_ * LANES : (nn_ + 1) * LANES
        ].astype(BF16)
    start(reduce_c[TB][0])
    vec_round(1)
    reduce_on(reduce_y, reduce_last, MO0, ED)
    reduce_on(reduce_x, reduce_y, IN0)
    reduce_on(reduce_c, reduce_x, TB)
    refs.all_dnodes[...] = final.T
    g_nodes[...] = refs.all_dnodes[pl.ds(mine, own_rows)]
    vec_round(2)
    reduce_on(reduce_x, reduce_y, TB)
    reduce_on(reduce_y, reduce_last, IN0)
    vec_round(3)
    put_ffn(0)
    reduce_on(reduce_y, reduce_last, TB)
    vec_round(4)
    for layer in range(2):
        at = layer * VEC_PER_LAYER
        for k in range(6):
            refs.o_node_biases[k, layer : layer + 1] = sums[10, at + k : at + k + 1]
        refs.o_node_gains[layer] = sums[10, at + VEC_ROWS[GN1] : at + VEC_ROWS[GN2] + 1]
        for k in range(4):
            first = at + VEC_ROWS[FB] + k
            refs.o_ffn_bias[layer : layer + 1, k * ff : (k + 1) * ff] = sums[10, first : first + 1, :ff]
        first = at + VEC_ROWS[C1]
        refs.o_edge_biases[layer] = sums[10, first : first + 4, :ew]
        refs.o_edge_gains[layer : layer + 1] = sums[10, first + 4 : first + 5, :ew]
    put_message(0)
    put_edge()
    copies, total = reduce_last[TB]
    wait(copies)
    refs.o_time[...] = total(0, plan.tb_rows)
    save_edges.wait()
    save_grads.wait()


def vmem(shape, dtype):
    return pltpu.VMEM(shape, dtype)


def run_whole(plan, operands):
    lanes, slots, width, ew, ff, layers = LANES, plan.slots, plan.width, plan.ew, plan.ff, plan.layers
    rows_in = 2 * width + ew
    node_rows = lanes // plan.nbr_total if plan.fast else lanes
    outs = dict(
        nodes_out=((node_rows, width), F32),
        edges_out=((slots, ew, lanes), F32),
        g_nodes=((node_rows, width), F32),
        g_edges=((slots, ew, lanes), F32),
    )
    scratch = dict(
        onehot=vmem((slots, 3 * lanes, lanes), BF16),
        eb=vmem((layers, slots, ew, lanes), BF16),
        pool=vmem((plan.pool_rows, lanes), BF16),
        psum=vmem((slots, ew, lanes), F32),
        proj=vmem((width, 3 * lanes + ew), BF16),
        proj_e=vmem((ew, 3 * lanes + ew), BF16),
        own=vmem((width, lanes), F32),
        own_e=vmem((ew, lanes), F32),
        state=vmem((3, width, lanes), F32),
        ext=vmem((3, 3, width, lanes), BF16),
        joined_a=vmem((layers, width, lanes), F32),
        joined_c=vmem((layers, width, lanes), F32),
        h1b=vmem((layers, width, lanes), BF16),
        act=vmem((layers, ff, lanes), BF16),
        slope_f=vmem((layers, ff, lanes), BF16),
        ubar=vmem((layers, width, lanes), F32),
        ds=vmem((width, lanes), BF16),
        acc_mid=vmem((width, width), F32),
        acc_e=vmem((ew, width), F32),
        acc_z=vmem((width, 3 * lanes), F32),
        acc_zs=vmem((width, lanes), F32),
        acc_b2=vmem((width, lanes), F32),
        acc_h2=vmem((ew, ew), F32),
        acc_h3=vmem((ew, ew), F32),
        acc_ee=vmem((ew, ew), F32),
        acc_t=vmem((ew, 3 * lanes), F32),
        acc_ts=vmem((ew, lanes), F32),
        acc_c=vmem((4, ew, lanes), F32),
        wide=vmem((up_to(rows_in, lanes), CHUNK * lanes), F32),
        vrow=vmem((width, lanes), F32),
        dcur=vmem((width, lanes), F32),
        g_part=vmem((3, width, lanes), F32),
        halo_send=vmem((3, width // 2, lanes), BF16),
        halo_core=vmem((3, width // 2, lanes), BF16),
        halo_half=vmem((3, width // 2, lanes), BF16),
        halo_x=vmem((width // 2, lanes), BF16),
        halo_recv=vmem((3, 4, width // 2, lanes), BF16),
        ar_part=vmem((2, width, lanes), F32),
        ar_one=vmem((2, width // 2, lanes), F32),
        ar_two=vmem((2, width // 2, lanes), BF16),
        ar_three=vmem((2, width // 2, lanes), BF16),
        mask_rows=vmem((slots, lanes), F32),
        vectors=vmem((width, lanes), F32),
        ar_tot=vmem((2, width, lanes), F32),
        send_sem=pltpu.SemaphoreType.DMA((160,)),
        recv_sem=pltpu.SemaphoreType.DMA((160,)),
        local_sem=pltpu.SemaphoreType.DMA((4,)),
        edge_state=vmem((slots, ew, lanes), F32),
        edge_grad=vmem((slots, ew, lanes), F32),
    )
    kept = dict(
        g_eint=((layers, ew, up_to(rows_in, lanes)), BF16),
        g_ehid=((layers, 2, ew, 2 * lanes), BF16),
        g_vec=((width, lanes), F32),
    )
    if plan.fast:
        scratch.update({name: vmem(*spec) for name, spec in kept.items()})
        own_rows = lanes // plan.nbr_total
        scratch.update(
            dict(
                counts=vmem((1, lanes), F32),
                all_nodes=vmem((lanes, width), F32),
                all_dnodes=vmem((lanes, width), F32),
                all_misc=vmem((plan.nbr_total, 8, lanes), F32),
                time_hot=vmem((8 * plan.k_time, lanes), BF16),
                time_rows=vmem((8 * plan.k_time, width), BF16),
                vec_sums=vmem((11, layers * VEC_PER_LAYER, width), F32),
                w_in=vmem((layers, rows_in, width), BF16),
                w_et=vmem((layers, width, ew), BF16),
                w_mid=vmem((layers, width, width), BF16),
                w_midt=vmem((layers, width, width), BF16),
                w_out=vmem((layers, width, width), BF16),
                f_in=vmem((layers, width, ff), BF16),
                f_outt=vmem((layers, width, ff), BF16),
                e_int=vmem((layers, ew, rows_in), BF16),
                e_e=vmem((layers, ew, ew), BF16),
                e_hid=vmem((layers, 2, ew, ew), BF16),
                e_hidt=vmem((layers, 2, ew, ew), BF16),
            )
        )
        outs.update(
            dict(
                o_in=((layers, plan.k_in, lanes), F32),
                o_mid=((layers, plan.k_mid, lanes), F32),
                o_out=((layers, plan.k_mid, lanes), F32),
                o_fin=((layers, plan.k_mid, ff), F32),
                o_foutt=((layers, plan.k_mid, ff), F32),
                o_edge=((layers, ew // 4, plan.k_in), F32),
                o_hid=((layers, 2, plan.k_hid, ew // 4), F32),
                o_time=((plan.tb_rows, lanes), F32),
                o_node_biases=((6, layers, width), F32),
                o_node_gains=((layers, 2, width), F32),
                o_ffn_bias=((layers, 4 * ff), F32),
                o_edge_gains=((layers, ew), F32),
                o_edge_biases=((layers, 4, ew), F32),
            )
        )
    else:
        outs.update(
            dict(
                g_in=((layers, rows_in, width), BF16),
                g_mid=((layers, width, width), BF16),
                g_out=((layers, width, width), BF16),
                g_fin=((layers, width, ff), BF16),
                g_foutt=((layers, width, ff), BF16),
                **kept,
            )
        )
    names = (*operands, *outs, *scratch)
    in_hbm, in_smem = dict(edges=1, d_edges=1, edges_out=1, g_edges=1), dict(time_index=1)
    place = lambda name: pl.BlockSpec(
        memory_space=pl.ANY if name in in_hbm else pltpu.SMEM if name in in_smem else pltpu.VMEM
    )
    results = pl.pallas_call(
        functools.partial(whole_kernel, plan, names),
        out_shape=tuple(jax.ShapeDtypeStruct(*spec) for spec in outs.values()),
        in_specs=[place(name) for name in operands],
        out_specs=[place(name) for name in outs],
        scratch_shapes=list(scratch.values()),
        compiler_params=pltpu.CompilerParams(
            collective_id=1, has_side_effects=True, vmem_limit_bytes=63 * 1024 * 1024
        ),
    )(*operands.values())
    return Refs(outs, results)


def hand_over(values):
    count = len(values)

    def kernel(*refs):
        sources, results, held = refs[:count], refs[count : 2 * count], refs[2 * count : 3 * count]
        come, go = refs[3 * count :]
        arriving = [pltpu.make_async_copy(sources[k], held[k], come.at[k]) for k in range(count)]
        leaving = [pltpu.make_async_copy(held[k], results[k], go.at[k]) for k in range(count)]
        for copy in arriving:
            copy.start()
        for first, second in zip(arriving, leaving, strict=True):
            first.wait()
            second.start()
        for copy in leaving:
            copy.wait()

    specs = [pl.BlockSpec(memory_space=pl.ANY)] * count
    return pl.pallas_call(
        kernel,
        out_shape=[jax.ShapeDtypeStruct(value.shape, value.dtype) for value in values],
        in_specs=specs,
        out_specs=specs,
        scratch_shapes=[
            *(pltpu.VMEM(value.shape, value.dtype) for value in values),
            pltpu.SemaphoreType.DMA((count,)),
            pltpu.SemaphoreType.DMA((count,)),
        ],
    )(*values)


def gather_all(value, res_dim, nbr_dim):
    value = lax.all_gather(value, "res", axis=res_dim, tiled=True)
    return lax.all_gather(value, "nbr", axis=nbr_dim, tiled=True)


def scatter_sum(value, res_dim, nbr_dim):
    value = lax.psum_scatter(value, "res", scatter_dimension=res_dim, tiled=True)
    return lax.psum_scatter(value, "nbr", scatter_dimension=nbr_dim, tiled=True).astype(F32)


def low(value):
    return value.astype(BF16)


def per_device(
    nodes,
    edges,
    protein_ids,
    time_index,
    neighbors,
    edge_mask,
    time_table,
    msg_in,
    msg_mid,
    msg_out,
    ffn_in,
    ffn_out,
    edge_in,
    edge_hidden,
    node_gains,
    node_biases,
    ffn_bias,
    edge_gains,
    edge_biases,
    d_nodes,
    d_edges,
):
    res_total, nbr_total = lax.axis_size("res"), lax.axis_size("nbr")
    own_rows, width = nodes.shape
    ew = edges.shape[2]
    row_count, slot_count = neighbors.shape
    layers = msg_in.shape[0]
    n_at = lax.axis_index("nbr")
    ff = ffn_bias.shape[1] // nbr_total
    shards = (msg_in.shape[1], msg_mid.shape[1], edge_hidden.shape[2], time_table.shape[0])
    plan = Plan(res_total, nbr_total, slot_count, width, ew, ff, layers, shards)

    operands = dict(
        neighbors=neighbors.T,
        mask=edge_mask.T,
        edges=jnp.transpose(edges, (1, 2, 0)),
        d_edges=jnp.transpose(d_edges, (1, 2, 0)),
        node_biases=jnp.swapaxes(node_biases, 0, 1),
        node_gains=node_gains,
        ffn_bias=ffn_bias,
        edge_gains=edge_gains,
        edge_biases=edge_biases,
    )
    if plan.fast:
        operands.update(
            nodes=nodes,
            d_nodes=d_nodes,
            protein_ids=protein_ids[None, :],
            time_index=time_index,
            msg_in=msg_in,
            msg_mid=msg_mid,
            msg_out=msg_out,
            ffn_in=ffn_in,
            ffn_outt=jnp.swapaxes(ffn_out, 1, 2),
            edge_in_t=jnp.swapaxes(edge_in, 1, 2),
            edge_hidden=edge_hidden,
            time_table=time_table,
        )
        out = run_whole(plan, operands)
        (
            nodes_out, edges_out, g_nodes, g_edges, g_time, g_in, g_mid, g_out, g_fin, g_foutt, g_edge_t,
            g_hid, g_gains, g_biases, g_ffn_bias, g_edge_gains, g_edge_biases,
        ) = hand_over(
            [
                out.nodes_out, out.edges_out, out.g_nodes, out.g_edges, out.o_time, out.o_in, out.o_mid,
                out.o_out, out.o_fin, out.o_foutt, out.o_edge, out.o_hid, out.o_node_gains,
                out.o_node_biases, out.o_ffn_bias, out.o_edge_gains, out.o_edge_biases,
            ]
        )
        return (
            nodes_out,
            jnp.transpose(edges_out, (2, 0, 1)),
            g_nodes,
            jnp.transpose(g_edges, (2, 0, 1)),
            g_time,
            g_in,
            g_mid,
            g_out,
            g_fin,
            jnp.swapaxes(g_foutt, 1, 2),
            jnp.swapaxes(g_edge_t, 1, 2),
            g_hid,
            g_gains,
            jnp.swapaxes(g_biases, 0, 1),
            g_ffn_bias,
            g_edge_gains,
            g_edge_biases,
        )

    count_row = jnp.sum(edge_mask.astype(F32), axis=1)
    matches = protein_ids[:, None] == jnp.arange(time_index.shape[0], dtype=jnp.int32)[None, :]
    step_rows = jnp.sum(jnp.where(matches, time_index[None, :], 0), axis=1)
    mine = lambda a: lax.dynamic_slice_in_dim(a, n_at * own_rows, own_rows, axis=0)
    node_vectors = lambda rows: (rows[:, : SH2 + 1], rows[:, GN1 : GN2 + 1])
    table_low = gather_all(low(time_table), 0, 1)
    w_in = gather_all(low(msg_in), 1, 2)
    w_mid = gather_all(low(msg_mid), 1, 2)
    e_in = gather_all(low(edge_in), 1, 2)
    e_hid = gather_all(low(edge_hidden), 2, 3)
    step_onehot = (
        step_rows[:, None] == jnp.arange(table_low.shape[0], dtype=jnp.int32)[None, :]
    ).astype(BF16)
    state = nodes + jnp.dot(step_onehot, table_low, preferred_element_type=F32)
    count_block = jnp.zeros((8, width), F32).at[0, :row_count].set(count_row)
    packed = lax.all_gather(jnp.concatenate([state, d_nodes, count_block], axis=0), "nbr", axis=0)
    operands.update(
        dict(
            h0=packed[:, :own_rows].reshape(row_count, width).T,
            dh=packed[:, own_rows : 2 * own_rows].reshape(row_count, width).T,
            counts=jnp.sum(packed[:, 2 * own_rows, :row_count], axis=0)[None, :],
            w_in=w_in,
            w_et=jnp.swapaxes(w_in[:, 2 * width :], 1, 2),
            w_mid=w_mid,
            w_midt=jnp.swapaxes(w_mid, 1, 2),
            w_out=gather_all(low(msg_out), 1, 2),
            f_in=lax.all_gather(low(ffn_in), "res", axis=1, tiled=True),
            f_outt=lax.all_gather(jnp.swapaxes(low(ffn_out), 1, 2), "res", axis=1, tiled=True),
            e_int=jnp.swapaxes(e_in, 1, 2),
            e_e=e_in[:, 2 * width :],
            e_hid=e_hid,
            e_hidt=jnp.swapaxes(e_hid, 2, 3),
        )
    )
    out = run_whole(plan, operands)
    g_nodes = mine(out.g_nodes)
    g_table_full = lax.dot_general(
        step_onehot.astype(F32),
        g_nodes,
        (((0,), (0,)), ((), ())),
        precision=lax.Precision.HIGHEST,
        preferred_element_type=F32,
    )
    rows = out.g_vec.T[: layers * VECTORS].reshape(layers, VECTORS, width)
    shared = rows[:, B3 : GN2 + 1] * (1.0 / nbr_total)
    g_bias_ffn = lax.dynamic_update_slice_in_dim(
        jnp.zeros_like(ffn_bias), rows[:, FB, :ff], n_at * ff, axis=1
    )
    vectors, g_ffn_bias, g_edge_biases, g_edge_gains = lax.psum(
        (
            jnp.concatenate([rows[:, :B3], shared], axis=1),
            g_bias_ffn,
            rows[:, C1 : C4 + 1, :ew],
            rows[:, GE, :ew],
        ),
        ("res", "nbr"),
    )
    g_node_biases, g_node_gains = node_vectors(vectors)
    scatter_res = lambda a: lax.psum_scatter(a, "res", scatter_dimension=1, tiled=True).astype(F32)
    return (
        mine(out.nodes_out),
        jnp.transpose(out.edges_out, (2, 0, 1)),
        g_nodes,
        jnp.transpose(out.g_edges, (2, 0, 1)),
        scatter_sum(low(g_table_full), 0, 1),
        scatter_sum(out.g_in, 1, 2),
        scatter_sum(out.g_mid, 1, 2),
        scatter_sum(out.g_out, 1, 2),
        scatter_res(out.g_fin),
        jnp.swapaxes(scatter_res(out.g_foutt), 1, 2),
        jnp.swapaxes(scatter_sum(out.g_eint[:, :, : 2 * width + ew], 2, 1), 1, 2),
        scatter_sum(jnp.swapaxes(out.g_ehid[..., :ew], 2, 3), 2, 3),
        g_node_gains,
        g_node_biases,
        g_ffn_bias,
        g_edge_gains,
        g_edge_biases,
    )


def solution(mesh):
    return jax.shard_map(
        per_device,
        mesh=mesh,
        in_specs=(
            P(("res", "nbr"), None),
            P("res", "nbr", None),
            P(("res", "nbr")),
            P(),
            P("res", "nbr"),
            P("res", "nbr"),
            P("res", "nbr"),
            P(None, "res", "nbr"),
            P(None, "res", "nbr"),
            P(None, "res", "nbr"),
            P(None, "res", "nbr"),
            P(None, "nbr", "res"),
            P(None, "res", "nbr"),
            P(None, None, "res", "nbr"),
            P(),
            P(),
            P(),
            P(),
            P(),
            P(("res", "nbr"), None),
            P("res", "nbr", None),
        ),
        out_specs=(
            P(("res", "nbr"), None),
            P("res", "nbr", None),
            P(("res", "nbr"), None),
            P("res", "nbr", None),
            P("res", "nbr"),
            P(None, "res", "nbr"),
            P(None, "res", "nbr"),
            P(None, "res", "nbr"),
            P(None, "res", "nbr"),
            P(None, "nbr", "res"),
            P(None, "res", "nbr"),
            P(None, None, "res", "nbr"),
            P(),
            P(),
            P(),
            P(),
            P(),
        ),
        check_vma=False,
    )
```
